32 devices in a mesh: section: 4 (over y, x), dp: 8 (over z, core).
Axes of the slice: x: 2, y: 2, z: 4, core: 2. Of those that a mesh axis runs over, the one named last changes fastest.
Arguments:
- section_inputs: bfloat16 [2, 4, 4, 1024, 1024], P(None, 'section', None, 'dp'), may hold values from -6 to 6
- top_grad: bfloat16 [2, 4, 1024, 1024], P(None, None, 'dp'), may hold values from -0.15625 to 0.15625
- plan: int32 [2, 4], replicated, may hold values from 0 to 3, each once within a row
- up_weight: bfloat16 [2, 4, 1024, 2048], P(None, 'section'), as said below
- down_weight: bfloat16 [2, 4, 2048, 1024], P(None, 'section'), as said below
- up_moment: float32 [4, 1024, 2048], P('section', 'dp'), may hold values from -6 to 6
- down_moment: float32 [4, 2048, 1024], P('section', 'dp'), may hold values from -6 to 6
Outputs:
- new_up_weight: bfloat16 [2, 4, 1024, 2048], P(None, 'section', 'dp')
- new_down_weight: bfloat16 [2, 4, 2048, 1024], P(None, 'section', 'dp')
- new_up_moment: float32 [4, 1024, 2048], P('section', 'dp')
- new_down_moment: float32 [4, 2048, 1024], P('section', 'dp')
The draws below stay inside these ranges and needn't reach their ends.
Inputs may be any that keep to these rules, and one draw needn't show every extreme that they name: up_weight[1, s] equals up_weight[0, 3 - s] for every s: both relays hold the same model. down_weight[1, s] equals down_weight[0, 3 - s] for every s. `plan`: each row names every micro-batch once.
All inputs are finite; a program needn't handle non-finite values.
Results may differ from the reference program's by a relative error of at most 0.02.
Values may be sent and summed in bfloat16 or wider, within the bound.
No kernel may reach another device: no remote copies, remote signals or barrier semaphores. Data moves between devices by JAX's collectives and lax.ppermute only.
A program may use at most 128 MiB of HBM per device.

```python
import jax
import jax.numpy as jnp
from jax import lax

D = 1024
FF_WIN = 2048
MB = 4
TOK_MB = 128
SECTIONS = 4
TOKENS = 1024
N_DP = 8


def draw_up_weight(key, part):
    inner = jax.random.fold_in(key, 11)
    base = jax.random.normal(inner, (SECTIONS, D, FF_WIN), jnp.float32) * D ** (-0.5)
    return jnp.stack([base, base[::-1]]).astype(jnp.bfloat16)


def draw_down_weight(key, part):
    inner = jax.random.fold_in(key, 23)
    base = jax.random.normal(inner, (SECTIONS, FF_WIN, D), jnp.float32) * FF_WIN ** (-0.5)
    return jnp.stack([base, base[::-1]]).astype(jnp.bfloat16)


def steps_of(rng, dims, cuts, smallest, largest):
    loudness, own = 1.0, jax.random.fold_in(rng, 6)
    for position, shards_of in cuts:
        steps = jnp.exp(jax.random.uniform(jax.random.fold_in(own, position), (shards_of,), jnp.float32, smallest / len(cuts), largest / len(cuts)))
        loudness = loudness * jnp.repeat(steps, dims[position] // shards_of).reshape([-1 if axis == position else 1 for axis in range(len(dims))])
    return loudness


def bell_draw(stream_key, extent, width, most, cuts=(), held_as=jnp.bfloat16):
    loudness = steps_of(stream_key, extent, cuts, -0.22, 0.18) if cuts else 1.0
    result = jax.random.normal(stream_key, extent, jnp.float32) * width * loudness
    return jnp.minimum(jnp.maximum(result, -most), most).astype(held_as)


def setup_inputs(seed: int = 0) -> dict:
    key_of = jax.random.split(jax.random.key(seed), 8)
    return {
        "section_inputs": bell_draw(key_of[0], (2, SECTIONS, MB, TOKENS, D), 1.0, 6.0, ((1, 4), (3, 8))),
        "top_grad": bell_draw(key_of[1], (2, MB, TOKENS, D), ((2 * N_DP * MB * TOK_MB) ** -0.5), 0.15625, ((2, 8),)),
        "plan": jax.vmap(lambda own: jax.random.permutation(own, MB))(jax.random.split(key_of[2], 2)).reshape((2, MB)).astype(jnp.int32),
        "up_weight": draw_up_weight(jax.random.fold_in(key_of[7], 71), 0),
        "down_weight": draw_down_weight(jax.random.fold_in(key_of[7], 71), 0),
        "up_moment": bell_draw(key_of[5], (SECTIONS, D, FF_WIN), 1.0, 6.0, ((0, 4), (1, 8)), jnp.float32),
        "down_moment": bell_draw(key_of[6], (SECTIONS, FF_WIN, D), 1.0, 6.0, ((0, 4), (1, 8)), jnp.float32),
    }


norm_epsilon = 1e-06
momentum_decay = 0.9
step_size = 0.01
root_half = 0.7071067811865476
inv_root_tau = 0.3989422804014327

def gelu_value(preact):
    return 0.5 * preact * (1.0 + lax.erf(preact * root_half))

def gelu_slope(preact):
    return 0.5 * (1.0 + lax.erf(preact * root_half)) + preact * jnp.exp(-0.5 * preact * preact) * inv_root_tau

def times_transpose(left, right):
    return lax.dot_general(left, right, (((1,), (1,)), ((), ())), preferred_element_type=jnp.float32)

def local_backward(inputs, incoming, w_up, w_down):
    preact = jnp.dot(inputs, w_up, preferred_element_type=jnp.float32)
    hidden = gelu_value(preact).astype(jnp.bfloat16)
    summed = inputs.astype(jnp.float32) + jnp.dot(hidden, w_down, preferred_element_type=jnp.float32)
    centre = summed - lax.optimization_barrier(jnp.mean(summed, axis=-1, keepdims=True))
    scale_inv = lax.rsqrt(lax.optimization_barrier(jnp.mean(centre * centre, axis=-1, keepdims=True)) + norm_epsilon)
    normed = centre * scale_inv
    upstream = incoming.astype(jnp.float32)
    grad_sum = scale_inv * (upstream - lax.optimization_barrier(jnp.mean(upstream, axis=-1, keepdims=True)) - normed * lax.optimization_barrier(jnp.mean(upstream * normed, axis=-1, keepdims=True)))
    grad_sum_low = grad_sum.astype(jnp.bfloat16)
    grad_pre = (times_transpose(grad_sum_low, w_down) * gelu_slope(preact)).astype(jnp.bfloat16)
    grad_in = (grad_sum + times_transpose(grad_pre, w_up)).astype(jnp.bfloat16)
    return (grad_in, hidden, grad_pre, grad_sum_low)

def group_partial(left, right):
    left_groups = left.reshape(MB, N_DP, TOK_MB, left.shape[-1]).astype(jnp.float32)
    right_groups = right.reshape(MB, N_DP, TOK_MB, right.shape[-1]).astype(jnp.float32)
    parts = jnp.einsum('mgtd,mgtf->gdf', left_groups, right_groups)
    rounded = lax.optimization_barrier(parts.astype(jnp.bfloat16))
    return lax.optimization_barrier(jnp.sum(rounded.astype(jnp.float32), axis=0))

def section_backward(inputs, incoming, w_up, w_down):
    flat_in = inputs.reshape(MB * TOKENS, D)
    flat_grad = incoming.reshape(MB * TOKENS, D)
    grad_in, hidden, grad_pre, grad_sum_low = local_backward(flat_in, flat_grad, w_up, w_down)
    up_part = group_partial(flat_in, grad_pre)
    down_part = group_partial(hidden, grad_sum_low)
    return (grad_in.reshape(MB, TOKENS, D), up_part, down_part)

def reference(section_inputs, top_grad, plan, up_weight, down_weight, up_moment, down_moment):
    up_sums = [[None] * SECTIONS, [None] * SECTIONS]
    down_sums = [[None] * SECTIONS, [None] * SECTIONS]
    for direction in range(2):
        if direction == 0:
            devices = list(range(SECTIONS - 1, -1, -1))
        else:
            devices = list(range(SECTIONS))
        incoming = top_grad[direction]
        order = plan[direction].astype(jnp.int32)
        for device in devices:
            inputs = jnp.take(section_inputs[direction, device], order, axis=0)
            incoming, up_part, down_part = section_backward(inputs, incoming, up_weight[direction, device], down_weight[direction, device])
            up_sums[direction][device] = up_part
            down_sums[direction][device] = down_part
    grad_up = jnp.stack([up_sums[0][k] + up_sums[1][SECTIONS - 1 - k] for k in range(SECTIONS)])
    grad_down = jnp.stack([down_sums[0][k] + down_sums[1][SECTIONS - 1 - k] for k in range(SECTIONS)])
    new_up_moment = momentum_decay * up_moment + grad_up
    new_down_moment = momentum_decay * down_moment + grad_down
    fresh_up = (up_weight[0].astype(jnp.float32) - step_size * new_up_moment).astype(jnp.bfloat16)
    fresh_down = (down_weight[0].astype(jnp.float32) - step_size * new_down_moment).astype(jnp.bfloat16)
    new_up_weight = jnp.stack([fresh_up, fresh_up[::-1]])
    new_down_weight = jnp.stack([fresh_down, fresh_down[::-1]])
    return (new_up_weight, new_down_weight, new_up_moment, new_down_moment)
```

```python
import functools

import jax
import jax.numpy as jnp
from jax import lax
from jax.experimental import pallas as pl
from jax.experimental.pallas import tpu as pltpu
from jax.sharding import PartitionSpec as P

norm_epsilon = 1e-06
momentum_decay = 0.9
step_size = 0.01
root_half = 0.7071067811865476
inv_root_tau = 0.3989422804014327

f32 = jnp.float32
bf16 = jnp.bfloat16
lag = 2
any_space = pl.BlockSpec(memory_space=pl.ANY)


def params(mib):
    return pltpu.CompilerParams(
        dimension_semantics=("arbitrary",), vmem_limit_bytes=mib * 1024 * 1024
    )


def dot(left, right, over):
    return lax.dot_general(left, right, (over, ((), ())), preferred_element_type=f32)


def tile_of(width):
    return min(512, width)


def forward_body(info, u_ref, p_ref, q_ref, *rest):
    h_ref, slope_ref, y_ref, r_ref, total = rest[-5:]
    j = pl.program_id(0)
    rows, model = total.shape
    u = u_ref[...].reshape(rows, model)
    pre = dot(u, p_ref[0, 0], ((1,), (0,)))
    cdf = 0.5 * (1.0 + lax.erf(pre * root_half))
    hidden = (pre * cdf).astype(bf16)
    slope = cdf + pre * (jnp.exp(-0.5 * pre * pre) * inv_root_tau)
    h_ref[...] = hidden.reshape(h_ref.shape)
    slope_ref[...] = slope.astype(bf16).reshape(slope_ref.shape)
    part = dot(hidden, q_ref[0, 0], ((1,), (0,)))

    @pl.when(j == 0)
    def _():
        total[...] = u.astype(f32) + part

    @pl.when(j > 0)
    def _():
        total[...] += part

    @pl.when(j == pl.num_programs(0) - 1)
    def _():
        z = total[...]
        centre = z - jnp.mean(z, axis=-1, keepdims=True)
        r = lax.rsqrt(jnp.mean(centre * centre, axis=-1, keepdims=True) + norm_epsilon)
        y_ref[...] = (centre * r).astype(bf16).reshape(y_ref.shape)
        r_ref[...] = r.reshape(r_ref.shape)


def forward(inputs, w_up, w_down, source, weights, place, places, previous=None):
    _, _, micro, tokens, model = inputs.shape
    width = w_up.shape[3]
    tile = tile_of(width)
    info = jnp.stack([source, weights, place]).astype(jnp.int32)
    shapes = (
        jax.ShapeDtypeStruct((places, micro, tokens, width), bf16),
        jax.ShapeDtypeStruct((places, micro, tokens, width), bf16),
        jax.ShapeDtypeStruct((places, micro, tokens, model), bf16),
        jax.ShapeDtypeStruct((places, micro, tokens, 1), f32),
    )
    in_specs = [
        pl.BlockSpec((1, 1, micro, tokens, model), lambda j, i: (i[0], 0, 0, 0, 0)),
        pl.BlockSpec((1, 1, model, tile), lambda j, i: (i[1], 0, 0, j)),
        pl.BlockSpec((1, 1, tile, model), lambda j, i: (i[1], 0, j, 0)),
    ]
    operands = [inputs, w_up, w_down]
    aliases = {}
    if previous is not None:
        in_specs += [any_space] * 4
        operands += list(previous)
        aliases = {4 + k: k for k in range(4)}
    flops = 4 * micro * tokens * model * width
    return pl.pallas_call(
        forward_body,
        grid_spec=pltpu.PrefetchScalarGridSpec(
            num_scalar_prefetch=1,
            grid=(width // tile,),
            in_specs=in_specs,
            out_specs=[
                pl.BlockSpec((1, micro, tokens, tile), lambda j, i: (i[2], 0, 0, j)),
                pl.BlockSpec((1, micro, tokens, tile), lambda j, i: (i[2], 0, 0, j)),
                pl.BlockSpec((1, micro, tokens, model), lambda j, i: (i[2], 0, 0, 0)),
                pl.BlockSpec((1, micro, tokens, 1), lambda j, i: (i[2], 0, 0, 0)),
            ],
            scratch_shapes=[pltpu.VMEM((micro * tokens, model), f32)],
        ),
        out_shape=shapes,
        input_output_aliases=aliases,
        compiler_params=params(40),
        cost_estimate=pl.CostEstimate(
            flops=2 * flops, bytes_accessed=4 * model * width, transcendentals=0
        ),
        name="forward",
    )(info, *operands)


def sum_gradient(e, y, r):
    mean_e = jnp.mean(e, axis=-1, keepdims=True)
    mean_ey = jnp.mean(e * y, axis=-1, keepdims=True)
    return r * (e - mean_e - y * mean_ey)


def chain_body(kept, info, recv_ref, top_ref, y_ref, r_ref, slope_ref, p_ref, q_ref, *rest):
    if kept:
        out_ref, pre_ref, sum_ref, whole, low, total = rest[-6:]
    else:
        out_ref, whole, low, total = rest[-4:]
        pre_ref = sum_ref = None
    j = pl.program_id(0)
    active = info[0] > 0

    @pl.when(jnp.logical_and(active, j == 0))
    def _():
        e = jnp.where(info[4] > 0, top_ref[0, 0], recv_ref[...]).astype(f32)
        grad = sum_gradient(e, y_ref[0, 0].astype(f32), r_ref[0, 0])
        whole[...] = grad
        low[...] = grad.astype(bf16)
        if kept:
            sum_ref[0] = grad.astype(bf16)

    @pl.when(active)
    def _():
        grad_pre = (
            dot(low[...], q_ref[0, 0], ((1,), (1,))) * slope_ref[0, 0].astype(f32)
        ).astype(bf16)
        if kept:
            pre_ref[0] = grad_pre

        @pl.when(info[5] > 0)
        def _():
            part = dot(grad_pre, p_ref[0, 0], ((1,), (1,)))

            @pl.when(j == 0)
            def _():
                total[...] = whole[...] + part

            @pl.when(j > 0)
            def _():
                total[...] += part

            @pl.when(j == pl.num_programs(0) - 1)
            def _():
                out_ref[...] = total[...].astype(bf16)


def chain_step(relay, kept, scalars, recv, top_grad, saved, w_up, w_down, previous):
    _, slopes, ys, rs = saved
    tokens, model = recv.shape
    width = w_up.shape[3]
    micro = top_grad.shape[1]
    tile = tile_of(width)
    in_specs = [
        pl.BlockSpec((tokens, model), lambda j, i: (0, 0)),
        pl.BlockSpec((1, 1, tokens, model), lambda j, i: (relay, i[1], 0, 0)),
        pl.BlockSpec((1, 1, tokens, model), lambda j, i: (relay, i[2], 0, 0)),
        pl.BlockSpec((1, 1, tokens, 1), lambda j, i: (relay, i[2], 0, 0)),
        pl.BlockSpec((1, 1, tokens, tile), lambda j, i: (relay, i[2], 0, j * i[0])),
        pl.BlockSpec((1, 1, model, tile), lambda j, i: (relay, 0, 0, j * i[5])),
        pl.BlockSpec((1, 1, tile, model), lambda j, i: (relay, 0, j * i[0], 0)),
    ]
    operands = [recv, top_grad, ys, rs, slopes, w_up, w_down]
    out_shape = [jax.ShapeDtypeStruct((tokens, model), bf16)]
    out_specs = [pl.BlockSpec((tokens, model), lambda j, i: (0, 0))]
    aliases = {}
    if kept:
        out_shape += [
            jax.ShapeDtypeStruct((micro + 1, tokens, width), bf16),
            jax.ShapeDtypeStruct((micro + 1, tokens, model), bf16),
        ]
        out_specs += [
            pl.BlockSpec((1, tokens, tile), lambda j, i: (i[3], 0, j * i[0])),
            pl.BlockSpec((1, tokens, model), lambda j, i: (i[3], 0, 0)),
        ]
        if previous is not None:
            in_specs += [any_space] * 2
            operands += list(previous)
            aliases = {8: 1, 9: 2}
    flops = 4 * tokens * model * width
    return pl.pallas_call(
        functools.partial(chain_body, kept),
        grid_spec=pltpu.PrefetchScalarGridSpec(
            num_scalar_prefetch=1,
            grid=(width // tile,),
            in_specs=in_specs,
            out_specs=out_specs,
            scratch_shapes=[
                pltpu.VMEM((tokens, model), f32),
                pltpu.VMEM((tokens, model), bf16),
                pltpu.VMEM((tokens, model), f32),
            ],
        ),
        out_shape=out_shape,
        input_output_aliases=aliases,
        compiler_params=params(24),
        cost_estimate=pl.CostEstimate(
            flops=2 * flops, bytes_accessed=4 * model * width, transcendentals=0
        ),
        name="chain",
    )(scalars, *operands)


def home_body(micro, info, *refs):
    e_refs = refs[:micro]
    top_ref, y_ref, r_ref, slope_ref, q_ref, pre_ref, sum_ref = refs[micro:]
    j = pl.program_id(0)
    tokens, model = top_ref.shape[2:]

    @pl.when(j == 0)
    def _():
        for slot in range(micro):
            place = info[1 + slot]
            e = jnp.where(info[0] > 0, top_ref[0, slot], e_refs[slot][0]).astype(f32)
            grad = sum_gradient(e, y_ref[0, place].astype(f32), r_ref[0, place])
            sum_ref[place] = grad.astype(bf16)

    low = sum_ref[...].reshape(micro * tokens, model)
    slope = slope_ref[...].reshape(micro * tokens, slope_ref.shape[3])
    grad_pre = dot(low, q_ref[0, 0], ((1,), (1,))) * slope.astype(f32)
    pre_ref[...] = grad_pre.astype(bf16).reshape(pre_ref.shape)


def home_step(info, arrived, top_grad, saved, w_down):
    _, slopes, ys, rs = saved
    _, micro, tokens, model = top_grad.shape
    width = w_down.shape[2]
    tile = tile_of(width)

    def slot_spec(slot):
        return pl.BlockSpec((1, tokens, model), lambda j, i: (i[1 + micro + slot], 0, 0))

    return pl.pallas_call(
        functools.partial(home_body, micro),
        grid_spec=pltpu.PrefetchScalarGridSpec(
            num_scalar_prefetch=1,
            grid=(width // tile,),
            in_specs=[slot_spec(slot) for slot in range(micro)]
            + [
                pl.BlockSpec((1, micro, tokens, model), lambda j, i: (1, 0, 0, 0)),
                pl.BlockSpec((1, micro, tokens, model), lambda j, i: (0, 0, 0, 0)),
                pl.BlockSpec((1, micro, tokens, 1), lambda j, i: (0, 0, 0, 0)),
                pl.BlockSpec((1, micro, tokens, tile), lambda j, i: (0, 0, 0, j)),
                pl.BlockSpec((1, 1, tile, model), lambda j, i: (0, 0, j, 0)),
            ],
            out_specs=[
                pl.BlockSpec((micro, tokens, tile), lambda j, i: (0, 0, j)),
                pl.BlockSpec((micro, tokens, model), lambda j, i: (0, 0, 0)),
            ],
        ),
        out_shape=[
            jax.ShapeDtypeStruct((micro, tokens, width), bf16),
            jax.ShapeDtypeStruct((micro, tokens, model), bf16),
        ],
        compiler_params=params(32),
        cost_estimate=pl.CostEstimate(
            flops=4 * micro * tokens * model * width,
            bytes_accessed=2 * model * width,
            transcendentals=0,
        ),
        name="home",
    )(info, *([arrived] * micro), top_grad, ys, rs, slopes, w_down)


def weight_body(la_ref, ra_ref, lb_ref, rb_ref, out_ref):
    def flat(ref):
        value = ref[...]
        return value.reshape(-1, value.shape[-1])

    total = dot(flat(la_ref), flat(ra_ref), ((0,), (0,)))
    total += dot(flat(lb_ref), flat(rb_ref), ((0,), (0,)))
    out_ref[...] = total.astype(bf16)


def weight_gradient(left_a, right_a, left_b, right_b, micro, split_left):
    tokens = right_a.shape[-2]
    rows, columns = left_a.shape[-1], right_a.shape[-1]
    tile = tile_of(rows if split_left else columns)

    def spec(array, split):
        lead = array.ndim - 3
        block = (1,) * lead + (micro, tokens, tile if split else array.shape[-1])
        if split:
            return pl.BlockSpec(block, lambda j: (0,) * (lead + 2) + (j,))
        return pl.BlockSpec(block, lambda j: (0,) * (lead + 3))

    out_block = (tile, columns) if split_left else (rows, tile)
    return pl.pallas_call(
        weight_body,
        grid=((rows if split_left else columns) // tile,),
        in_specs=[
            spec(left_a, split_left),
            spec(right_a, not split_left),
            spec(left_b, split_left),
            spec(right_b, not split_left),
        ],
        out_specs=pl.BlockSpec(out_block, (lambda j: (j, 0)) if split_left else (lambda j: (0, j))),
        out_shape=jax.ShapeDtypeStruct((rows, columns), bf16),
        compiler_params=params(40),
        cost_estimate=pl.CostEstimate(
            flops=4 * micro * tokens * rows * columns,
            bytes_accessed=2 * rows * columns,
            transcendentals=0,
        ),
        name="weights",
    )(left_a, right_a, left_b, right_b)


def on_device(section_inputs, top_grad, plan, up_weight, down_weight, up_moment, down_moment):
    sections = lax.axis_size("section")
    position = lax.axis_index("section")
    replica = lax.axis_index("dp")
    micro, tokens, model = top_grad.shape[1:]
    plan = plan.astype(jnp.int32)
    zero = jnp.int32(0)
    last = sections - 1

    def hop(value, pairs):
        return lax.ppermute(value, "section", pairs) if pairs else None

    mirrored = lax.ppermute(
        section_inputs[1, 0], "section", [(i, last - i) for i in range(sections)]
    )

    first = jnp.where(position >= sections // 2, 0, 1).astype(jnp.int32)
    saved = forward(section_inputs, up_weight, down_weight, first, first, first, 2)
    saved = forward(
        section_inputs, up_weight, down_weight, 1 - first, 1 - first, 1 - first, 2, saved
    )
    saved_home = forward(mirrored[None, None], up_weight, down_weight, zero, zero, zero, 1)

    blank = jnp.zeros((tokens, model), bf16)
    ticks = micro + lag * last
    received = [{}, {}]
    home = []
    kept = None
    for tick in range(ticks):
        for relay in range(2):
            start = (last - position) if relay == 0 else position
            slot = tick - lag * start
            active = jnp.logical_and(slot >= 0, slot < micro)
            if relay == 1:
                active = jnp.logical_and(active, position < last)

            def busy(i, tick=tick, relay=relay):
                return 0 <= tick - lag * ((last - i) if relay == 0 else i) < micro

            if relay == 1 and not any(busy(i) for i in range(last)):
                continue
            slot = jnp.clip(slot, 0, micro - 1)
            place = plan[relay, slot]
            asked = active if relay == 1 else jnp.logical_and(active, position > 0)
            scalars = jnp.stack(
                [
                    active.astype(jnp.int32),
                    slot,
                    place,
                    jnp.where(active, place, micro),
                    (start == 0).astype(jnp.int32),
                    asked.astype(jnp.int32),
                ]
            ).astype(jnp.int32)
            recv = received[relay].pop(tick, None)
            if recv is None:
                recv = blank
            done = chain_step(
                relay, relay == 0, scalars, recv, top_grad, saved, up_weight, down_weight, kept
            )
            out = done[0]
            if relay == 0:
                kept = done[1:]
                pairs = [(i, i - 1) for i in range(1, sections) if busy(i)]
            else:
                pairs = [(i, i + 1) for i in range(sections - 2) if busy(i)]
                home.append(hop(out, [(i, last - 1 - i) for i in range(last) if busy(i)]))
            got = hop(out, pairs)
            if got is not None:
                received[relay][tick + lag] = got

    origin = jnp.clip(last - 1 - position, 0, last - 1)
    info = jnp.concatenate(
        [
            (position == last).astype(jnp.int32)[None],
            plan[1],
            jnp.arange(micro, dtype=jnp.int32) + lag * origin,
        ]
    )
    home_pre, home_sum = home_step(info, jnp.stack(home), top_grad, saved_home, down_weight)

    up_part = weight_gradient(section_inputs[0], kept[0], mirrored, home_pre, micro, False)
    up_sum = lax.psum_scatter(up_part, "dp", scatter_dimension=0, tiled=True)
    down_part = weight_gradient(saved[0], kept[1], saved_home[0], home_sum, micro, True)
    down_sum = lax.psum_scatter(down_part, "dp", scatter_dimension=0, tiled=True)

    def update(weight, moment, total):
        rows = moment.shape[1]
        held = lax.dynamic_slice_in_dim(weight[0, 0], replica * rows, rows, 0)
        fresh_moment = momentum_decay * moment[0] + total.astype(f32)
        fresh = (held.astype(f32) - step_size * fresh_moment).astype(bf16)
        far = lax.ppermute(fresh, "section", [(i, last - i) for i in range(sections)])
        return jnp.stack([fresh, far])[:, None], fresh_moment[None]

    new_up_weight, new_up_moment = update(up_weight, up_moment, up_sum)
    new_down_weight, new_down_moment = update(down_weight, down_moment, down_sum)
    return (new_up_weight, new_down_weight, new_up_moment, new_down_moment)


def solution(mesh):
    in_specs = (
        P(None, "section", None, "dp", None),
        P(None, None, "dp", None),
        P(),
        P(None, "section", None, None),
        P(None, "section", None, None),
        P("section", "dp", None),
        P("section", "dp", None),
    )
    out_specs = (
        P(None, "section", "dp", None),
        P(None, "section", "dp", None),
        P("section", "dp", None),
        P("section", "dp", None),
    )
    return jax.shard_map(
        on_device, mesh=mesh, in_specs=in_specs, out_specs=out_specs, check_vma=False
    )
```

```python
import jax
import jax.numpy as jnp
import numpy as np
from jax import lax
from jax.experimental import pallas as pl
from jax.experimental.pallas import tpu as pltpu
from jax.sharding import PartitionSpec as P

norm_epsilon = 1e-06
momentum_decay = 0.9
step_size = 0.01
root_half = 0.7071067811865476
inv_root_tau = 0.3989422804014327

f32 = jnp.float32
bf16 = jnp.bfloat16
any_space = pl.BlockSpec(memory_space=pl.ANY)


def params(mib):
    return pltpu.CompilerParams(
        dimension_semantics=("arbitrary",), vmem_limit_bytes=mib * 1024 * 1024
    )


def in_hbm(x):
    return pltpu.with_memory_space_constraint(x, pltpu.HBM)


def dot(left, right, over):
    return lax.dot_general(left, right, (over, ((), ())), preferred_element_type=f32)


def tile_of(width):
    return min(512, width)


def forward_body(per, info, plan, *refs):
    u_refs = refs[:per]
    p_ref, q_ref = refs[per : per + 2]
    us_ref, h_ref, slope_ref, y_ref, r_ref, rows_ref, total = refs[-7:]
    j = pl.program_id(0)

    @pl.when(j == 0)
    def _():
        tokens = u_refs[0].shape[3]
        for k in range(per):
            u = u_refs[k][0, 0, 0]
            rows_ref[k * tokens : (k + 1) * tokens] = u
            us_ref[0, 0, k * tokens : (k + 1) * tokens] = u

    u = rows_ref[...]
    pre = dot(u, p_ref[0, 0], ((1,), (0,)))
    cdf = 0.5 * (1.0 + lax.erf(pre * root_half))
    hidden = (pre * cdf).astype(bf16)
    slope = cdf + pre * (jnp.exp(-0.5 * pre * pre) * inv_root_tau)
    h_ref[0, 0] = hidden
    slope_ref[0, 0] = slope.astype(bf16)
    part = dot(hidden, q_ref[0, 0], ((1,), (0,)))

    @pl.when(j == 0)
    def _():
        total[...] = u.astype(f32) + part

    @pl.when(j > 0)
    def _():
        total[...] += part

    @pl.when(j == pl.num_programs(0) - 1)
    def _():
        z = total[...]
        centre = z - jnp.mean(z, axis=-1, keepdims=True)
        r = lax.rsqrt(jnp.mean(centre * centre, axis=-1, keepdims=True) + norm_epsilon)
        y_ref[0, 0] = (centre * r).astype(bf16)
        r_ref[0, 0] = r


def forward(group, per, inputs, w_up, w_down, info, plan, previous, after, places):
    _, _, micro, tokens, model = inputs.shape
    width = w_up.shape[3]
    tile = tile_of(width)
    groups, rows = micro // per, per * tokens

    def u_spec(k):
        return pl.BlockSpec(
            (1, 1, 1, tokens, model), lambda j, i, p: (i[0], 0, p[i[2], group * per + k], 0, 0)
        )

    def out(columns, split=False, dtype=bf16):
        shape = pltpu.HBM((places, groups, rows, columns), dtype)
        block = (1, 1, rows, tile if split else columns)
        if split:
            return shape, pl.BlockSpec(block, lambda j, i, p: (i[3], group, 0, j))
        return shape, pl.BlockSpec(block, lambda j, i, p: (i[3], group, 0, 0))

    outs = [out(model), out(width, True), out(width, True), out(model), out(1, False, f32)]
    in_specs = [u_spec(k) for k in range(per)] + [
        pl.BlockSpec((1, 1, model, tile), lambda j, i, p: (i[1], 0, 0, j)),
        pl.BlockSpec((1, 1, tile, model), lambda j, i, p: (i[1], 0, j, 0)),
    ]
    operands = [in_hbm(inputs)] * per + [in_hbm(w_up), in_hbm(w_down)]
    aliases = {}
    if previous is not None:
        aliases = {2 + len(operands) + k: k for k in range(5)}
        in_specs += [any_space] * 5
        operands += [in_hbm(x) for x in previous]
    for x in after:
        if previous is None or not any(x is y for y in previous):
            in_specs.append(any_space)
            operands.append(in_hbm(x) if x.ndim > 2 else x)

    def body(*refs):
        forward_body(per, *refs)

    return pl.pallas_call(
        body,
        grid_spec=pltpu.PrefetchScalarGridSpec(
            num_scalar_prefetch=2,
            grid=(width // tile,),
            in_specs=in_specs,
            out_specs=[spec for _, spec in outs],
            scratch_shapes=[pltpu.VMEM((rows, model), bf16), pltpu.VMEM((rows, model), f32)],
        ),
        out_shape=[shape for shape, _ in outs],
        input_output_aliases=aliases,
        compiler_params=params(40),
        cost_estimate=pl.CostEstimate(
            flops=8 * rows * model * width, bytes_accessed=4 * model * width, transcendentals=0
        ),
        name="forward",
    )(info, plan, *operands)


def sum_gradient(e, y, r):
    mean_e = jnp.mean(e, axis=-1, keepdims=True)
    mean_ey = jnp.mean(e * y, axis=-1, keepdims=True)
    return r * (e - mean_e - y * mean_ey)


columns_of_table = 6


def chain_step(call, table, recv, top_grad, saved, w_up, w_down, previous, after):
    base = call * columns_of_table
    _, _, slopes, ys, rs = saved
    rows, model = recv[0].shape
    width = w_up.shape[3]
    tile = tile_of(width)
    groups = slopes.shape[1]
    tokens = top_grad.shape[2]
    per = rows // tokens

    def body(info, *rest):
        recv_refs, rest = rest[: len(recv)], rest[len(recv) :]
        top_ref, y_ref, r_ref, slope_ref, p_ref, q_ref = rest[:6]
        out_ref, pre_ref, sum_ref, whole, low, total = rest[-6:]
        j = pl.program_id(0)
        active = info[base] > 0

        @pl.when(jnp.logical_and(active, j == 0))
        def _():
            top = top_ref[0].reshape(rows, model)
            e = jnp.where(info[base + 4] == 1, top, recv_refs[-1][...])
            if len(recv) > 1:
                e = jnp.where(info[base + 4] == 2, recv_refs[0][...], e)
            e = e.astype(f32)
            grad = sum_gradient(e, y_ref[0, 0].astype(f32), r_ref[0, 0])
            whole[...] = grad
            low[...] = grad.astype(bf16)
            sum_ref[0] = grad.astype(bf16)

        @pl.when(active)
        def _():
            grad_pre = (
                dot(low[...], q_ref[0, 0], ((1,), (1,))) * slope_ref[0, 0].astype(f32)
            ).astype(bf16)
            pre_ref[0] = grad_pre

            @pl.when(info[base + 5] > 0)
            def _():
                part = dot(grad_pre, p_ref[0, 0], ((1,), (1,)))

                @pl.when(j == 0)
                def _():
                    total[...] = whole[...] + part

                @pl.when(j > 0)
                def _():
                    total[...] += part

                @pl.when(j == pl.num_programs(0) - 1)
                def _():
                    out_ref[...] = total[...].astype(bf16)

    in_specs = [pl.BlockSpec((rows, model), lambda j, i: (0, 0))] * len(recv) + [
        pl.BlockSpec((1, per, tokens, model), lambda j, i: (i[base + 1], i[base + 2], 0, 0)),
        pl.BlockSpec((1, 1, rows, model), lambda j, i: (i[base + 1], i[base + 2], 0, 0)),
        pl.BlockSpec((1, 1, rows, 1), lambda j, i: (i[base + 1], i[base + 2], 0, 0)),
        pl.BlockSpec(
            (1, 1, rows, tile), lambda j, i: (i[base + 1], i[base + 2], 0, j * i[base])
        ),
        pl.BlockSpec((1, 1, model, tile), lambda j, i: (i[base + 1], 0, 0, j * i[base + 5])),
        pl.BlockSpec((1, 1, tile, model), lambda j, i: (i[base + 1], 0, j * i[base], 0)),
    ]
    operands = list(recv) + [in_hbm(x) for x in (top_grad, ys, rs, slopes, w_up, w_down)]
    aliases = {}
    if previous is not None:
        aliases = {1 + len(operands): 1, 2 + len(operands): 2}
        in_specs += [any_space] * 2
        operands += [in_hbm(x) for x in previous]
    for x in after:
        if previous is None or not any(x is y for y in previous):
            in_specs.append(any_space)
            operands.append(in_hbm(x) if x.ndim > 2 else x)
    return pl.pallas_call(
        body,
        grid_spec=pltpu.PrefetchScalarGridSpec(
            num_scalar_prefetch=1,
            grid=(width // tile,),
            in_specs=in_specs,
            out_specs=[
                pl.BlockSpec((rows, model), lambda j, i: (0, 0)),
                pl.BlockSpec((1, rows, tile), lambda j, i: (i[base + 3], 0, j * i[base])),
                pl.BlockSpec((1, rows, model), lambda j, i: (i[base + 3], 0, 0)),
            ],
            scratch_shapes=[
                pltpu.VMEM((rows, model), f32),
                pltpu.VMEM((rows, model), bf16),
                pltpu.VMEM((rows, model), f32),
            ],
        ),
        out_shape=[
            jax.ShapeDtypeStruct((rows, model), bf16),
            pltpu.HBM((groups + 1, rows, width), bf16),
            pltpu.HBM((groups + 1, rows, model), bf16),
        ],
        input_output_aliases=aliases,
        compiler_params=params(32),
        cost_estimate=pl.CostEstimate(
            flops=8 * rows * model * width, bytes_accessed=4 * model * width, transcendentals=0
        ),
        name="chain",
    )(table, *operands)


def home_step(info, arrived, top_grad, saved, w_down, after):
    _, _, slopes, ys, rs = saved
    groups, rows, model = slopes.shape[1], slopes.shape[2], ys.shape[3]
    micro, tokens = top_grad.shape[1:3]
    width = w_down.shape[2]
    tile = tile_of(width)

    def body(info, *refs):
        e_refs = refs[:groups]
        top_ref, y_ref, r_ref, slope_ref, q_ref = refs[groups : groups + 5]
        pre_ref, sum_ref = refs[-2:]

        @pl.when(pl.program_id(0) == 0)
        def _():
            for g in range(groups):
                top = top_ref[0].reshape(groups, rows, model)[g]
                e = jnp.where(info[0] > 0, top, e_refs[g][...]).astype(f32)
                grad = sum_gradient(e, y_ref[0, g].astype(f32), r_ref[0, g])
                sum_ref[g] = grad.astype(bf16)

        low = sum_ref[...].reshape(groups * rows, model)
        slope = slope_ref[0].reshape(groups * rows, tile)
        grad_pre = dot(low, q_ref[0, 0], ((1,), (1,))) * slope.astype(f32)
        pre_ref[...] = grad_pre.astype(bf16).reshape(pre_ref.shape)

    return pl.pallas_call(
        body,
        grid_spec=pltpu.PrefetchScalarGridSpec(
            num_scalar_prefetch=1,
            grid=(width // tile,),
            in_specs=[pl.BlockSpec((rows, model), lambda j, i: (0, 0))] * groups
            + [
                pl.BlockSpec((1, micro, tokens, model), lambda j, i: (1, 0, 0, 0)),
                pl.BlockSpec((1, groups, rows, model), lambda j, i: (0, 0, 0, 0)),
                pl.BlockSpec((1, groups, rows, 1), lambda j, i: (0, 0, 0, 0)),
                pl.BlockSpec((1, groups, rows, tile), lambda j, i: (0, 0, 0, j)),
                pl.BlockSpec((1, 1, tile, model), lambda j, i: (0, 0, j, 0)),
            ]
            + [any_space] * len(after),
            out_specs=[
                pl.BlockSpec((groups, rows, tile), lambda j, i: (0, 0, j)),
                pl.BlockSpec((groups, rows, model), lambda j, i: (0, 0, 0)),
            ],
        ),
        out_shape=[
            pltpu.HBM((groups, rows, width), bf16),
            pltpu.HBM((groups, rows, model), bf16),
        ],
        compiler_params=params(40),
        cost_estimate=pl.CostEstimate(
            flops=4 * groups * rows * model * width,
            bytes_accessed=2 * model * width,
            transcendentals=0,
        ),
        name="home",
    )(
        info,
        *arrived,
        *[in_hbm(x) for x in (top_grad, ys, rs, slopes, w_down)],
        *[in_hbm(x) if x.ndim > 2 else x for x in after],
    )


def weight_gradient(left_a, right_a, left_b, right_b, groups, split_left, after):
    tokens = right_a.shape[-2]
    rows, columns = left_a.shape[-1], right_a.shape[-1]
    tile = tile_of(rows if split_left else columns)

    def body(la_ref, ra_ref, lb_ref, rb_ref, *rest):
        def flat(ref):
            return ref[...].reshape(-1, ref.shape[-1])

        total = dot(flat(la_ref), flat(ra_ref), ((0,), (0,)))
        total += dot(flat(lb_ref), flat(rb_ref), ((0,), (0,)))
        rest[-1][...] = total.astype(bf16)

    def spec(array, split):
        lead = array.ndim - 3
        block = (1,) * lead + (groups, tokens, tile if split else array.shape[-1])
        if split:
            return pl.BlockSpec(block, lambda j: (0,) * (lead + 2) + (j,))
        return pl.BlockSpec(block, lambda j: (0,) * (lead + 3))

    out_block = (tile, columns) if split_left else (rows, tile)
    return pl.pallas_call(
        body,
        grid=((rows if split_left else columns) // tile,),
        in_specs=[
            spec(left_a, split_left),
            spec(right_a, not split_left),
            spec(left_b, split_left),
            spec(right_b, not split_left),
        ]
        + [any_space] * len(after),
        out_specs=pl.BlockSpec(out_block, (lambda j: (j, 0)) if split_left else (lambda j: (0, j))),
        out_shape=pltpu.HBM((rows, columns), bf16),
        compiler_params=params(40),
        cost_estimate=pl.CostEstimate(
            flops=4 * groups * tokens * rows * columns,
            bytes_accessed=2 * rows * columns,
            transcendentals=0,
        ),
        name="weights",
    )(*[in_hbm(x) for x in (left_a, right_a, left_b, right_b)], *[in_hbm(x) for x in after])


def update(replica, weight, moment, total):
    _, rows, columns = moment.shape
    tile = min(64, rows)
    steps = rows // tile

    def body(info, weight_ref, moment_ref, total_ref, fresh_ref, out_ref):
        fresh_moment = momentum_decay * moment_ref[0] + total_ref[...].astype(f32)
        out_ref[0] = fresh_moment
        fresh_ref[...] = (weight_ref[0, 0].astype(f32) - step_size * fresh_moment).astype(bf16)

    return pl.pallas_call(
        body,
        grid_spec=pltpu.PrefetchScalarGridSpec(
            num_scalar_prefetch=1,
            grid=(steps,),
            in_specs=[
                pl.BlockSpec((1, 1, tile, columns), lambda j, i: (0, 0, i[0] * steps + j, 0)),
                pl.BlockSpec((1, tile, columns), lambda j, i: (0, j, 0)),
                pl.BlockSpec((tile, columns), lambda j, i: (j, 0)),
            ],
            out_specs=[
                pl.BlockSpec((tile, columns), lambda j, i: (j, 0)),
                pl.BlockSpec((1, tile, columns), lambda j, i: (0, j, 0)),
            ],
        ),
        out_shape=[
            jax.ShapeDtypeStruct((rows, columns), bf16),
            pltpu.HBM((1, rows, columns), f32),
        ],
        compiler_params=params(24),
        cost_estimate=pl.CostEstimate(
            flops=4 * rows * columns, bytes_accessed=12 * rows * columns, transcendentals=0
        ),
        name="update",
    )(replica, in_hbm(weight), in_hbm(moment), total)


def on_device(section_inputs, top_grad, plan, up_weight, down_weight, up_moment, down_moment):
    sections = lax.axis_size("section")
    position = lax.axis_index("section").astype(jnp.int32)
    micro, tokens, model = top_grad.shape[1:]
    plan = plan.astype(jnp.int32)
    per = 2 if micro % 2 == 0 else 1
    groups, rows = micro // per, per * tokens
    last, half = sections - 1, sections // 2

    def hop(value, pairs):
        return lax.ppermute(value, "section", pairs) if pairs else None

    mirrored = lax.ppermute(
        section_inputs[1, 0], "section", [(i, last - i) for i in range(sections)]
    )[None, None]

    upper = (position >= half).astype(jnp.int32)
    near = jnp.minimum(position, last - position)
    start = (near, last - near)
    relay = (1 - upper, upper)

    def begins(kind, i):
        return min(i, last - i) if kind == 0 else last - min(i, last - i)

    calls = [
        (tick, kind)
        for tick in range(groups + last)
        for kind in range(2)
        if any(0 <= tick - begins(kind, i) < groups for i in range(sections))
    ]
    ticks = np.array([tick for tick, _ in calls], np.int32)
    second = np.array([kind for _, kind in calls], np.int32)
    group = jnp.where(second == 1, ticks - start[1], ticks - start[0])
    of = jnp.where(second == 1, relay[1], relay[0])
    needless = jnp.logical_and(of == 1, position == last)
    active = (group >= 0) & (group < groups) & ~needless
    group = jnp.clip(group, 0, groups - 1)
    asked = active & ~((of == 0) & (position == 0))
    table = jnp.stack(
        [
            active.astype(jnp.int32),
            of,
            group,
            jnp.where(active & (of == 0), group, groups),
            jnp.where(
                jnp.where(of == 0, position == last, position == 0),
                1,
                jnp.where((second == 1) & (near == half - 1), 2, 0),
            ),
            asked.astype(jnp.int32),
        ],
        axis=1,
    ).reshape(-1)
    kinds = [jnp.stack([relay[k]] * 4) for k in range(2)]
    home_kind = jnp.array([0, 0, 1, 0], jnp.int32)

    saved = None
    saved_home = None
    order = []

    def run_forward(kind, g):
        nonlocal saved, order
        saved = forward(
            g, per, section_inputs, up_weight, down_weight, kinds[kind], plan, saved, order, 2
        )
        order = [saved[0]]

    def run_home_forward(g):
        nonlocal saved_home, order
        saved_home = forward(
            g, per, mirrored, up_weight, down_weight, home_kind, plan, saved_home, order, 1
        )
        order = [saved_home[0]]

    pending = [(0, g) for g in range(groups)] + [(1, g) for g in range(groups)]
    late = []
    blank = jnp.zeros((rows, model), bf16)
    received = {}
    arrived = {}
    kept = None
    for call, (tick, kind) in enumerate(calls):
        newest = min(tick - (sections - half if kind else 0), groups - 1)
        while pending and any(k < kind or (k == kind and g <= newest) for k, g in pending):
            run_forward(*pending.pop(0))
        if call == len(calls) - 1:
            for g in range(groups):
                run_home_forward(g)

        def busy(i):
            return 0 <= tick - begins(kind, i) < groups

        recv = [
            received.pop((tick, kind, way))
            for way in range(2)
            if (tick, kind, way) in received
        ] or [blank]
        out, *kept = chain_step(
            call, table, recv, top_grad, saved, up_weight, down_weight, kept, order
        )
        order = [kept[0]] + [x for n, x in late if n < call]
        late = [(n, x) for n, x in late if n >= call]
        relay_of = [(0 if i >= half else 1) if kind == 0 else (1 if i >= half else 0) for i in range(sections)]
        to = [i - 1 if relay_of[i] == 0 else i + 1 for i in range(sections)]
        live = [
            i
            for i in range(sections)
            if busy(i) and 0 <= to[i] <= last and not (relay_of[i] == 1 and to[i] == last)
        ]
        crossing = [i for i in live if kind == 0 and (i >= half) != (to[i] >= half)]
        for pairs, kind_after, way in (
            ([(i, to[i]) for i in live if i in crossing], 1, 0),
            ([(i, to[i]) for i in live if i not in crossing], kind, 1),
        ):
            got = hop(out, pairs)
            if got is not None:
                received[(tick + 1, kind_after, way)] = got
        pairs = [(i, last - 1 - i) for i in range(last) if busy(i) and relay_of[i] == 1]
        got = hop(out, pairs)
        if got is not None:
            for i, k in pairs:
                arrived[(k, tick - begins(kind, i))] = got
            late.append((call, got))
        if pending and (kind == 1 or pending[0][0] == 0 or tick + 1 >= groups):
            run_forward(*pending.pop(0))

    came = []
    for g in range(groups):
        options = []
        for k in range(last):
            value = arrived[(k, g)]
            if not any(value is x for x, _ in options):
                options.append((value, []))
            next(places for x, places in options if x is value).append(k)
        value = options[0][0]
        for other, places in options[1:]:
            here = either([position == k for k in places])
            value = jnp.where(here, other, value)
        came.append(value)
    home_pre, home_sum = home_step(
        (position == last).astype(jnp.int32)[None], came, top_grad, saved_home, down_weight, order
    )

    up_part = weight_gradient(saved[0], kept[0], saved_home[0], home_pre, groups, False, [])
    up_sum = lax.psum_scatter(up_part, "dp", scatter_dimension=0, tiled=True)
    down_part = weight_gradient(
        saved[1], kept[1], saved_home[1], home_sum, groups, True, [up_part]
    )
    down_sum = lax.psum_scatter(down_part, "dp", scatter_dimension=0, tiled=True)
    replica = lax.axis_index("dp").astype(jnp.int32)[None]

    def finish(weight, moment, total):
        fresh, fresh_moment = update(replica, weight, moment, total)
        far = lax.ppermute(fresh, "section", [(i, last - i) for i in range(sections)])
        return jnp.stack([fresh, far])[:, None], fresh_moment

    new_up_weight, new_up_moment = finish(up_weight, up_moment, up_sum)
    new_down_weight, new_down_moment = finish(down_weight, down_moment, down_sum)
    return (new_up_weight, new_down_weight, new_up_moment, new_down_moment)


def either(conditions):
    result = conditions[0]
    for condition in conditions[1:]:
        result = jnp.logical_or(result, condition)
    return result


def solution(mesh):
    in_specs = (
        P(None, "section", None, "dp", None),
        P(None, None, "dp", None),
        P(),
        P(None, "section", None, None),
        P(None, "section", None, None),
        P("section", "dp", None),
        P("section", "dp", None),
    )
    out_specs = (
        P(None, "section", "dp", None),
        P(None, "section", "dp", None),
        P("section", "dp", None),
        P("section", "dp", None),
    )
    return jax.shard_map(
        on_device, mesh=mesh, in_specs=in_specs, out_specs=out_specs, check_vma=False
    )
```

```python
import jax
import jax.numpy as jnp
import numpy as np
from jax import lax
from jax.experimental import pallas as pl
from jax.experimental.pallas import tpu as pltpu
from jax.sharding import PartitionSpec as P

norm_epsilon = 1e-06
momentum_decay = 0.9
step_size = 0.01
root_half = 0.7071067811865476
inv_root_tau = 0.3989422804014327

f32 = jnp.float32
bf16 = jnp.bfloat16
any_space = pl.BlockSpec(memory_space=pl.ANY)


def params(mib):
    return pltpu.CompilerParams(
        dimension_semantics=("arbitrary",), vmem_limit_bytes=mib * 1024 * 1024
    )


def in_vmem(x):
    return pltpu.with_memory_space_constraint(x, pltpu.VMEM)


def in_hbm(x):
    return pltpu.with_memory_space_constraint(x, pltpu.HBM)


def dot(left, right, over):
    return lax.dot_general(left, right, (over, ((), ())), preferred_element_type=f32)


def tile_of(width):
    return min(512, width)


def forward(per, inputs, w_up, w_down, info, plan, previous, after, places, resident):
    _, _, micro, tokens, model = inputs.shape
    width = w_up.shape[3]
    tile = tile_of(width)
    groups, rows, every = micro // per, per * tokens, micro * tokens

    def body(info_ref, plan_ref, *refs):
        u_refs = refs[:micro]
        p_ref, q_ref = refs[micro : micro + 2]
        outs = refs[len(operands) :]
        us_ref, h_ref, slope_ref, y_ref, r_ref = outs[:5]
        rows_ref, total = outs[-2:]
        j = pl.program_id(0)

        @pl.when(j == 0)
        def _():
            for k in range(micro):
                u = u_refs[k][0, 0, 0]
                rows_ref[k * tokens : (k + 1) * tokens] = u
                us_ref[0, k // per, k % per * tokens : (k % per + 1) * tokens] = u

        if resident:
            outs[5][...] = p_ref[0, 0]
            outs[6][...] = q_ref[0, 0]
        for g in range(groups):
            here = slice(g * rows, (g + 1) * rows)
            u = rows_ref[here]
            pre = dot(u, p_ref[0, 0], ((1,), (0,)))
            cdf = 0.5 * (1.0 + lax.erf(pre * root_half))
            hidden = (pre * cdf).astype(bf16)
            slope = cdf + pre * (jnp.exp(-0.5 * pre * pre) * inv_root_tau)
            h_ref[0, g] = hidden
            slope_ref[g] = slope.astype(bf16)
            part = dot(hidden, q_ref[0, 0], ((1,), (0,)))
            base = jnp.where(j == 0, u.astype(f32), total[here])
            total[here] = base + part

        @pl.when(j == pl.num_programs(0) - 1)
        def _():
            for g in range(groups):
                z = total[g * rows : (g + 1) * rows]
                centre = z - jnp.mean(z, axis=-1, keepdims=True)
                r = lax.rsqrt(jnp.mean(centre * centre, axis=-1, keepdims=True) + norm_epsilon)
                y_ref[g] = (centre * r).astype(bf16)
                r_ref[g] = r

    def u_spec(k):
        return pl.BlockSpec(
            (1, 1, 1, tokens, model), lambda j, i, p: (i[0], 0, p[i[2], k], 0, 0)
        )

    in_specs = [u_spec(k) for k in range(micro)] + [
        pl.BlockSpec((1, 1, model, tile), lambda j, i, p: (i[1], 0, 0, j)),
        pl.BlockSpec((1, 1, tile, model), lambda j, i, p: (i[1], 0, j, 0)),
    ]
    operands = [in_hbm(inputs)] * micro + [in_hbm(w_up), in_hbm(w_down)]
    aliases = {}
    if previous is not None:
        aliases = {2 + len(operands) + k: k for k in range(2)}
        in_specs += [any_space] * 2
        operands += [in_hbm(x) for x in previous]
    for x in after:
        in_specs.append(any_space)
        operands.append(in_hbm(x) if x.ndim > 2 else x)
    out_shape = [
        pltpu.HBM((places, groups, rows, model), bf16),
        pltpu.HBM((places, groups, rows, width), bf16),
        pltpu.VMEM((groups, rows, width), bf16),
        pltpu.VMEM((groups, rows, model), bf16),
        pltpu.VMEM((groups, rows, 1), f32),
    ]
    out_specs = [
        pl.BlockSpec((1, groups, rows, model), lambda j, i, p: (i[3], 0, 0, 0)),
        pl.BlockSpec((1, groups, rows, tile), lambda j, i, p: (i[3], 0, 0, j)),
        pl.BlockSpec((groups, rows, tile), lambda j, i, p: (0, 0, j)),
        pl.BlockSpec((groups, rows, model), lambda j, i, p: (0, 0, 0)),
        pl.BlockSpec((groups, rows, 1), lambda j, i, p: (0, 0, 0)),
    ]
    if resident:
        out_shape += [pltpu.VMEM((model, width), bf16), pltpu.VMEM((width, model), bf16)]
        out_specs += [
            pl.BlockSpec((model, tile), lambda j, i, p: (0, j)),
            pl.BlockSpec((tile, model), lambda j, i, p: (j, 0)),
        ]
    return pl.pallas_call(
        body,
        grid_spec=pltpu.PrefetchScalarGridSpec(
            num_scalar_prefetch=2,
            grid=(width // tile,),
            in_specs=in_specs,
            out_specs=out_specs,
            scratch_shapes=[pltpu.VMEM((every, model), bf16), pltpu.VMEM((every, model), f32)],
        ),
        out_shape=out_shape,
        input_output_aliases=aliases,
        compiler_params=params(30),
        cost_estimate=pl.CostEstimate(
            flops=8 * every * model * width, bytes_accessed=4 * model * width, transcendentals=0
        ),
        name="forward",
    )(info, plan, *operands)


def sum_gradient(e, y, r):
    mean_e = jnp.mean(e, axis=-1, keepdims=True)
    mean_ey = jnp.mean(e * y, axis=-1, keepdims=True)
    return r * (e - mean_e - y * mean_ey)


columns_of_table = 6


def chain_step(call, table, recv, top_grad, saved, previous, after):
    base = call * columns_of_table
    slopes, ys, rs, w_up, w_down = saved
    rows, model = recv[0].shape
    width = w_up.shape[1]
    tile = tile_of(width)
    groups = slopes.shape[0]
    tokens = top_grad.shape[2]
    per = rows // tokens

    def body(info, *rest):
        recv_refs, rest = rest[: len(recv)], rest[len(recv) :]
        top_ref, y_ref, r_ref, slope_ref, p_ref, q_ref = rest[:6]
        out_ref, pre_ref, sum_ref, whole, low, total = rest[-6:]
        j = pl.program_id(0)
        active = info[base] > 0

        @pl.when(jnp.logical_and(active, j == 0))
        def _():
            top = top_ref[0].reshape(rows, model)
            e = jnp.where(info[base + 4] == 1, top, recv_refs[-1][...])
            if len(recv) > 1:
                e = jnp.where(info[base + 4] == 2, recv_refs[0][...], e)
            e = e.astype(f32)
            grad = sum_gradient(e, y_ref[0].astype(f32), r_ref[0])
            whole[...] = grad
            low[...] = grad.astype(bf16)
            sum_ref[0] = grad.astype(bf16)

        @pl.when(active)
        def _():
            grad_pre = (
                dot(low[...], q_ref[...], ((1,), (1,))) * slope_ref[0].astype(f32)
            ).astype(bf16)
            pre_ref[0] = grad_pre

            @pl.when(info[base + 5] > 0)
            def _():
                part = dot(grad_pre, p_ref[...], ((1,), (1,)))

                @pl.when(j == 0)
                def _():
                    total[...] = whole[...] + part

                @pl.when(j > 0)
                def _():
                    total[...] += part

                @pl.when(j == pl.num_programs(0) - 1)
                def _():
                    out_ref[...] = total[...].astype(bf16)

    in_specs = [pl.BlockSpec((rows, model), lambda j, i: (0, 0))] * len(recv) + [
        pl.BlockSpec((1, per, tokens, model), lambda j, i: (i[base + 1], i[base + 2], 0, 0)),
        pl.BlockSpec((1, rows, model), lambda j, i: (i[base + 2], 0, 0)),
        pl.BlockSpec((1, rows, 1), lambda j, i: (i[base + 2], 0, 0)),
        pl.BlockSpec((1, rows, tile), lambda j, i: (i[base + 2], 0, j * i[base])),
        pl.BlockSpec((model, tile), lambda j, i: (0, j * i[base + 5])),
        pl.BlockSpec((tile, model), lambda j, i: (j * i[base], 0)),
    ]
    operands = list(recv) + [in_hbm(top_grad)]
    operands += [in_vmem(x) for x in (ys, rs, slopes, w_up, w_down)]
    aliases = {}
    if previous is not None:
        aliases = {1 + len(operands): 1, 2 + len(operands): 2}
        in_specs += [any_space] * 2
        operands += [in_hbm(x) for x in previous]
    for x in after:
        if previous is None or not any(x is y for y in previous):
            in_specs.append(any_space)
            operands.append(in_hbm(x) if x.ndim > 2 else x)
    return pl.pallas_call(
        body,
        grid_spec=pltpu.PrefetchScalarGridSpec(
            num_scalar_prefetch=1,
            grid=(width // tile,),
            in_specs=in_specs,
            out_specs=[
                pl.BlockSpec((rows, model), lambda j, i: (0, 0)),
                pl.BlockSpec((1, rows, tile), lambda j, i: (i[base + 3], 0, j * i[base])),
                pl.BlockSpec((1, rows, model), lambda j, i: (i[base + 3], 0, 0)),
            ],
            scratch_shapes=[
                pltpu.VMEM((rows, model), f32),
                pltpu.VMEM((rows, model), bf16),
                pltpu.VMEM((rows, model), f32),
            ],
        ),
        out_shape=[
            jax.ShapeDtypeStruct((rows, model), bf16),
            pltpu.HBM((groups + 1, rows, width), bf16),
            pltpu.HBM((groups + 1, rows, model), bf16),
        ],
        input_output_aliases=aliases,
        compiler_params=params(20),
        cost_estimate=pl.CostEstimate(
            flops=8 * rows * model * width, bytes_accessed=4 * model * width, transcendentals=0
        ),
        name="chain",
    )(table, *operands)


def home_step(info, arrived, top_grad, saved, w_down, after):
    slopes, ys, rs = saved
    groups, rows, model = ys.shape
    micro, tokens = top_grad.shape[1:3]
    width = w_down.shape[2]
    tile = tile_of(width)

    def body(info, *refs):
        e_refs = refs[:groups]
        top_ref, y_ref, r_ref, slope_ref, q_ref = refs[groups : groups + 5]
        pre_ref, sum_ref = refs[-2:]

        @pl.when(pl.program_id(0) == 0)
        def _():
            for g in range(groups):
                top = top_ref[0].reshape(groups, rows, model)[g]
                e = jnp.where(info[0] > 0, top, e_refs[g][...]).astype(f32)
                grad = sum_gradient(e, y_ref[g].astype(f32), r_ref[g])
                sum_ref[g] = grad.astype(bf16)

        low = sum_ref[...].reshape(groups * rows, model)
        slope = slope_ref[...].reshape(groups * rows, tile)
        grad_pre = dot(low, q_ref[0, 0], ((1,), (1,))) * slope.astype(f32)
        pre_ref[...] = grad_pre.astype(bf16).reshape(pre_ref.shape)

    return pl.pallas_call(
        body,
        grid_spec=pltpu.PrefetchScalarGridSpec(
            num_scalar_prefetch=1,
            grid=(width // tile,),
            in_specs=[pl.BlockSpec((rows, model), lambda j, i: (0, 0))] * groups
            + [
                pl.BlockSpec((1, micro, tokens, model), lambda j, i: (1, 0, 0, 0)),
                pl.BlockSpec((groups, rows, model), lambda j, i: (0, 0, 0)),
                pl.BlockSpec((groups, rows, 1), lambda j, i: (0, 0, 0)),
                pl.BlockSpec((groups, rows, tile), lambda j, i: (0, 0, j)),
                pl.BlockSpec((1, 1, tile, model), lambda j, i: (0, 0, j, 0)),
            ]
            + [any_space] * len(after),
            out_specs=[
                pl.BlockSpec((groups, rows, tile), lambda j, i: (0, 0, j)),
                pl.BlockSpec((groups, rows, model), lambda j, i: (0, 0, 0)),
            ],
        ),
        out_shape=[
            pltpu.HBM((groups, rows, width), bf16),
            pltpu.HBM((groups, rows, model), bf16),
        ],
        compiler_params=params(28),
        cost_estimate=pl.CostEstimate(
            flops=4 * groups * rows * model * width,
            bytes_accessed=2 * model * width,
            transcendentals=0,
        ),
        name="home",
    )(
        info,
        *arrived,
        in_hbm(top_grad),
        *[in_vmem(x) for x in (ys, rs, slopes)],
        in_hbm(w_down),
        *[in_hbm(x) if x.ndim > 2 else x for x in after],
    )


def weight_gradient(left_a, right_a, left_b, right_b, groups, split_left, after):
    tokens = right_a.shape[-2]
    rows, columns = left_a.shape[-1], right_a.shape[-1]
    tile = tile_of(rows if split_left else columns)

    def body(la_ref, ra_ref, lb_ref, rb_ref, *rest):
        def flat(ref):
            return ref[...].reshape(-1, ref.shape[-1])

        total = dot(flat(la_ref), flat(ra_ref), ((0,), (0,)))
        total += dot(flat(lb_ref), flat(rb_ref), ((0,), (0,)))
        rest[-1][...] = total.astype(bf16)

    def spec(array, split):
        lead = array.ndim - 3
        block = (1,) * lead + (groups, tokens, tile if split else array.shape[-1])
        if split:
            return pl.BlockSpec(block, lambda j: (0,) * (lead + 2) + (j,))
        return pl.BlockSpec(block, lambda j: (0,) * (lead + 3))

    out_block = (tile, columns) if split_left else (rows, tile)
    return pl.pallas_call(
        body,
        grid=((rows if split_left else columns) // tile,),
        in_specs=[
            spec(left_a, split_left),
            spec(right_a, not split_left),
            spec(left_b, split_left),
            spec(right_b, not split_left),
        ]
        + [any_space] * len(after),
        out_specs=pl.BlockSpec(out_block, (lambda j: (j, 0)) if split_left else (lambda j: (0, j))),
        out_shape=pltpu.HBM((rows, columns), bf16),
        compiler_params=params(32),
        cost_estimate=pl.CostEstimate(
            flops=4 * groups * tokens * rows * columns,
            bytes_accessed=2 * rows * columns,
            transcendentals=0,
        ),
        name="weights",
    )(*[in_hbm(x) for x in (left_a, right_a, left_b, right_b)], *[in_hbm(x) for x in after])


def update(replica, weight, moment, total):
    _, rows, columns = moment.shape
    tile = min(64, rows)
    steps = rows // tile

    def body(info, weight_ref, moment_ref, total_ref, fresh_ref, out_ref):
        fresh_moment = momentum_decay * moment_ref[0] + total_ref[...].astype(f32)
        out_ref[0] = fresh_moment
        fresh_ref[...] = (weight_ref[0, 0].astype(f32) - step_size * fresh_moment).astype(bf16)

    return pl.pallas_call(
        body,
        grid_spec=pltpu.PrefetchScalarGridSpec(
            num_scalar_prefetch=1,
            grid=(steps,),
            in_specs=[
                pl.BlockSpec((1, 1, tile, columns), lambda j, i: (0, 0, i[0] * steps + j, 0)),
                pl.BlockSpec((1, tile, columns), lambda j, i: (0, j, 0)),
                pl.BlockSpec((tile, columns), lambda j, i: (j, 0)),
            ],
            out_specs=[
                pl.BlockSpec((tile, columns), lambda j, i: (j, 0)),
                pl.BlockSpec((1, tile, columns), lambda j, i: (0, j, 0)),
            ],
        ),
        out_shape=[
            jax.ShapeDtypeStruct((rows, columns), bf16),
            pltpu.HBM((1, rows, columns), f32),
        ],
        compiler_params=params(24),
        cost_estimate=pl.CostEstimate(
            flops=4 * rows * columns, bytes_accessed=12 * rows * columns, transcendentals=0
        ),
        name="update",
    )(replica, in_hbm(weight), in_hbm(moment), total)


def on_device(section_inputs, top_grad, plan, up_weight, down_weight, up_moment, down_moment):
    sections = lax.axis_size("section")
    position = lax.axis_index("section").astype(jnp.int32)
    micro, tokens, model = top_grad.shape[1:]
    plan = plan.astype(jnp.int32)
    per = 2 if micro % 2 == 0 else 1
    groups, rows = micro // per, per * tokens
    last, half = sections - 1, sections // 2

    def hop(value, pairs):
        return lax.ppermute(value, "section", pairs) if pairs else None

    mirrored = lax.ppermute(
        section_inputs[1, 0], "section", [(i, last - i) for i in range(sections)]
    )[None, None]

    upper = (position >= half).astype(jnp.int32)
    near = jnp.minimum(position, last - position)
    start = (near, last - near)
    relay = (1 - upper, upper)

    def begins(kind, i):
        return min(i, last - i) if kind == 0 else last - min(i, last - i)

    calls = [
        (tick, kind)
        for tick in range(groups + last)
        for kind in range(2)
        if any(0 <= tick - begins(kind, i) < groups for i in range(sections))
    ]
    ticks = np.array([tick for tick, _ in calls], np.int32)
    second = np.array([kind for _, kind in calls], np.int32)
    group = jnp.where(second == 1, ticks - start[1], ticks - start[0])
    of = jnp.where(second == 1, relay[1], relay[0])
    needless = jnp.logical_and(of == 1, position == last)
    active = (group >= 0) & (group < groups) & ~needless
    group = jnp.clip(group, 0, groups - 1)
    asked = active & ~((of == 0) & (position == 0))
    table = jnp.stack(
        [
            active.astype(jnp.int32),
            of,
            group,
            jnp.where(active & (of == 0), group, groups),
            jnp.where(
                jnp.where(of == 0, position == last, position == 0),
                1,
                jnp.where((second == 1) & (near == half - 1), 2, 0),
            ),
            asked.astype(jnp.int32),
        ],
        axis=1,
    ).reshape(-1)
    kinds = [jnp.stack([relay[k]] * 4) for k in range(2)]
    home_kind = jnp.array([0, 0, 1, 0], jnp.int32)

    blocks = None
    saved = [None, None]
    order = []

    def run_forward(kind, after):
        nonlocal blocks, order
        *blocks, slopes, ys, rs, w_up, w_down = forward(
            per, section_inputs, up_weight, down_weight, kinds[kind], plan, blocks, order + after, 2, True
        )
        saved[kind] = (slopes, ys, rs, w_up, w_down)
        order = [blocks[0]]

    late = []
    run_forward(0, [])
    blank = jnp.zeros((rows, model), bf16)
    received = {}
    arrived = {}
    kept = None
    for call, (tick, kind) in enumerate(calls):
        if kind == 1 and saved[1] is None:
            run_forward(1, [])
        if call == len(calls) - 1:
            *home_blocks, slopes, ys, rs = forward(
                per, mirrored, up_weight, down_weight, home_kind, plan, None, order + late, 1, False
            )
            saved_home = (slopes, ys, rs)
            order = [home_blocks[0]]

        def busy(i):
            return 0 <= tick - begins(kind, i) < groups

        recv = [
            received.pop((tick, kind, way))
            for way in range(2)
            if (tick, kind, way) in received
        ] or [blank]
        out, *kept = chain_step(call, table, recv, top_grad, saved[kind], kept, order)
        order = [kept[0]]
        relay_of = [(0 if i >= half else 1) if kind == 0 else (1 if i >= half else 0) for i in range(sections)]
        to = [i - 1 if relay_of[i] == 0 else i + 1 for i in range(sections)]
        live = [
            i
            for i in range(sections)
            if busy(i) and 0 <= to[i] <= last and not (relay_of[i] == 1 and to[i] == last)
        ]
        crossing = [i for i in live if kind == 0 and (i >= half) != (to[i] >= half)]
        for pairs, kind_after, way in (
            ([(i, to[i]) for i in live if i in crossing], 1, 0),
            ([(i, to[i]) for i in live if i not in crossing], kind, 1),
        ):
            got = hop(out, pairs)
            if got is not None:
                received[(tick + 1, kind_after, way)] = got
        pairs = [(i, last - 1 - i) for i in range(last) if busy(i) and relay_of[i] == 1]
        got = hop(out, pairs)
        if got is not None:
            for i, k in pairs:
                arrived[(k, tick - begins(kind, i))] = got
            if tick < half:
                late.append(got)
        if saved[1] is None and tick + 1 >= groups:
            run_forward(1, [mirrored[0, 0]])

    came = []
    for g in range(groups):
        options = []
        for k in range(last):
            value = arrived[(k, g)]
            if not any(value is x for x, _ in options):
                options.append((value, []))
            next(places for x, places in options if x is value).append(k)
        value = options[0][0]
        for other, places in options[1:]:
            here = either([position == k for k in places])
            value = jnp.where(here, other, value)
        came.append(value)
    home_pre, home_sum = home_step(
        (position == last).astype(jnp.int32)[None], came, top_grad, saved_home, down_weight, order
    )

    up_part = weight_gradient(blocks[0], kept[0], home_blocks[0], home_pre, groups, False, [])
    up_sum = lax.psum_scatter(up_part, "dp", scatter_dimension=0, tiled=True)
    down_part = weight_gradient(blocks[1], kept[1], home_blocks[1], home_sum, groups, True, [])
    down_sum = lax.psum_scatter(down_part, "dp", scatter_dimension=0, tiled=True)
    replica = lax.axis_index("dp").astype(jnp.int32)[None]

    def finish(weight, moment, total):
        fresh, fresh_moment = update(replica, weight, moment, total)
        far = lax.ppermute(fresh, "section", [(i, last - i) for i in range(sections)])
        return jnp.stack([fresh, far])[:, None], fresh_moment

    new_up_weight, new_up_moment = finish(up_weight, up_moment, up_sum)
    new_down_weight, new_down_moment = finish(down_weight, down_moment, down_sum)
    return (new_up_weight, new_down_weight, new_up_moment, new_down_moment)


def either(conditions):
    result = conditions[0]
    for condition in conditions[1:]:
        result = jnp.logical_or(result, condition)
    return result


def solution(mesh):
    in_specs = (
        P(None, "section", None, "dp", None),
        P(None, None, "dp", None),
        P(),
        P(None, "section", None, None),
        P(None, "section", None, None),
        P("section", "dp", None),
        P("section", "dp", None),
    )
    out_specs = (
        P(None, "section", "dp", None),
        P(None, "section", "dp", None),
        P("section", "dp", None),
        P("section", "dp", None),
    )
    return jax.shard_map(
        on_device, mesh=mesh, in_specs=in_specs, out_specs=out_specs, check_vma=False
    )
```

```python
import jax
import jax.numpy as jnp
import numpy as np
from jax import lax
from jax.experimental import pallas as pl
from jax.experimental.pallas import tpu as pltpu
from jax.sharding import PartitionSpec as P

norm_epsilon = 1e-06
momentum_decay = 0.9
step_size = 0.01
root_half = 0.7071067811865476
inv_root_tau = 0.3989422804014327

f32 = jnp.float32
bf16 = jnp.bfloat16
any_space = pl.BlockSpec(memory_space=pl.ANY)


def params(mib):
    return pltpu.CompilerParams(
        dimension_semantics=("arbitrary",), vmem_limit_bytes=mib * 1024 * 1024
    )


def in_vmem(x):
    return pltpu.with_memory_space_constraint(x, pltpu.VMEM)


def in_hbm(x):
    return pltpu.with_memory_space_constraint(x, pltpu.HBM)


def dot(left, right, over):
    return lax.dot_general(left, right, (over, ((), ())), preferred_element_type=f32)


def tile_of(width):
    return min(512, width)


def forward(per, inputs, w_up, w_down, info, plan, previous, after, places, resident):
    _, _, micro, tokens, model = inputs.shape
    width = w_up.shape[3]
    tile = tile_of(width)
    groups, rows, every = micro // per, per * tokens, micro * tokens

    def body(info_ref, plan_ref, *refs):
        u_refs = refs[:micro]
        p_ref, q_ref = refs[micro : micro + 2]
        outs = refs[len(operands) :]
        us_ref, h_ref, slope_ref, y_ref, r_ref = outs[:5]
        rows_ref, total = outs[-2:]
        j = pl.program_id(0)

        @pl.when(j == 0)
        def _():
            for k in range(micro):
                u = u_refs[k][0, 0, 0]
                rows_ref[k * tokens : (k + 1) * tokens] = u
                us_ref[0, k // per, k % per * tokens : (k % per + 1) * tokens] = u

        if resident:
            outs[5][...] = p_ref[0, 0]
            outs[6][...] = q_ref[0, 0]
        for g in range(groups):
            here = slice(g * rows, (g + 1) * rows)
            u = rows_ref[here]
            pre = dot(u, p_ref[0, 0], ((1,), (0,)))
            cdf = 0.5 * (1.0 + lax.erf(pre * root_half))
            hidden = (pre * cdf).astype(bf16)
            slope = cdf + pre * (jnp.exp(-0.5 * pre * pre) * inv_root_tau)
            h_ref[0, g] = hidden
            slope_ref[g] = slope.astype(bf16)
            part = dot(hidden, q_ref[0, 0], ((1,), (0,)))
            base = jnp.where(j == 0, u.astype(f32), total[here])
            total[here] = base + part

        @pl.when(j == pl.num_programs(0) - 1)
        def _():
            for g in range(groups):
                z = total[g * rows : (g + 1) * rows]
                centre = z - jnp.mean(z, axis=-1, keepdims=True)
                r = lax.rsqrt(jnp.mean(centre * centre, axis=-1, keepdims=True) + norm_epsilon)
                y_ref[g] = (centre * r).astype(bf16)
                r_ref[g] = r

    def u_spec(k):
        return pl.BlockSpec(
            (1, 1, 1, tokens, model), lambda j, i, p: (i[0], 0, p[i[2], k], 0, 0)
        )

    in_specs = [u_spec(k) for k in range(micro)] + [
        pl.BlockSpec((1, 1, model, tile), lambda j, i, p: (i[1], 0, 0, j)),
        pl.BlockSpec((1, 1, tile, model), lambda j, i, p: (i[1], 0, j, 0)),
    ]
    operands = [in_hbm(inputs)] * micro + [in_hbm(w_up), in_hbm(w_down)]
    aliases = {}
    if previous is not None:
        aliases = {2 + len(operands) + k: k for k in range(2)}
        in_specs += [any_space] * 2
        operands += [in_hbm(x) for x in previous]
    for x in after:
        in_specs.append(any_space)
        operands.append(in_hbm(x) if x.ndim > 2 else x)
    out_shape = [
        pltpu.HBM((places, groups, rows, model), bf16),
        pltpu.HBM((places, groups, rows, width), bf16),
        pltpu.VMEM((groups, rows, width), bf16),
        pltpu.VMEM((groups, rows, model), bf16),
        pltpu.VMEM((groups, rows, 1), f32),
    ]
    out_specs = [
        pl.BlockSpec((1, groups, rows, model), lambda j, i, p: (i[3], 0, 0, 0)),
        pl.BlockSpec((1, groups, rows, tile), lambda j, i, p: (i[3], 0, 0, j)),
        pl.BlockSpec((groups, rows, tile), lambda j, i, p: (0, 0, j)),
        pl.BlockSpec((groups, rows, model), lambda j, i, p: (0, 0, 0)),
        pl.BlockSpec((groups, rows, 1), lambda j, i, p: (0, 0, 0)),
    ]
    if resident:
        out_shape += [pltpu.VMEM((model, width), bf16), pltpu.VMEM((width, model), bf16)]
        out_specs += [
            pl.BlockSpec((model, tile), lambda j, i, p: (0, j)),
            pl.BlockSpec((tile, model), lambda j, i, p: (j, 0)),
        ]
    return pl.pallas_call(
        body,
        grid_spec=pltpu.PrefetchScalarGridSpec(
            num_scalar_prefetch=2,
            grid=(width // tile,),
            in_specs=in_specs,
            out_specs=out_specs,
            scratch_shapes=[pltpu.VMEM((every, model), bf16), pltpu.VMEM((every, model), f32)],
        ),
        out_shape=out_shape,
        input_output_aliases=aliases,
        compiler_params=params(30),
        cost_estimate=pl.CostEstimate(
            flops=8 * every * model * width, bytes_accessed=4 * model * width, transcendentals=0
        ),
        name="forward",
    )(info, plan, *operands)


def sum_gradient(e, y, r):
    mean_e = jnp.mean(e, axis=-1, keepdims=True)
    mean_ey = jnp.mean(e * y, axis=-1, keepdims=True)
    return r * (e - mean_e - y * mean_ey)


columns_of_table = 4


def chain_step(call, group, table, recv, top_grad, saved, previous, after):
    base = call * columns_of_table
    slopes, ys, rs, w_up, w_down = saved
    groups, rows, model = ys.shape
    width = w_up.shape[1]
    tile = tile_of(width)
    tokens = top_grad.shape[2]
    per = rows // tokens

    def body(info, e_ref, y_ref, r_ref, slope_ref, p_ref, q_ref, *rest):
        out_ref, pre_ref, sum_ref, whole, low, total = rest[-6:]
        j = pl.program_id(0)
        active = info[base] > 0

        @pl.when(jnp.logical_and(active, j == 0))
        def _():
            e = e_ref[...].reshape(rows, model).astype(f32)
            grad = sum_gradient(e, y_ref[0].astype(f32), r_ref[0])
            whole[...] = grad
            low[...] = grad.astype(bf16)
            sum_ref[0] = grad.astype(bf16)

        @pl.when(active)
        def _():
            grad_pre = (
                dot(low[...], q_ref[...], ((1,), (1,))) * slope_ref[0].astype(f32)
            ).astype(bf16)
            pre_ref[0] = grad_pre

            @pl.when(info[base + 3] > 0)
            def _():
                part = dot(grad_pre, p_ref[...], ((1,), (1,)))

                @pl.when(j == 0)
                def _():
                    total[...] = whole[...] + part

                @pl.when(j > 0)
                def _():
                    total[...] += part

                @pl.when(j == pl.num_programs(0) - 1)
                def _():
                    out_ref[...] = total[...].astype(bf16)

    if recv is None:
        e_spec = pl.BlockSpec((1, per, tokens, model), lambda j, i: (i[base + 1], group, 0, 0))
        operands = [in_hbm(top_grad)]
    else:
        e_spec = pl.BlockSpec((rows, model), lambda j, i: (0, 0))
        operands = [recv]
    in_specs = [
        e_spec,
        pl.BlockSpec((1, rows, model), lambda j, i: (group, 0, 0)),
        pl.BlockSpec((1, rows, 1), lambda j, i: (group, 0, 0)),
        pl.BlockSpec((1, rows, tile), lambda j, i: (group, 0, j * i[base])),
        pl.BlockSpec((model, tile), lambda j, i: (0, j * i[base + 3])),
        pl.BlockSpec((tile, model), lambda j, i: (j * i[base], 0)),
    ]
    operands += [in_vmem(x) for x in (ys, rs, slopes, w_up, w_down)]
    aliases = {}
    if previous is not None:
        aliases = {1 + len(operands): 1, 2 + len(operands): 2}
        in_specs += [any_space] * 2
        operands += [in_hbm(x) for x in previous]
    for x in after:
        if previous is None or not any(x is y for y in previous):
            in_specs.append(any_space)
            operands.append(in_hbm(x) if x.ndim > 2 else x)
    return pl.pallas_call(
        body,
        grid_spec=pltpu.PrefetchScalarGridSpec(
            num_scalar_prefetch=1,
            grid=(width // tile,),
            in_specs=in_specs,
            out_specs=[
                pl.BlockSpec((rows, model), lambda j, i: (0, 0)),
                pl.BlockSpec((1, rows, tile), lambda j, i: (i[base + 2], 0, j * i[base])),
                pl.BlockSpec((1, rows, model), lambda j, i: (i[base + 2], 0, 0)),
            ],
            scratch_shapes=[
                pltpu.VMEM((rows, model), f32),
                pltpu.VMEM((rows, model), bf16),
                pltpu.VMEM((rows, model), f32),
            ],
        ),
        out_shape=[
            jax.ShapeDtypeStruct((rows, model), bf16),
            pltpu.HBM((groups + 1, rows, width), bf16),
            pltpu.HBM((groups + 1, rows, model), bf16),
        ],
        input_output_aliases=aliases,
        compiler_params=params(20),
        cost_estimate=pl.CostEstimate(
            flops=8 * rows * model * width, bytes_accessed=4 * model * width, transcendentals=0
        ),
        name="chain",
    )(table, *operands)


def home_step(info, arrived, top_grad, saved, w_down, after):
    slopes, ys, rs = saved
    groups, rows, model = ys.shape
    micro, tokens = top_grad.shape[1:3]
    width = w_down.shape[2]
    tile = tile_of(width)

    def body(info, *refs):
        e_refs = refs[:groups]
        top_ref, y_ref, r_ref, slope_ref, q_ref = refs[groups : groups + 5]
        pre_ref, sum_ref = refs[-2:]

        @pl.when(pl.program_id(0) == 0)
        def _():
            for g in range(groups):
                top = top_ref[0].reshape(groups, rows, model)[g]
                e = jnp.where(info[0] > 0, top, e_refs[g][...]).astype(f32)
                grad = sum_gradient(e, y_ref[g].astype(f32), r_ref[g])
                sum_ref[g] = grad.astype(bf16)

        low = sum_ref[...].reshape(groups * rows, model)
        slope = slope_ref[...].reshape(groups * rows, tile)
        grad_pre = dot(low, q_ref[0, 0], ((1,), (1,))) * slope.astype(f32)
        pre_ref[...] = grad_pre.astype(bf16).reshape(pre_ref.shape)

    return pl.pallas_call(
        body,
        grid_spec=pltpu.PrefetchScalarGridSpec(
            num_scalar_prefetch=1,
            grid=(width // tile,),
            in_specs=[pl.BlockSpec((rows, model), lambda j, i: (0, 0))] * groups
            + [
                pl.BlockSpec((1, micro, tokens, model), lambda j, i: (1, 0, 0, 0)),
                pl.BlockSpec((groups, rows, model), lambda j, i: (0, 0, 0)),
                pl.BlockSpec((groups, rows, 1), lambda j, i: (0, 0, 0)),
                pl.BlockSpec((groups, rows, tile), lambda j, i: (0, 0, j)),
                pl.BlockSpec((1, 1, tile, model), lambda j, i: (0, 0, j, 0)),
            ]
            + [any_space] * len(after),
            out_specs=[
                pl.BlockSpec((groups, rows, tile), lambda j, i: (0, 0, j)),
                pl.BlockSpec((groups, rows, model), lambda j, i: (0, 0, 0)),
            ],
        ),
        out_shape=[
            pltpu.HBM((groups, rows, width), bf16),
            pltpu.HBM((groups, rows, model), bf16),
        ],
        compiler_params=params(28),
        cost_estimate=pl.CostEstimate(
            flops=4 * groups * rows * model * width,
            bytes_accessed=2 * model * width,
            transcendentals=0,
        ),
        name="home",
    )(
        info,
        *arrived,
        in_hbm(top_grad),
        *[in_vmem(x) for x in (ys, rs, slopes)],
        in_hbm(w_down),
        *[in_hbm(x) if x.ndim > 2 else x for x in after],
    )


def weight_gradient(left_a, right_a, left_b, right_b, groups, split_left, after):
    tokens = right_a.shape[-2]
    rows, columns = left_a.shape[-1], right_a.shape[-1]
    tile = tile_of(rows if split_left else columns)

    def body(la_ref, ra_ref, lb_ref, rb_ref, *rest):
        def flat(ref):
            return ref[...].reshape(-1, ref.shape[-1])

        total = dot(flat(la_ref), flat(ra_ref), ((0,), (0,)))
        total += dot(flat(lb_ref), flat(rb_ref), ((0,), (0,)))
        rest[-1][...] = total.astype(bf16)

    def spec(array, split):
        lead = array.ndim - 3
        block = (1,) * lead + (groups, tokens, tile if split else array.shape[-1])
        if split:
            return pl.BlockSpec(block, lambda j: (0,) * (lead + 2) + (j,))
        return pl.BlockSpec(block, lambda j: (0,) * (lead + 3))

    out_block = (tile, columns) if split_left else (rows, tile)
    return pl.pallas_call(
        body,
        grid=((rows if split_left else columns) // tile,),
        in_specs=[
            spec(left_a, split_left),
            spec(right_a, not split_left),
            spec(left_b, split_left),
            spec(right_b, not split_left),
        ]
        + [any_space] * len(after),
        out_specs=pl.BlockSpec(out_block, (lambda j: (j, 0)) if split_left else (lambda j: (0, j))),
        out_shape=pltpu.HBM((rows, columns), bf16),
        compiler_params=params(32),
        cost_estimate=pl.CostEstimate(
            flops=4 * groups * tokens * rows * columns,
            bytes_accessed=2 * rows * columns,
            transcendentals=0,
        ),
        name="weights",
    )(*[in_hbm(x) for x in (left_a, right_a, left_b, right_b)], *[in_hbm(x) for x in after])


def update(replica, weight, moment, total):
    _, rows, columns = moment.shape
    tile = min(64, rows)
    steps = rows // tile

    def body(info, weight_ref, moment_ref, total_ref, fresh_ref, out_ref):
        fresh_moment = momentum_decay * moment_ref[0] + total_ref[...].astype(f32)
        out_ref[0] = fresh_moment
        fresh_ref[...] = (weight_ref[0, 0].astype(f32) - step_size * fresh_moment).astype(bf16)

    return pl.pallas_call(
        body,
        grid_spec=pltpu.PrefetchScalarGridSpec(
            num_scalar_prefetch=1,
            grid=(steps,),
            in_specs=[
                pl.BlockSpec((1, 1, tile, columns), lambda j, i: (0, 0, i[0] * steps + j, 0)),
                pl.BlockSpec((1, tile, columns), lambda j, i: (0, j, 0)),
                pl.BlockSpec((tile, columns), lambda j, i: (j, 0)),
            ],
            out_specs=[
                pl.BlockSpec((tile, columns), lambda j, i: (j, 0)),
                pl.BlockSpec((1, tile, columns), lambda j, i: (0, j, 0)),
            ],
        ),
        out_shape=[
            jax.ShapeDtypeStruct((rows, columns), bf16),
            pltpu.HBM((1, rows, columns), f32),
        ],
        compiler_params=params(24),
        cost_estimate=pl.CostEstimate(
            flops=4 * rows * columns, bytes_accessed=12 * rows * columns, transcendentals=0
        ),
        name="update",
    )(replica, in_hbm(weight), in_hbm(moment), total)


def on_device(section_inputs, top_grad, plan, up_weight, down_weight, up_moment, down_moment):
    sections = lax.axis_size("section")
    position = lax.axis_index("section").astype(jnp.int32)
    micro, tokens, model = top_grad.shape[1:]
    plan = plan.astype(jnp.int32)
    per = 2 if micro % 2 == 0 else 1
    groups, rows = micro // per, per * tokens
    last, half = sections - 1, sections // 2

    def hop(value, pairs):
        return lax.ppermute(value, "section", pairs) if pairs else None

    mirrored = lax.ppermute(
        section_inputs[1, 0], "section", [(i, last - i) for i in range(sections)]
    )[None, None]

    upper = (position >= half).astype(jnp.int32)
    relay = (1 - upper, upper)
    calls = [(stage, group) for stage in range(sections) for group in range(groups)]
    stages = np.array([stage for stage, _ in calls], np.int32)
    own = np.array([group for _, group in calls], np.int32)
    of = jnp.where(stages < half, relay[0], relay[1])
    active = (jnp.where(of == 0, last - position, position) == stages) & ~(
        (of == 1) & (position == last)
    )
    table = jnp.stack(
        [
            active.astype(jnp.int32),
            of,
            jnp.where(active & (of == 0), own, groups),
            (active & (stages < last)).astype(jnp.int32),
        ],
        axis=1,
    ).reshape(-1)
    kinds = [jnp.stack([relay[k]] * 4) for k in range(2)]
    home_kind = jnp.array([0, 0, 1, 0], jnp.int32)

    blocks = None
    saved = [None, None]
    order = []

    def run_forward(kind, after):
        nonlocal blocks, order
        *blocks, slopes, ys, rs, w_up, w_down = forward(
            per, section_inputs, up_weight, down_weight, kinds[kind], plan, blocks, after, 2, True
        )
        saved[kind] = (slopes, ys, rs, w_up, w_down)
        order = [blocks[0]]

    run_forward(0, [])
    late = []
    received = {}
    arrived = {}
    kept = None
    for call, (stage, group) in enumerate(calls):
        if stage == last and group == 0:
            *home_blocks, slopes, ys, rs = forward(
                per, mirrored, up_weight, down_weight, home_kind, plan, None, order + late, 1, False
            )
            saved_home = (slopes, ys, rs)
            order = [home_blocks[0]]
        recv = received.pop((stage, group), None)
        out, *kept = chain_step(
            call, group, table, recv, top_grad, saved[int(stage >= half)], kept, order
        )
        order = [kept[0]]
        pairs = [(last - stage, last - stage - 1)] if stage < last else []
        if stage < last - 1:
            pairs.append((stage, stage + 1))
        got = hop(out, pairs)
        if got is not None:
            received[(stage + 1, group)] = got
        if stage < last:
            got = hop(out, [(stage, last - 1 - stage)])
            arrived[(last - 1 - stage, group)] = got
            if stage < half:
                late.append(got)
        if saved[1] is None and group == groups - 1:
            run_forward(1, order + [mirrored[0, 0]])

    came = []
    for group in range(groups):
        value = arrived[(0, group)]
        for k in range(1, last):
            value = jnp.where(position == k, arrived[(k, group)], value)
        came.append(value)
    home_pre, home_sum = home_step(
        (position == last).astype(jnp.int32)[None], came, top_grad, saved_home, down_weight, order
    )

    up_part = weight_gradient(blocks[0], kept[0], home_blocks[0], home_pre, groups, False, [])
    up_sum = lax.psum_scatter(up_part, "dp", scatter_dimension=0, tiled=True)
    down_part = weight_gradient(blocks[1], kept[1], home_blocks[1], home_sum, groups, True, [])
    down_sum = lax.psum_scatter(down_part, "dp", scatter_dimension=0, tiled=True)
    replica = lax.axis_index("dp").astype(jnp.int32)[None]

    def finish(weight, moment, total):
        fresh, fresh_moment = update(replica, weight, moment, total)
        far = lax.ppermute(fresh, "section", [(i, last - i) for i in range(sections)])
        return jnp.stack([fresh, far])[:, None], fresh_moment

    new_up_weight, new_up_moment = finish(up_weight, up_moment, up_sum)
    new_down_weight, new_down_moment = finish(down_weight, down_moment, down_sum)
    return (new_up_weight, new_down_weight, new_up_moment, new_down_moment)


def solution(mesh):
    in_specs = (
        P(None, "section", None, "dp", None),
        P(None, None, "dp", None),
        P(),
        P(None, "section", None, None),
        P(None, "section", None, None),
        P("section", "dp", None),
        P("section", "dp", None),
    )
    out_specs = (
        P(None, "section", "dp", None),
        P(None, "section", "dp", None),
        P("section", "dp", None),
        P("section", "dp", None),
    )
    return jax.shard_map(
        on_device, mesh=mesh, in_specs=in_specs, out_specs=out_specs, check_vma=False
    )
```

```python
import jax
import jax.numpy as jnp
import numpy as np
from jax import lax
from jax.experimental import pallas as pl
from jax.experimental.pallas import tpu as pltpu
from jax.sharding import PartitionSpec as P

norm_epsilon = 1e-06
momentum_decay = 0.9
step_size = 0.01
root_half = 0.7071067811865476
inv_root_tau = 0.3989422804014327

f32 = jnp.float32
bf16 = jnp.bfloat16
any_space = pl.BlockSpec(memory_space=pl.ANY)


def params(mib):
    return pltpu.CompilerParams(
        dimension_semantics=("arbitrary",), vmem_limit_bytes=mib * 1024 * 1024
    )


def in_vmem(x):
    return pltpu.with_memory_space_constraint(x, pltpu.VMEM)


def in_hbm(x):
    return pltpu.with_memory_space_constraint(x, pltpu.HBM)


def dot(left, right, over):
    return lax.dot_general(left, right, (over, ((), ())), preferred_element_type=f32)


def tile_of(width, most=512):
    return min(most, width)


def forward(per, inputs, w_up, w_down, info, plan, previous, after, places, resident):
    _, _, micro, tokens, model = inputs.shape
    width = w_up.shape[3]
    tile = tile_of(width, 256)
    groups, rows, every = micro // per, per * tokens, micro * tokens

    def body(info_ref, plan_ref, *refs):
        u_refs = refs[:micro]
        p_ref, q_ref = refs[micro : micro + 2]
        outs = refs[len(operands) :]
        us_ref, h_ref, slope_ref, y_ref, r_ref = outs[:5]
        rows_ref, total = outs[-2:]
        j = pl.program_id(0)

        @pl.when(j == 0)
        def _():
            for k in range(micro):
                u = u_refs[k][0, 0, 0]
                rows_ref[k * tokens : (k + 1) * tokens] = u
                us_ref[0, k // per, k % per * tokens : (k % per + 1) * tokens] = u

        if resident:
            outs[5][...] = p_ref[0, 0]
            outs[6][...] = q_ref[0, 0]
        for g in range(groups):
            here = slice(g * rows, (g + 1) * rows)
            u = rows_ref[here]
            pre = dot(u, p_ref[0, 0], ((1,), (0,)))
            cdf = 0.5 * (1.0 + lax.erf(pre * root_half))
            hidden = (pre * cdf).astype(bf16)
            slope = cdf + pre * (jnp.exp(-0.5 * pre * pre) * inv_root_tau)
            h_ref[0, g] = hidden
            slope_ref[g] = slope.astype(bf16)
            part = dot(hidden, q_ref[0, 0], ((1,), (0,)))
            base = jnp.where(j == 0, u.astype(f32), total[here])
            total[here] = base + part

        @pl.when(j == pl.num_programs(0) - 1)
        def _():
            for g in range(groups):
                z = total[g * rows : (g + 1) * rows]
                centre = z - jnp.mean(z, axis=-1, keepdims=True)
                r = lax.rsqrt(jnp.mean(centre * centre, axis=-1, keepdims=True) + norm_epsilon)
                y_ref[g] = (centre * r).astype(bf16)
                r_ref[g] = r

    def u_spec(k):
        return pl.BlockSpec(
            (1, 1, 1, tokens, model), lambda j, i, p: (i[0], 0, p[i[2], k], 0, 0)
        )

    in_specs = [u_spec(k) for k in range(micro)] + [
        pl.BlockSpec((1, 1, model, tile), lambda j, i, p: (i[1], 0, 0, j)),
        pl.BlockSpec((1, 1, tile, model), lambda j, i, p: (i[1], 0, j, 0)),
    ]
    operands = [in_hbm(inputs)] * micro + [in_hbm(w_up), in_hbm(w_down)]
    aliases = {}
    if previous is not None:
        aliases = {2 + len(operands) + k: k for k in range(2)}
        in_specs += [any_space] * 2
        operands += [in_hbm(x) for x in previous]
    for x in after:
        in_specs.append(any_space)
        operands.append(in_hbm(x) if x.ndim > 2 else x)
    out_shape = [
        pltpu.HBM((places, groups, rows, model), bf16),
        pltpu.HBM((places, groups, rows, width), bf16),
        pltpu.VMEM((groups, rows, width), bf16),
        pltpu.VMEM((groups, rows, model), bf16),
        pltpu.VMEM((groups, rows, 1), f32),
    ]
    out_specs = [
        pl.BlockSpec((1, groups, rows, model), lambda j, i, p: (i[3], 0, 0, 0)),
        pl.BlockSpec((1, groups, rows, tile), lambda j, i, p: (i[3], 0, 0, j)),
        pl.BlockSpec((groups, rows, tile), lambda j, i, p: (0, 0, j)),
        pl.BlockSpec((groups, rows, model), lambda j, i, p: (0, 0, 0)),
        pl.BlockSpec((groups, rows, 1), lambda j, i, p: (0, 0, 0)),
    ]
    if resident:
        out_shape += [pltpu.VMEM((model, width), bf16), pltpu.VMEM((width, model), bf16)]
        out_specs += [
            pl.BlockSpec((model, tile), lambda j, i, p: (0, j)),
            pl.BlockSpec((tile, model), lambda j, i, p: (j, 0)),
        ]
    return pl.pallas_call(
        body,
        grid_spec=pltpu.PrefetchScalarGridSpec(
            num_scalar_prefetch=2,
            grid=(width // tile,),
            in_specs=in_specs,
            out_specs=out_specs,
            scratch_shapes=[pltpu.VMEM((every, model), bf16), pltpu.VMEM((every, model), f32)],
        ),
        out_shape=out_shape,
        input_output_aliases=aliases,
        compiler_params=params(20),
        cost_estimate=pl.CostEstimate(
            flops=8 * every * model * width, bytes_accessed=4 * model * width, transcendentals=0
        ),
        name="forward",
    )(info, plan, *operands)


def sum_gradient(e, y, r):
    mean_e = jnp.mean(e, axis=-1, keepdims=True)
    mean_ey = jnp.mean(e * y, axis=-1, keepdims=True)
    return r * (e - mean_e - y * mean_ey)


columns_of_table = 4


def chain_step(call, group, table, recv, top_grad, saved, previous, after):
    base = call * columns_of_table
    slopes, ys, rs, w_up, w_down = saved
    groups, rows, model = ys.shape
    width = w_up.shape[1]
    tile = tile_of(width)
    tokens = top_grad.shape[2]
    per = rows // tokens

    def body(info, e_ref, y_ref, r_ref, slope_ref, p_ref, q_ref, *rest):
        out_ref, pre_ref, sum_ref, whole, low, total = rest[-6:]
        j = pl.program_id(0)
        active = info[base] > 0

        @pl.when(jnp.logical_and(active, j == 0))
        def _():
            e = e_ref[...].reshape(rows, model).astype(f32)
            grad = sum_gradient(e, y_ref[0].astype(f32), r_ref[0])
            whole[...] = grad
            low[...] = grad.astype(bf16)
            sum_ref[0] = grad.astype(bf16)

        @pl.when(active)
        def _():
            grad_pre = (
                dot(low[...], q_ref[...], ((1,), (1,))) * slope_ref[0].astype(f32)
            ).astype(bf16)
            pre_ref[0] = grad_pre

            @pl.when(info[base + 3] > 0)
            def _():
                part = dot(grad_pre, p_ref[...], ((1,), (1,)))

                @pl.when(j == 0)
                def _():
                    total[...] = whole[...] + part

                @pl.when(j > 0)
                def _():
                    total[...] += part

                @pl.when(j == pl.num_programs(0) - 1)
                def _():
                    out_ref[...] = total[...].astype(bf16)

    if recv is None:
        e_spec = pl.BlockSpec((1, per, tokens, model), lambda j, i: (i[base + 1], group, 0, 0))
        operands = [in_hbm(top_grad)]
    else:
        e_spec = pl.BlockSpec((rows, model), lambda j, i: (0, 0))
        operands = [recv]
    in_specs = [
        e_spec,
        pl.BlockSpec((1, rows, model), lambda j, i: (group, 0, 0)),
        pl.BlockSpec((1, rows, 1), lambda j, i: (group, 0, 0)),
        pl.BlockSpec((1, rows, tile), lambda j, i: (group, 0, j * i[base])),
        pl.BlockSpec((model, tile), lambda j, i: (0, j * i[base + 3])),
        pl.BlockSpec((tile, model), lambda j, i: (j * i[base], 0)),
    ]
    operands += [in_vmem(x) for x in (ys, rs, slopes, w_up, w_down)]
    aliases = {}
    if previous is not None:
        aliases = {1 + len(operands): 1, 2 + len(operands): 2}
        in_specs += [any_space] * 2
        operands += [in_hbm(x) for x in previous]
    for x in after:
        if previous is None or not any(x is y for y in previous):
            in_specs.append(any_space)
            operands.append(in_hbm(x) if x.ndim > 2 else x)
    return pl.pallas_call(
        body,
        grid_spec=pltpu.PrefetchScalarGridSpec(
            num_scalar_prefetch=1,
            grid=(width // tile,),
            in_specs=in_specs,
            out_specs=[
                pl.BlockSpec((rows, model), lambda j, i: (0, 0)),
                pl.BlockSpec((1, rows, tile), lambda j, i: (i[base + 2], 0, j * i[base])),
                pl.BlockSpec((1, rows, model), lambda j, i: (i[base + 2], 0, 0)),
            ],
            scratch_shapes=[
                pltpu.VMEM((rows, model), f32),
                pltpu.VMEM((rows, model), bf16),
                pltpu.VMEM((rows, model), f32),
            ],
        ),
        out_shape=[
            jax.ShapeDtypeStruct((rows, model), bf16),
            pltpu.HBM((groups + 1, rows, width), bf16),
            pltpu.HBM((groups + 1, rows, model), bf16),
        ],
        input_output_aliases=aliases,
        compiler_params=params(16),
        cost_estimate=pl.CostEstimate(
            flops=8 * rows * model * width, bytes_accessed=4 * model * width, transcendentals=0
        ),
        name="chain",
    )(table, *operands)


def home_step(info, arrived, top_grad, saved, w_down, after):
    slopes, ys, rs = saved
    groups, rows, model = ys.shape
    micro, tokens = top_grad.shape[1:3]
    width = w_down.shape[2]
    tile = tile_of(width)

    def body(info, *refs):
        e_refs = refs[:groups]
        top_ref, y_ref, r_ref, slope_ref, q_ref = refs[groups : groups + 5]
        pre_ref, sum_ref = refs[-2:]

        @pl.when(pl.program_id(0) == 0)
        def _():
            for g in range(groups):
                top = top_ref[0].reshape(groups, rows, model)[g]
                e = jnp.where(info[0] > 0, top, e_refs[g][...]).astype(f32)
                grad = sum_gradient(e, y_ref[g].astype(f32), r_ref[g])
                sum_ref[g] = grad.astype(bf16)

        low = sum_ref[...].reshape(groups * rows, model)
        slope = slope_ref[...].reshape(groups * rows, tile)
        grad_pre = dot(low, q_ref[0, 0], ((1,), (1,))) * slope.astype(f32)
        pre_ref[...] = grad_pre.astype(bf16).reshape(pre_ref.shape)

    return pl.pallas_call(
        body,
        grid_spec=pltpu.PrefetchScalarGridSpec(
            num_scalar_prefetch=1,
            grid=(width // tile,),
            in_specs=[pl.BlockSpec((rows, model), lambda j, i: (0, 0))] * groups
            + [
                pl.BlockSpec((1, micro, tokens, model), lambda j, i: (1, 0, 0, 0)),
                pl.BlockSpec((groups, rows, model), lambda j, i: (0, 0, 0)),
                pl.BlockSpec((groups, rows, 1), lambda j, i: (0, 0, 0)),
                pl.BlockSpec((groups, rows, tile), lambda j, i: (0, 0, j)),
                pl.BlockSpec((1, 1, tile, model), lambda j, i: (0, 0, j, 0)),
            ]
            + [any_space] * len(after),
            out_specs=[
                pl.BlockSpec((groups, rows, tile), lambda j, i: (0, 0, j)),
                pl.BlockSpec((groups, rows, model), lambda j, i: (0, 0, 0)),
            ],
        ),
        out_shape=[
            pltpu.HBM((groups, rows, width), bf16),
            pltpu.HBM((groups, rows, model), bf16),
        ],
        compiler_params=params(20),
        cost_estimate=pl.CostEstimate(
            flops=4 * groups * rows * model * width,
            bytes_accessed=2 * model * width,
            transcendentals=0,
        ),
        name="home",
    )(
        info,
        *arrived,
        in_hbm(top_grad),
        *[in_vmem(x) for x in (ys, rs, slopes)],
        in_hbm(w_down),
        *[in_hbm(x) if x.ndim > 2 else x for x in after],
    )


def weight_gradient(core, left_a, right_a, left_b, right_b, groups, replicas, split_left, came):
    tokens = right_a.shape[-2]
    rows, columns = left_a.shape[-1] // replicas, right_a.shape[-1]
    lines = replicas // 2
    tile = columns if split_left else tile_of(columns)
    steps = lines if split_left else columns // tile
    lefts = 1 if split_left else lines
    pair = rows % 128 != 0
    wide = 2 * rows if pair else rows

    def place(z, i):
        return z if pair else 2 * z + i[0]

    def body(info, *refs):
        def flat(ref):
            return ref[...].reshape(-1, ref.shape[-1])

        def product(left_refs, right_ref):
            left = [flat(ref) for ref in left_refs]
            if pair:
                left = [jnp.where(info[0] == 0, x[:, :rows], x[:, rows:]) for x in left]
            left = left[0] if len(left) == 1 else jnp.concatenate(left, axis=1)
            return dot(left, flat(right_ref), ((0,), (0,)))

        total = product(refs[:lefts], refs[lefts])
        total += product(refs[lefts + 1 : 2 * lefts + 1], refs[2 * lefts + 1])
        total = total.reshape(lefts, rows, tile)
        if came is not None:
            total += refs[2 * lefts + 2][...].astype(f32)
        refs[-1][...] = total.astype(bf16)

    def left_specs(array):
        lead = array.ndim - 3
        block = (1,) * lead + (groups, tokens, wide)
        if split_left:
            return [pl.BlockSpec(block, lambda j, i: (0,) * (lead + 2) + (place(j, i),))]
        return [
            pl.BlockSpec(block, lambda j, i, z=z: (0,) * (lead + 2) + (place(z, i),))
            for z in range(lines)
        ]

    def right_spec(array):
        lead = array.ndim - 3
        block = (1,) * lead + (groups, tokens, tile)
        if split_left:
            return pl.BlockSpec(block, lambda j, i: (0,) * (lead + 3))
        return pl.BlockSpec(block, lambda j, i: (0,) * (lead + 2) + (j,))

    if split_left:
        out_spec = pl.BlockSpec((1, rows, tile), lambda j, i: (j, 0, 0))
    else:
        out_spec = pl.BlockSpec((lines, rows, tile), lambda j, i: (0, 0, j))
    operands = [in_hbm(left_a)] * lefts + [in_hbm(right_a)]
    operands += [in_hbm(left_b)] * lefts + [in_hbm(right_b)]
    in_specs = left_specs(left_a) + [right_spec(right_a)]
    in_specs += left_specs(left_b) + [right_spec(right_b)]
    if came is not None:
        operands.append(came)
        in_specs.append(out_spec)
    return pl.pallas_call(
        body,
        grid_spec=pltpu.PrefetchScalarGridSpec(
            num_scalar_prefetch=1, grid=(steps,), in_specs=in_specs, out_specs=out_spec
        ),
        out_shape=jax.ShapeDtypeStruct((lines, rows, columns), bf16),
        compiler_params=params(28),
        cost_estimate=pl.CostEstimate(
            flops=4 * groups * tokens * rows * lines * columns,
            bytes_accessed=2 * rows * lines * columns,
            transcendentals=0,
        ),
        name="weights",
    )(core, *operands)


def update(replica, weight, moment, total):
    _, rows, columns = moment.shape
    tile = min(64, rows)
    steps = rows // tile

    def body(info, weight_ref, moment_ref, total_ref, fresh_ref, out_ref):
        fresh_moment = momentum_decay * moment_ref[0] + total_ref[...].astype(f32)
        out_ref[0] = fresh_moment
        fresh_ref[...] = (weight_ref[0, 0].astype(f32) - step_size * fresh_moment).astype(bf16)

    return pl.pallas_call(
        body,
        grid_spec=pltpu.PrefetchScalarGridSpec(
            num_scalar_prefetch=1,
            grid=(steps,),
            in_specs=[
                pl.BlockSpec((1, 1, tile, columns), lambda j, i: (0, 0, i[0] * steps + j, 0)),
                pl.BlockSpec((1, tile, columns), lambda j, i: (0, j, 0)),
                pl.BlockSpec((tile, columns), lambda j, i: (j, 0)),
            ],
            out_specs=[
                pl.BlockSpec((tile, columns), lambda j, i: (j, 0)),
                pl.BlockSpec((1, tile, columns), lambda j, i: (0, j, 0)),
            ],
        ),
        out_shape=[
            jax.ShapeDtypeStruct((rows, columns), bf16),
            pltpu.HBM((1, rows, columns), f32),
        ],
        compiler_params=params(24),
        cost_estimate=pl.CostEstimate(
            flops=4 * rows * columns, bytes_accessed=12 * rows * columns, transcendentals=0
        ),
        name="update",
    )(replica, in_hbm(weight), in_hbm(moment), total)


def on_device(section_inputs, top_grad, plan, up_weight, down_weight, up_moment, down_moment):
    sections = lax.axis_size("section")
    position = lax.axis_index("section").astype(jnp.int32)
    micro, tokens, model = top_grad.shape[1:]
    plan = plan.astype(jnp.int32)
    per = 2 if micro % 2 == 0 else 1
    groups, rows = micro // per, per * tokens
    last, half = sections - 1, sections // 2

    def hop(value, pairs):
        return lax.ppermute(value, "section", pairs) if pairs else None

    mirrored = lax.ppermute(
        section_inputs[1, 0], "section", [(i, last - i) for i in range(sections)]
    )[None, None]

    upper = (position >= half).astype(jnp.int32)
    relay = (1 - upper, upper)
    calls = [(stage, group) for stage in range(sections) for group in range(groups)]
    stages = np.array([stage for stage, _ in calls], np.int32)
    own = np.array([group for _, group in calls], np.int32)
    of = jnp.where(stages < half, relay[0], relay[1])
    active = (jnp.where(of == 0, last - position, position) == stages) & ~(
        (of == 1) & (position == last)
    )
    table = jnp.stack(
        [
            active.astype(jnp.int32),
            of,
            jnp.where(active & (of == 0), own, groups),
            (active & (stages < last)).astype(jnp.int32),
        ],
        axis=1,
    ).reshape(-1)
    kinds = [jnp.stack([relay[k]] * 4) for k in range(2)]
    home_kind = jnp.array([0, 0, 1, 0], jnp.int32)

    blocks = None
    saved = [None, None]
    order = []

    def run_forward(kind, after):
        nonlocal blocks, order
        *blocks, slopes, ys, rs, w_up, w_down = forward(
            per, section_inputs, up_weight, down_weight, kinds[kind], plan, blocks, after, 2, True
        )
        saved[kind] = (slopes, ys, rs, w_up, w_down)
        order = [blocks[0]]

    run_forward(0, [])
    received = {}
    arrived = {}
    kept = None
    for call, (stage, group) in enumerate(calls):
        if stage == last and group == 0:
            *home_blocks, slopes, ys, rs = forward(
                per, mirrored, up_weight, down_weight, home_kind, plan, None, order, 1, False
            )
            saved_home = (slopes, ys, rs)
            order = [home_blocks[0]]
        recv = received.pop((stage, group), None)
        asked = [arrived[(last - 1, 1)]] if (stage, group) == (half, 0) and groups > 1 else []
        out, *kept = chain_step(
            call, group, table, recv, top_grad, saved[int(stage >= half)], kept, order + asked
        )
        order = [kept[0]]
        pairs = [(last - stage, last - stage - 1)] if stage < last else []
        if stage < last - 1:
            pairs.append((stage, stage + 1))
        got = hop(out, pairs)
        if got is not None:
            received[(stage + 1, group)] = got
        if stage < last:
            to = last - 1 - stage
            arrived[(to, group)] = out if to == stage else hop(out, [(stage, to)])
        if saved[1] is None and group == groups - 1:
            run_forward(1, order + [mirrored[0, 0], arrived[(last - 1, 0)]])

    came = []
    for group in range(groups):
        value = arrived[(0, group)]
        for k in range(1, last):
            value = jnp.where(position == k, arrived[(k, group)], value)
        came.append(value)
    home_pre, home_sum = home_step(
        (position == last).astype(jnp.int32)[None], came, top_grad, saved_home, down_weight, order
    )

    replicas = lax.axis_size("dp")
    core = (lax.axis_index("dp") % 2).astype(jnp.int32)[None]
    swap = [(i, i ^ 1) for i in range(replicas)]
    along = [list(range(c, replicas, 2)) for c in range(2)]
    sources = (
        (blocks[1], kept[1], home_blocks[1], home_sum, groups, replicas, True),
        (blocks[0], kept[0], home_blocks[0], home_pre, groups, replicas, False),
    )
    came = [lax.ppermute(weight_gradient(1 - core, *x, None), "dp", swap) for x in sources]

    def summed(x, other):
        part = weight_gradient(core, *x, other)
        return lax.psum_scatter(
            part.reshape(-1, part.shape[-1]),
            "dp",
            scatter_dimension=0,
            axis_index_groups=along,
            tiled=True,
        )

    down_sum, up_sum = [summed(x, other) for x, other in zip(sources, came)]
    replica = lax.axis_index("dp").astype(jnp.int32)[None]

    def finish(weight, moment, total):
        fresh, fresh_moment = update(replica, weight, moment, total)
        far = lax.ppermute(fresh, "section", [(i, last - i) for i in range(sections)])
        return jnp.stack([fresh, far])[:, None], fresh_moment

    new_up_weight, new_up_moment = finish(up_weight, up_moment, up_sum)
    new_down_weight, new_down_moment = finish(down_weight, down_moment, down_sum)
    return (new_up_weight, new_down_weight, new_up_moment, new_down_moment)


def solution(mesh):
    in_specs = (
        P(None, "section", None, "dp", None),
        P(None, None, "dp", None),
        P(),
        P(None, "section", None, None),
        P(None, "section", None, None),
        P("section", "dp", None),
        P("section", "dp", None),
    )
    out_specs = (
        P(None, "section", "dp", None),
        P(None, "section", "dp", None),
        P("section", "dp", None),
        P("section", "dp", None),
    )
    return jax.shard_map(
        on_device, mesh=mesh, in_specs=in_specs, out_specs=out_specs, check_vma=False
    )
```

```python
import jax
import jax.numpy as jnp
import numpy as np
from jax import lax
from jax.experimental import pallas as pl
from jax.experimental.pallas import tpu as pltpu
from jax.sharding import PartitionSpec as P

norm_epsilon = 1e-06
momentum_decay = 0.9
step_size = 0.01
root_half = 0.7071067811865476
inv_root_tau = 0.3989422804014327

f32 = jnp.float32
bf16 = jnp.bfloat16
any_space = pl.BlockSpec(memory_space=pl.ANY)
light = pl.CostEstimate(flops=1000, bytes_accessed=1000, transcendentals=0)


def params(mib):
    return pltpu.CompilerParams(
        dimension_semantics=("arbitrary",), vmem_limit_bytes=mib * 1024 * 1024
    )


def in_vmem(x):
    return pltpu.with_memory_space_constraint(x, pltpu.VMEM)


def in_hbm(x):
    return pltpu.with_memory_space_constraint(x, pltpu.HBM)


def dot(left, right, over):
    return lax.dot_general(left, right, (over, ((), ())), preferred_element_type=f32)


def tile_of(width):
    return min(512, width)


def forward(per, inputs, w_up, w_down, info, plan, previous, after, places):
    _, _, micro, tokens, model = inputs.shape
    width = w_up.shape[3]
    tile = tile_of(width)
    groups, rows, every = micro // per, per * tokens, micro * tokens

    def body(info_ref, plan_ref, *refs):
        u_refs = refs[:micro]
        p_ref, q_ref = refs[micro : micro + 2]
        outs = refs[len(operands) :]
        us_ref, h_ref, slope_ref, y_ref, r_ref = outs[:5]
        rows_ref, total = outs[-2:]
        j = pl.program_id(0)

        @pl.when(j == 0)
        def _():
            for k in range(micro):
                u = u_refs[k][0, 0, 0]
                rows_ref[k * tokens : (k + 1) * tokens] = u
                us_ref[0, k // per, k % per * tokens : (k % per + 1) * tokens] = u

        for g in range(groups):
            here = slice(g * rows, (g + 1) * rows)
            u = rows_ref[here]
            pre = dot(u, p_ref[0, 0], ((1,), (0,)))
            cdf = 0.5 * (1.0 + lax.erf(pre * root_half))
            hidden = (pre * cdf).astype(bf16)
            slope = cdf + pre * (jnp.exp(-0.5 * pre * pre) * inv_root_tau)
            h_ref[0, g] = hidden
            slope_ref[g] = slope.astype(bf16)
            part = dot(hidden, q_ref[0, 0], ((1,), (0,)))
            base = jnp.where(j == 0, u.astype(f32), total[here])
            total[here] = base + part

        @pl.when(j == pl.num_programs(0) - 1)
        def _():
            for g in range(groups):
                z = total[g * rows : (g + 1) * rows]
                centre = z - jnp.mean(z, axis=-1, keepdims=True)
                r = lax.rsqrt(jnp.mean(centre * centre, axis=-1, keepdims=True) + norm_epsilon)
                y_ref[g] = (centre * r).astype(bf16)
                r_ref[g] = r

    def u_spec(k):
        return pl.BlockSpec(
            (1, 1, 1, tokens, model), lambda j, i, p: (i[0], 0, p[i[2], k], 0, 0)
        )

    in_specs = [u_spec(k) for k in range(micro)] + [
        pl.BlockSpec((1, 1, model, tile), lambda j, i, p: (i[1], 0, 0, j)),
        pl.BlockSpec((1, 1, tile, model), lambda j, i, p: (i[1], 0, j, 0)),
    ]
    operands = [in_hbm(inputs)] * micro + [in_hbm(w_up), in_hbm(w_down)]
    aliases = {}
    if previous is not None:
        aliases = {2 + len(operands) + k: k for k in range(2)}
        in_specs += [any_space] * 2
        operands += [in_hbm(x) for x in previous]
    for x in after:
        in_specs.append(any_space)
        operands.append(in_hbm(x) if x.ndim > 2 else x)
    out_shape = [
        pltpu.HBM((places, groups, rows, model), bf16),
        pltpu.HBM((places, groups, rows, width), bf16),
        pltpu.VMEM((groups, rows, width), bf16),
        pltpu.VMEM((groups, rows, model), bf16),
        pltpu.VMEM((groups, rows, 1), f32),
    ]
    out_specs = [
        pl.BlockSpec((1, groups, rows, model), lambda j, i, p: (i[3], 0, 0, 0)),
        pl.BlockSpec((1, groups, rows, tile), lambda j, i, p: (i[3], 0, 0, j)),
        pl.BlockSpec((groups, rows, tile), lambda j, i, p: (0, 0, j)),
        pl.BlockSpec((groups, rows, model), lambda j, i, p: (0, 0, 0)),
        pl.BlockSpec((groups, rows, 1), lambda j, i, p: (0, 0, 0)),
    ]
    return pl.pallas_call(
        body,
        grid_spec=pltpu.PrefetchScalarGridSpec(
            num_scalar_prefetch=2,
            grid=(width // tile,),
            in_specs=in_specs,
            out_specs=out_specs,
            scratch_shapes=[pltpu.VMEM((every, model), bf16), pltpu.VMEM((every, model), f32)],
        ),
        out_shape=out_shape,
        input_output_aliases=aliases,
        compiler_params=params(30),
        cost_estimate=light,
        name="forward",
    )(info, plan, *operands)


def sum_gradient(e, y, r):
    mean_e = jnp.mean(e, axis=-1, keepdims=True)
    mean_ey = jnp.mean(e * y, axis=-1, keepdims=True)
    return r * (e - mean_e - y * mean_ey)


columns_of_table = 4


def chain_step(call, group, table, recv, top_grad, saved, w_up, w_down, previous, after):
    base = call * columns_of_table
    slopes, ys, rs = saved
    groups, rows, model = ys.shape
    width = w_up.shape[3]
    tile = tile_of(width)
    tokens = top_grad.shape[2]
    per = rows // tokens

    def body(info, e_ref, y_ref, r_ref, slope_ref, p_ref, q_ref, *rest):
        out_ref, pre_ref, sum_ref, whole, low, total = rest[-6:]
        j = pl.program_id(0)
        active = info[base] > 0

        @pl.when(jnp.logical_and(active, j == 0))
        def _():
            e = e_ref[...].reshape(rows, model).astype(f32)
            grad = sum_gradient(e, y_ref[0].astype(f32), r_ref[0])
            whole[...] = grad
            low[...] = grad.astype(bf16)
            sum_ref[0] = grad.astype(bf16)

        @pl.when(active)
        def _():
            grad_pre = (
                dot(low[...], q_ref[0, 0], ((1,), (1,))) * slope_ref[0].astype(f32)
            ).astype(bf16)
            pre_ref[0] = grad_pre

            @pl.when(info[base + 3] > 0)
            def _():
                part = dot(grad_pre, p_ref[0, 0], ((1,), (1,)))

                @pl.when(j == 0)
                def _():
                    total[...] = whole[...] + part

                @pl.when(j > 0)
                def _():
                    total[...] += part

                @pl.when(j == pl.num_programs(0) - 1)
                def _():
                    out_ref[...] = total[...].astype(bf16)

    if recv is None:
        e_spec = pl.BlockSpec((1, per, tokens, model), lambda j, i: (i[base + 1], group, 0, 0))
        operands = [in_hbm(top_grad)]
    else:
        e_spec = pl.BlockSpec((rows, model), lambda j, i: (0, 0))
        operands = [recv]
    in_specs = [
        e_spec,
        pl.BlockSpec((1, rows, model), lambda j, i: (group, 0, 0)),
        pl.BlockSpec((1, rows, 1), lambda j, i: (group, 0, 0)),
        pl.BlockSpec((1, rows, tile), lambda j, i: (group, 0, j * i[base])),
        pl.BlockSpec((1, 1, model, tile), lambda j, i: (i[base + 1], 0, 0, j * i[base + 3])),
        pl.BlockSpec((1, 1, tile, model), lambda j, i: (i[base + 1], 0, j * i[base], 0)),
    ]
    operands += [in_vmem(x) for x in (ys, rs, slopes)] + [in_hbm(w_up), in_hbm(w_down)]
    aliases = {}
    if previous is not None:
        aliases = {1 + len(operands): 1, 2 + len(operands): 2}
        in_specs += [any_space] * 2
        operands += [in_hbm(x) for x in previous]
    for x in after:
        if previous is None or not any(x is y for y in previous):
            in_specs.append(any_space)
            operands.append(in_hbm(x) if x.ndim > 2 else x)
    return pl.pallas_call(
        body,
        grid_spec=pltpu.PrefetchScalarGridSpec(
            num_scalar_prefetch=1,
            grid=(width // tile,),
            in_specs=in_specs,
            out_specs=[
                pl.BlockSpec((rows, model), lambda j, i: (0, 0)),
                pl.BlockSpec((1, rows, tile), lambda j, i: (i[base + 2], 0, j * i[base])),
                pl.BlockSpec((1, rows, model), lambda j, i: (i[base + 2], 0, 0)),
            ],
            scratch_shapes=[
                pltpu.VMEM((rows, model), f32),
                pltpu.VMEM((rows, model), bf16),
                pltpu.VMEM((rows, model), f32),
            ],
        ),
        out_shape=[
            jax.ShapeDtypeStruct((rows, model), bf16),
            pltpu.HBM((groups + 1, rows, width), bf16),
            pltpu.HBM((groups + 1, rows, model), bf16),
        ],
        input_output_aliases=aliases,
        compiler_params=params(20),
        cost_estimate=light,
        name="chain",
    )(table, *operands)


def home_step(info, arrived, top_grad, saved, w_down, after):
    slopes, ys, rs = saved
    groups, rows, model = ys.shape
    micro, tokens = top_grad.shape[1:3]
    width = w_down.shape[2]
    tile = tile_of(width)

    def body(info, *refs):
        e_refs = refs[:groups]
        top_ref, y_ref, r_ref, slope_ref, q_ref = refs[groups : groups + 5]
        pre_ref, sum_ref = refs[-2:]

        @pl.when(pl.program_id(0) == 0)
        def _():
            for g in range(groups):
                top = top_ref[0].reshape(groups, rows, model)[g]
                e = jnp.where(info[0] > 0, top, e_refs[g][...]).astype(f32)
                grad = sum_gradient(e, y_ref[g].astype(f32), r_ref[g])
                sum_ref[g] = grad.astype(bf16)

        low = sum_ref[...].reshape(groups * rows, model)
        slope = slope_ref[...].reshape(groups * rows, tile)
        grad_pre = dot(low, q_ref[0, 0], ((1,), (1,))) * slope.astype(f32)
        pre_ref[...] = grad_pre.astype(bf16).reshape(pre_ref.shape)

    return pl.pallas_call(
        body,
        grid_spec=pltpu.PrefetchScalarGridSpec(
            num_scalar_prefetch=1,
            grid=(width // tile,),
            in_specs=[pl.BlockSpec((rows, model), lambda j, i: (0, 0))] * groups
            + [
                pl.BlockSpec((1, micro, tokens, model), lambda j, i: (1, 0, 0, 0)),
                pl.BlockSpec((groups, rows, model), lambda j, i: (0, 0, 0)),
                pl.BlockSpec((groups, rows, 1), lambda j, i: (0, 0, 0)),
                pl.BlockSpec((groups, rows, tile), lambda j, i: (0, 0, j)),
                pl.BlockSpec((1, 1, tile, model), lambda j, i: (0, 0, j, 0)),
            ]
            + [any_space] * len(after),
            out_specs=[
                pl.BlockSpec((groups, rows, tile), lambda j, i: (0, 0, j)),
                pl.BlockSpec((groups, rows, model), lambda j, i: (0, 0, 0)),
            ],
        ),
        out_shape=[
            pltpu.HBM((groups, rows, width), bf16),
            pltpu.HBM((groups, rows, model), bf16),
        ],
        compiler_params=params(28),
        cost_estimate=light,
        name="home",
    )(
        info,
        *arrived,
        in_hbm(top_grad),
        *[in_vmem(x) for x in (ys, rs, slopes)],
        in_hbm(w_down),
        *[in_hbm(x) if x.ndim > 2 else x for x in after],
    )


def weight_gradient(left_a, right_a, left_b, right_b, groups, split_left, after):
    tokens = right_a.shape[-2]
    rows, columns = left_a.shape[-1], right_a.shape[-1]
    tile = tile_of(rows if split_left else columns)

    def body(la_ref, ra_ref, lb_ref, rb_ref, *rest):
        def flat(ref):
            return ref[...].reshape(-1, ref.shape[-1])

        total = dot(flat(la_ref), flat(ra_ref), ((0,), (0,)))
        total += dot(flat(lb_ref), flat(rb_ref), ((0,), (0,)))
        rest[-1][...] = total.astype(bf16)

    def spec(array, split):
        lead = array.ndim - 3
        block = (1,) * lead + (groups, tokens, tile if split else array.shape[-1])
        if split:
            return pl.BlockSpec(block, lambda j: (0,) * (lead + 2) + (j,))
        return pl.BlockSpec(block, lambda j: (0,) * (lead + 3))

    out_block = (tile, columns) if split_left else (rows, tile)
    return pl.pallas_call(
        body,
        grid=((rows if split_left else columns) // tile,),
        in_specs=[
            spec(left_a, split_left),
            spec(right_a, not split_left),
            spec(left_b, split_left),
            spec(right_b, not split_left),
        ]
        + [any_space] * len(after),
        out_specs=pl.BlockSpec(out_block, (lambda j: (j, 0)) if split_left else (lambda j: (0, j))),
        out_shape=pltpu.HBM((rows, columns), bf16),
        compiler_params=params(32),
        cost_estimate=light,
        name="weights",
    )(*[in_hbm(x) for x in (left_a, right_a, left_b, right_b)], *[in_hbm(x) for x in after])


def update(replica, weight, moment, total):
    _, rows, columns = moment.shape
    tile = min(64, rows)
    steps = rows // tile

    def body(info, weight_ref, moment_ref, total_ref, fresh_ref, out_ref):
        fresh_moment = momentum_decay * moment_ref[0] + total_ref[...].astype(f32)
        out_ref[0] = fresh_moment
        fresh_ref[...] = (weight_ref[0, 0].astype(f32) - step_size * fresh_moment).astype(bf16)

    return pl.pallas_call(
        body,
        grid_spec=pltpu.PrefetchScalarGridSpec(
            num_scalar_prefetch=1,
            grid=(steps,),
            in_specs=[
                pl.BlockSpec((1, 1, tile, columns), lambda j, i: (0, 0, i[0] * steps + j, 0)),
                pl.BlockSpec((1, tile, columns), lambda j, i: (0, j, 0)),
                pl.BlockSpec((tile, columns), lambda j, i: (j, 0)),
            ],
            out_specs=[
                pl.BlockSpec((tile, columns), lambda j, i: (j, 0)),
                pl.BlockSpec((1, tile, columns), lambda j, i: (0, j, 0)),
            ],
        ),
        out_shape=[
            jax.ShapeDtypeStruct((rows, columns), bf16),
            pltpu.HBM((1, rows, columns), f32),
        ],
        compiler_params=params(24),
        cost_estimate=light,
        name="update",
    )(replica, in_hbm(weight), in_hbm(moment), total)


def on_device(section_inputs, top_grad, plan, up_weight, down_weight, up_moment, down_moment):
    sections = lax.axis_size("section")
    position = lax.axis_index("section").astype(jnp.int32)
    micro, tokens, model = top_grad.shape[1:]
    plan = plan.astype(jnp.int32)
    per = 2 if micro % 2 == 0 else 1
    groups, rows = micro // per, per * tokens
    last, half = sections - 1, sections // 2

    def hop(value, pairs):
        return lax.ppermute(value, "section", pairs) if pairs else None

    mirrored = lax.ppermute(
        section_inputs[1, 0], "section", [(i, last - i) for i in range(sections)]
    )[None, None]

    upper = (position >= half).astype(jnp.int32)
    relay = (1 - upper, upper)
    calls = [(stage, group) for stage in range(sections) for group in range(groups)]
    stages = np.array([stage for stage, _ in calls], np.int32)
    own = np.array([group for _, group in calls], np.int32)
    of = jnp.where(stages < half, relay[0], relay[1])
    active = (jnp.where(of == 0, last - position, position) == stages) & ~(
        (of == 1) & (position == last)
    )
    table = jnp.stack(
        [
            active.astype(jnp.int32),
            of,
            jnp.where(active & (of == 0), own, groups),
            (active & (stages < last)).astype(jnp.int32),
        ],
        axis=1,
    ).reshape(-1)
    kinds = [jnp.stack([relay[k]] * 4) for k in range(2)]
    home_kind = jnp.array([0, 0, 1, 0], jnp.int32)

    blocks = None
    saved = [None, None]
    order = []

    def run_forward(kind, after):
        nonlocal blocks, order
        *blocks, slopes, ys, rs = forward(
            per, section_inputs, up_weight, down_weight, kinds[kind], plan, blocks, after, 2
        )
        saved[kind] = (slopes, ys, rs)
        order = [blocks[0]]

    run_forward(0, [])
    received = {}
    arrived = {}
    asked = {(1, 0): [(last - 1, 0)], (half, 0): [(last - 1, g) for g in range(1, groups)]}
    kept = None
    for call, (stage, group) in enumerate(calls):
        if stage == last and group == 0:
            *home_blocks, slopes, ys, rs = forward(
                per, mirrored, up_weight, down_weight, home_kind, plan, None, order, 1
            )
            saved_home = (slopes, ys, rs)
            order = [home_blocks[0]]
        recv = received.pop((stage, group), None)
        out, *kept = chain_step(
            call,
            group,
            table,
            recv,
            top_grad,
            saved[int(stage >= half)],
            up_weight,
            down_weight,
            kept,
            order + [arrived[x] for x in asked.get((stage, group), [])],
        )
        order = [kept[0]]
        pairs = [(last - stage, last - stage - 1)] if stage < last else []
        if stage < last - 1:
            pairs.append((stage, stage + 1))
        got = hop(out, pairs)
        if got is not None:
            received[(stage + 1, group)] = got
        if stage < last:
            to = last - 1 - stage
            arrived[(to, group)] = out if to == stage else hop(out, [(stage, to)])
        if saved[1] is None and group == groups - 1:
            run_forward(1, order + [mirrored[0, 0]])

    came = []
    for group in range(groups):
        value = arrived[(0, group)]
        for k in range(1, last):
            value = jnp.where(position == k, arrived[(k, group)], value)
        came.append(value)
    home_pre, home_sum = home_step(
        (position == last).astype(jnp.int32)[None], came, top_grad, saved_home, down_weight, order
    )

    up_part = weight_gradient(blocks[0], kept[0], home_blocks[0], home_pre, groups, False, [])
    up_sum = lax.psum_scatter(up_part, "dp", scatter_dimension=0, tiled=True)
    down_part = weight_gradient(blocks[1], kept[1], home_blocks[1], home_sum, groups, True, [])
    down_sum = lax.psum_scatter(down_part, "dp", scatter_dimension=0, tiled=True)
    replica = lax.axis_index("dp").astype(jnp.int32)[None]

    def finish(weight, moment, total):
        fresh, fresh_moment = update(replica, weight, moment, total)
        far = lax.ppermute(fresh, "section", [(i, last - i) for i in range(sections)])
        return jnp.stack([fresh, far])[:, None], fresh_moment

    new_up_weight, new_up_moment = finish(up_weight, up_moment, up_sum)
    new_down_weight, new_down_moment = finish(down_weight, down_moment, down_sum)
    return (new_up_weight, new_down_weight, new_up_moment, new_down_moment)


def solution(mesh):
    in_specs = (
        P(None, "section", None, "dp", None),
        P(None, None, "dp", None),
        P(),
        P(None, "section", None, None),
        P(None, "section", None, None),
        P("section", "dp", None),
        P("section", "dp", None),
    )
    out_specs = (
        P(None, "section", "dp", None),
        P(None, "section", "dp", None),
        P("section", "dp", None),
        P("section", "dp", None),
    )
    return jax.shard_map(
        on_device, mesh=mesh, in_specs=in_specs, out_specs=out_specs, check_vma=False
    )
```

```python
import jax
import jax.numpy as jnp
import numpy as np
from jax import lax
from jax.experimental import pallas as pl
from jax.experimental.pallas import tpu as pltpu
from jax.sharding import PartitionSpec as P

norm_epsilon = 1e-06
momentum_decay = 0.9
step_size = 0.01
root_half = 0.7071067811865476
inv_root_tau = 0.3989422804014327

f32 = jnp.float32
bf16 = jnp.bfloat16
any_space = pl.BlockSpec(memory_space=pl.ANY)
light = pl.CostEstimate(flops=1000, bytes_accessed=1000, transcendentals=0)


def params(mib):
    return pltpu.CompilerParams(
        dimension_semantics=("arbitrary",), vmem_limit_bytes=mib * 1024 * 1024
    )


def in_vmem(x):
    return pltpu.with_memory_space_constraint(x, pltpu.VMEM)


def in_hbm(x):
    return pltpu.with_memory_space_constraint(x, pltpu.HBM)


def dot(left, right, over):
    return lax.dot_general(left, right, (over, ((), ())), preferred_element_type=f32)


def tile_of(width):
    return min(512, width)


def forward(per, inputs, w_up, w_down, info, plan, previous, after, places):
    _, _, micro, tokens, model = inputs.shape
    width = w_up.shape[3]
    tile = tile_of(width)
    groups, rows, every = micro // per, per * tokens, micro * tokens

    def body(info_ref, plan_ref, *refs):
        u_refs = refs[:micro]
        p_ref, q_ref = refs[micro : micro + 2]
        outs = refs[len(operands) :]
        us_ref, h_ref, slope_ref, y_ref, r_ref = outs[:5]
        rows_ref, total = outs[-2:]
        j = pl.program_id(0)

        @pl.when(j == 0)
        def _():
            for k in range(micro):
                u = u_refs[k][0, 0, 0]
                rows_ref[k * tokens : (k + 1) * tokens] = u
                us_ref[0, k // per, k % per * tokens : (k % per + 1) * tokens] = u

        for g in range(groups):
            here = slice(g * rows, (g + 1) * rows)
            u = rows_ref[here]
            pre = dot(u, p_ref[0, 0], ((1,), (0,)))
            cdf = 0.5 * (1.0 + lax.erf(pre * root_half))
            hidden = (pre * cdf).astype(bf16)
            slope = cdf + pre * (jnp.exp(-0.5 * pre * pre) * inv_root_tau)
            h_ref[0, g] = hidden
            slope_ref[g] = slope.astype(bf16)
            part = dot(hidden, q_ref[0, 0], ((1,), (0,)))
            base = jnp.where(j == 0, u.astype(f32), total[here])
            total[here] = base + part

        @pl.when(j == pl.num_programs(0) - 1)
        def _():
            for g in range(groups):
                z = total[g * rows : (g + 1) * rows]
                centre = z - jnp.mean(z, axis=-1, keepdims=True)
                r = lax.rsqrt(jnp.mean(centre * centre, axis=-1, keepdims=True) + norm_epsilon)
                y_ref[g] = (centre * r).astype(bf16)
                r_ref[g] = r

    def u_spec(k):
        return pl.BlockSpec(
            (1, 1, 1, tokens, model), lambda j, i, p: (i[0], 0, p[i[2], k], 0, 0)
        )

    in_specs = [u_spec(k) for k in range(micro)] + [
        pl.BlockSpec((1, 1, model, tile), lambda j, i, p: (i[1], 0, 0, j)),
        pl.BlockSpec((1, 1, tile, model), lambda j, i, p: (i[1], 0, j, 0)),
    ]
    operands = [in_hbm(inputs)] * micro + [in_hbm(w_up), in_hbm(w_down)]
    aliases = {}
    if previous is not None:
        aliases = {2 + len(operands) + k: k for k in range(2)}
        in_specs += [any_space] * 2
        operands += [in_hbm(x) for x in previous]
    for x in after:
        in_specs.append(any_space)
        operands.append(in_hbm(x) if x.ndim > 2 else x)
    out_shape = [
        pltpu.HBM((places, groups, rows, model), bf16),
        pltpu.HBM((places, groups, rows, width), bf16),
        pltpu.VMEM((groups, rows, width), bf16),
        pltpu.VMEM((groups, rows, model), bf16),
        pltpu.VMEM((groups, rows, 1), f32),
    ]
    out_specs = [
        pl.BlockSpec((1, groups, rows, model), lambda j, i, p: (i[3], 0, 0, 0)),
        pl.BlockSpec((1, groups, rows, tile), lambda j, i, p: (i[3], 0, 0, j)),
        pl.BlockSpec((groups, rows, tile), lambda j, i, p: (0, 0, j)),
        pl.BlockSpec((groups, rows, model), lambda j, i, p: (0, 0, 0)),
        pl.BlockSpec((groups, rows, 1), lambda j, i, p: (0, 0, 0)),
    ]
    return pl.pallas_call(
        body,
        grid_spec=pltpu.PrefetchScalarGridSpec(
            num_scalar_prefetch=2,
            grid=(width // tile,),
            in_specs=in_specs,
            out_specs=out_specs,
            scratch_shapes=[pltpu.VMEM((every, model), bf16), pltpu.VMEM((every, model), f32)],
        ),
        out_shape=out_shape,
        input_output_aliases=aliases,
        compiler_params=params(30),
        cost_estimate=light,
        name="forward",
    )(info, plan, *operands)


def sum_gradient(e, y, r):
    mean_e = jnp.mean(e, axis=-1, keepdims=True)
    mean_ey = jnp.mean(e * y, axis=-1, keepdims=True)
    return r * (e - mean_e - y * mean_ey)


columns_of_table = 4


def chain_step(call, group, table, recv, top_grad, saved, w_up, w_down, previous, after):
    base = call * columns_of_table
    slopes, ys, rs = saved
    groups, rows, model = ys.shape
    width = w_up.shape[3]
    tile = tile_of(width)
    tokens = top_grad.shape[2]
    per = rows // tokens

    def body(info, e_ref, y_ref, r_ref, slope_ref, p_ref, q_ref, *rest):
        out_ref, pre_ref, sum_ref, whole, low, total = rest[-6:]
        j = pl.program_id(0)
        active = info[base] > 0

        @pl.when(jnp.logical_and(active, j == 0))
        def _():
            e = e_ref[...].reshape(rows, model).astype(f32)
            grad = sum_gradient(e, y_ref[0].astype(f32), r_ref[0])
            whole[...] = grad
            low[...] = grad.astype(bf16)
            sum_ref[0] = grad.astype(bf16)

        @pl.when(active)
        def _():
            grad_pre = (
                dot(low[...], q_ref[0, 0], ((1,), (1,))) * slope_ref[0].astype(f32)
            ).astype(bf16)
            pre_ref[0] = grad_pre

            @pl.when(info[base + 3] > 0)
            def _():
                part = dot(grad_pre, p_ref[0, 0], ((1,), (1,)))

                @pl.when(j == 0)
                def _():
                    total[...] = whole[...] + part

                @pl.when(j > 0)
                def _():
                    total[...] += part

                @pl.when(j == pl.num_programs(0) - 1)
                def _():
                    out_ref[...] = total[...].astype(bf16)

    if recv is None:
        e_spec = pl.BlockSpec((1, per, tokens, model), lambda j, i: (i[base + 1], group, 0, 0))
        operands = [in_hbm(top_grad)]
    else:
        e_spec = pl.BlockSpec((rows, model), lambda j, i: (0, 0))
        operands = [recv]
    in_specs = [
        e_spec,
        pl.BlockSpec((1, rows, model), lambda j, i: (group, 0, 0)),
        pl.BlockSpec((1, rows, 1), lambda j, i: (group, 0, 0)),
        pl.BlockSpec((1, rows, tile), lambda j, i: (group, 0, j * i[base])),
        pl.BlockSpec((1, 1, model, tile), lambda j, i: (i[base + 1], 0, 0, j * i[base + 3])),
        pl.BlockSpec((1, 1, tile, model), lambda j, i: (i[base + 1], 0, j * i[base], 0)),
    ]
    operands += [in_vmem(x) for x in (ys, rs, slopes)] + [in_hbm(w_up), in_hbm(w_down)]
    aliases = {}
    if previous is not None:
        aliases = {1 + len(operands): 1, 2 + len(operands): 2}
        in_specs += [any_space] * 2
        operands += [in_hbm(x) for x in previous]
    for x in after:
        if previous is None or not any(x is y for y in previous):
            in_specs.append(any_space)
            operands.append(in_hbm(x) if x.ndim > 2 else x)
    return pl.pallas_call(
        body,
        grid_spec=pltpu.PrefetchScalarGridSpec(
            num_scalar_prefetch=1,
            grid=(width // tile,),
            in_specs=in_specs,
            out_specs=[
                pl.BlockSpec((rows, model), lambda j, i: (0, 0)),
                pl.BlockSpec((1, rows, tile), lambda j, i: (i[base + 2], 0, j * i[base])),
                pl.BlockSpec((1, rows, model), lambda j, i: (i[base + 2], 0, 0)),
            ],
            scratch_shapes=[
                pltpu.VMEM((rows, model), f32),
                pltpu.VMEM((rows, model), bf16),
                pltpu.VMEM((rows, model), f32),
            ],
        ),
        out_shape=[
            jax.ShapeDtypeStruct((rows, model), bf16),
            pltpu.HBM((groups + 1, rows, width), bf16),
            pltpu.HBM((groups + 1, rows, model), bf16),
        ],
        input_output_aliases=aliases,
        compiler_params=params(20),
        cost_estimate=light,
        name="chain",
    )(table, *operands)


def home_step(info, arrived, top_grad, saved, w_down, after):
    slopes, ys, rs = saved
    groups, rows, model = ys.shape
    micro, tokens = top_grad.shape[1:3]
    width = w_down.shape[2]
    tile = tile_of(width)

    def body(info, *refs):
        e_refs = refs[:groups]
        top_ref, y_ref, r_ref, slope_ref, q_ref = refs[groups : groups + 5]
        pre_ref, sum_ref = refs[-2:]

        @pl.when(pl.program_id(0) == 0)
        def _():
            for g in range(groups):
                top = top_ref[0].reshape(groups, rows, model)[g]
                e = jnp.where(info[0] > 0, top, e_refs[g][...]).astype(f32)
                grad = sum_gradient(e, y_ref[g].astype(f32), r_ref[g])
                sum_ref[g] = grad.astype(bf16)

        low = sum_ref[...].reshape(groups * rows, model)
        slope = slope_ref[...].reshape(groups * rows, tile)
        grad_pre = dot(low, q_ref[0, 0], ((1,), (1,))) * slope.astype(f32)
        pre_ref[...] = grad_pre.astype(bf16).reshape(pre_ref.shape)

    return pl.pallas_call(
        body,
        grid_spec=pltpu.PrefetchScalarGridSpec(
            num_scalar_prefetch=1,
            grid=(width // tile,),
            in_specs=[pl.BlockSpec((rows, model), lambda j, i: (0, 0))] * groups
            + [
                pl.BlockSpec((1, micro, tokens, model), lambda j, i: (1, 0, 0, 0)),
                pl.BlockSpec((groups, rows, model), lambda j, i: (0, 0, 0)),
                pl.BlockSpec((groups, rows, 1), lambda j, i: (0, 0, 0)),
                pl.BlockSpec((groups, rows, tile), lambda j, i: (0, 0, j)),
                pl.BlockSpec((1, 1, tile, model), lambda j, i: (0, 0, j, 0)),
            ]
            + [any_space] * len(after),
            out_specs=[
                pl.BlockSpec((groups, rows, tile), lambda j, i: (0, 0, j)),
                pl.BlockSpec((groups, rows, model), lambda j, i: (0, 0, 0)),
            ],
        ),
        out_shape=[
            pltpu.HBM((groups, rows, width), bf16),
            pltpu.HBM((groups, rows, model), bf16),
        ],
        compiler_params=params(28),
        cost_estimate=light,
        name="home",
    )(
        info,
        *arrived,
        in_hbm(top_grad),
        *[in_vmem(x) for x in (ys, rs, slopes)],
        in_hbm(w_down),
        *[in_hbm(x) if x.ndim > 2 else x for x in after],
    )


def weight_gradient(core, left_a, right_a, left_b, right_b, groups, replicas, split_left, came, after):
    tokens = right_a.shape[-2]
    rows, columns = left_a.shape[-1] // replicas, right_a.shape[-1]
    lines = replicas // 2
    tile = columns if split_left else tile_of(columns)
    steps = lines if split_left else columns // tile
    lefts = 1 if split_left else lines
    pair = rows % 128 != 0
    wide = 2 * rows if pair else rows

    def place(z, i):
        return z if pair else 2 * z + i[0]

    def body(info, *refs):
        def flat(ref):
            return ref[...].reshape(-1, ref.shape[-1])

        def product(left_refs, right_ref):
            left = [flat(ref) for ref in left_refs]
            if pair:
                left = [jnp.where(info[0] == 0, x[:, :rows], x[:, rows:]) for x in left]
            left = left[0] if len(left) == 1 else jnp.concatenate(left, axis=1)
            return dot(left, flat(right_ref), ((0,), (0,)))

        total = product(refs[:lefts], refs[lefts])
        total += product(refs[lefts + 1 : 2 * lefts + 1], refs[2 * lefts + 1])
        total = total.reshape(lefts, rows, tile)
        if came is not None:
            total += refs[2 * lefts + 2][...].astype(f32)
        refs[-1][...] = total.astype(bf16)

    def left_specs(array):
        lead = array.ndim - 3
        block = (1,) * lead + (groups, tokens, wide)
        if split_left:
            return [pl.BlockSpec(block, lambda j, i: (0,) * (lead + 2) + (place(j, i),))]
        return [
            pl.BlockSpec(block, lambda j, i, z=z: (0,) * (lead + 2) + (place(z, i),))
            for z in range(lines)
        ]

    def right_spec(array):
        lead = array.ndim - 3
        block = (1,) * lead + (groups, tokens, tile)
        if split_left:
            return pl.BlockSpec(block, lambda j, i: (0,) * (lead + 3))
        return pl.BlockSpec(block, lambda j, i: (0,) * (lead + 2) + (j,))

    if split_left:
        out_spec = pl.BlockSpec((1, rows, tile), lambda j, i: (j, 0, 0))
    else:
        out_spec = pl.BlockSpec((lines, rows, tile), lambda j, i: (0, 0, j))
    operands = [in_hbm(left_a)] * lefts + [in_hbm(right_a)]
    operands += [in_hbm(left_b)] * lefts + [in_hbm(right_b)]
    in_specs = left_specs(left_a) + [right_spec(right_a)]
    in_specs += left_specs(left_b) + [right_spec(right_b)]
    if came is not None:
        operands.append(came)
        in_specs.append(out_spec)
    in_specs += [any_space] * len(after)
    operands += [in_hbm(x) for x in after]
    return pl.pallas_call(
        body,
        grid_spec=pltpu.PrefetchScalarGridSpec(
            num_scalar_prefetch=1, grid=(steps,), in_specs=in_specs, out_specs=out_spec
        ),
        out_shape=pltpu.HBM((lines, rows, columns), bf16),
        compiler_params=params(28),
        cost_estimate=light,
        name="weights",
    )(core, *operands)


def fold(places, part, came):
    _, rows, columns = part.shape
    tile = min(64, rows)

    def body(info, *refs):
        for k in range(2):
            value = refs[k][0].astype(f32)
            if came:
                value += refs[2 + k][...].astype(f32)
            refs[k - 2][...] = value.astype(bf16)

    plain = pl.BlockSpec((tile, columns), lambda j, i: (j, 0))
    return pl.pallas_call(
        body,
        grid_spec=pltpu.PrefetchScalarGridSpec(
            num_scalar_prefetch=1,
            grid=(rows // tile,),
            in_specs=[
                pl.BlockSpec((1, tile, columns), lambda j, i: (i[0], j, 0)),
                pl.BlockSpec((1, tile, columns), lambda j, i: (i[1], j, 0)),
            ]
            + [plain] * len(came),
            out_specs=[plain] * 2,
        ),
        out_shape=[jax.ShapeDtypeStruct((rows, columns), bf16)] * 2,
        compiler_params=params(16),
        cost_estimate=light,
        name="fold",
    )(places, in_hbm(part), in_hbm(part), *came)


def update(replica, weight, moment, part, came):
    _, rows, columns = moment.shape
    tile = min(64, rows)
    steps = rows // tile

    def body(info, weight_ref, moment_ref, part_ref, right_ref, left_ref, fresh_ref, out_ref):
        total = part_ref[0].astype(f32) + right_ref[...].astype(f32) + left_ref[...].astype(f32)
        fresh_moment = momentum_decay * moment_ref[0] + total
        out_ref[0] = fresh_moment
        fresh_ref[...] = (weight_ref[0, 0].astype(f32) - step_size * fresh_moment).astype(bf16)

    return pl.pallas_call(
        body,
        grid_spec=pltpu.PrefetchScalarGridSpec(
            num_scalar_prefetch=1,
            grid=(steps,),
            in_specs=[
                pl.BlockSpec((1, 1, tile, columns), lambda j, i: (0, 0, i[0] * steps + j, 0)),
                pl.BlockSpec((1, tile, columns), lambda j, i: (0, j, 0)),
                pl.BlockSpec((1, tile, columns), lambda j, i: (i[1], j, 0)),
                pl.BlockSpec((tile, columns), lambda j, i: (j, 0)),
                pl.BlockSpec((tile, columns), lambda j, i: (j, 0)),
            ],
            out_specs=[
                pl.BlockSpec((tile, columns), lambda j, i: (j, 0)),
                pl.BlockSpec((1, tile, columns), lambda j, i: (0, j, 0)),
            ],
        ),
        out_shape=[
            jax.ShapeDtypeStruct((rows, columns), bf16),
            pltpu.HBM((1, rows, columns), f32),
        ],
        compiler_params=params(24),
        cost_estimate=light,
        name="update",
    )(replica, in_hbm(weight), in_hbm(moment), in_hbm(part), *came)


def on_device(section_inputs, top_grad, plan, up_weight, down_weight, up_moment, down_moment):
    sections = lax.axis_size("section")
    position = lax.axis_index("section").astype(jnp.int32)
    micro, tokens, model = top_grad.shape[1:]
    plan = plan.astype(jnp.int32)
    per = 2 if micro % 2 == 0 else 1
    groups, rows = micro // per, per * tokens
    last, half = sections - 1, sections // 2

    def hop(value, pairs):
        return lax.ppermute(value, "section", pairs) if pairs else None

    mirrored = lax.ppermute(
        section_inputs[1, 0], "section", [(i, last - i) for i in range(sections)]
    )[None, None]

    upper = (position >= half).astype(jnp.int32)
    relay = (1 - upper, upper)
    calls = [(stage, group) for stage in range(sections) for group in range(groups)]
    stages = np.array([stage for stage, _ in calls], np.int32)
    own = np.array([group for _, group in calls], np.int32)
    of = jnp.where(stages < half, relay[0], relay[1])
    active = (jnp.where(of == 0, last - position, position) == stages) & ~(
        (of == 1) & (position == last)
    )
    table = jnp.stack(
        [
            active.astype(jnp.int32),
            of,
            jnp.where(active & (of == 0), own, groups),
            (active & (stages < last)).astype(jnp.int32),
        ],
        axis=1,
    ).reshape(-1)
    kinds = [jnp.stack([relay[k]] * 4) for k in range(2)]
    home_kind = jnp.array([0, 0, 1, 0], jnp.int32)

    blocks = None
    saved = [None, None]
    order = []

    def run_forward(kind, after):
        nonlocal blocks, order
        *blocks, slopes, ys, rs = forward(
            per, section_inputs, up_weight, down_weight, kinds[kind], plan, blocks, after, 2
        )
        saved[kind] = (slopes, ys, rs)
        order = [blocks[0]]

    run_forward(0, [])
    received = {}
    arrived = {}
    asked = {(1, 0): [(last - 1, 0)], (half, 0): [(last - 1, g) for g in range(1, groups)]}
    kept = None
    for call, (stage, group) in enumerate(calls):
        if stage == last and group == 0:
            *home_blocks, slopes, ys, rs = forward(
                per, mirrored, up_weight, down_weight, home_kind, plan, None, order, 1
            )
            saved_home = (slopes, ys, rs)
            order = [home_blocks[0]]
        recv = received.pop((stage, group), None)
        out, *kept = chain_step(
            call,
            group,
            table,
            recv,
            top_grad,
            saved[int(stage >= half)],
            up_weight,
            down_weight,
            kept,
            order + [arrived[x] for x in asked.get((stage, group), [])],
        )
        order = [kept[0]]
        pairs = [(last - stage, last - stage - 1)] if stage < last else []
        if stage < last - 1:
            pairs.append((stage, stage + 1))
        got = hop(out, pairs)
        if got is not None:
            received[(stage + 1, group)] = got
        if stage < last:
            to = last - 1 - stage
            arrived[(to, group)] = out if to == stage else hop(out, [(stage, to)])
        if saved[1] is None and group == groups - 1:
            run_forward(1, order + [mirrored[0, 0]])

    side = sorted(arrived)
    *values, kept[1] = lax.optimization_barrier([arrived[x] for x in side] + [kept[1]])
    arrived = dict(zip(side, values))
    came = []
    for group in range(groups):
        value = arrived[(0, group)]
        for k in range(1, last):
            value = jnp.where(position == k, arrived[(k, group)], value)
        came.append(value)
    home_pre, home_sum = home_step(
        (position == last).astype(jnp.int32)[None], came, top_grad, saved_home, down_weight, order
    )

    replicas = lax.axis_size("dp")
    replica = lax.axis_index("dp").astype(jnp.int32)
    lines, place, core = replicas // 2, replica // 2, replica % 2
    swap = [(i, i ^ 1) for i in range(replicas)]
    sources = (
        (blocks[1], kept[1], home_blocks[1], home_sum, groups, replicas, True),
        (blocks[0], kept[0], home_blocks[0], home_pre, groups, replicas, False),
    )
    other = (1 - core)[None]
    sent_down = weight_gradient(other, *sources[0], None, [])
    came_down = lax.ppermute(sent_down, "dp", swap)
    sent_up = weight_gradient(other, *sources[1], None, [sent_down])
    came_up = lax.ppermute(sent_up, "dp", swap)
    parts = [weight_gradient(core[None], *sources[0], came_down, [sent_up])]
    parts.append(weight_gradient(core[None], *sources[1], came_up, [parts[0]]))

    came = [[], []]
    for step in range(1, lines):
        places = jnp.stack(
            [jnp.minimum(place + lines - step, lines - 1), jnp.maximum(place - lines + step, 0)]
        )
        starts = [z for z in range(step) if z + 1 < lines]
        right = [(2 * z + c, 2 * z + 2 + c) for z in starts for c in range(2)]
        left = [(replicas - 1 - i, replicas - 1 - k) for i, k in right]
        for k in range(2):
            to_right, to_left = fold(places, parts[k], came[k])
            came[k] = [lax.ppermute(to_right, "dp", right), lax.ppermute(to_left, "dp", left)]

    where = jnp.stack([replica, place])

    def finish(weight, moment, part, arrivals):
        fresh, fresh_moment = update(where, weight, moment, part, arrivals)
        far = lax.ppermute(fresh, "section", [(i, last - i) for i in range(sections)])
        return jnp.stack([fresh, far])[:, None], fresh_moment

    new_down_weight, new_down_moment = finish(down_weight, down_moment, parts[0], came[0])
    new_up_weight, new_up_moment = finish(up_weight, up_moment, parts[1], came[1])
    return (new_up_weight, new_down_weight, new_up_moment, new_down_moment)


def solution(mesh):
    in_specs = (
        P(None, "section", None, "dp", None),
        P(None, None, "dp", None),
        P(),
        P(None, "section", None, None),
        P(None, "section", None, None),
        P("section", "dp", None),
        P("section", "dp", None),
    )
    out_specs = (
        P(None, "section", "dp", None),
        P(None, "section", "dp", None),
        P("section", "dp", None),
        P("section", "dp", None),
    )
    return jax.shard_map(
        on_device, mesh=mesh, in_specs=in_specs, out_specs=out_specs, check_vma=False
    )
```

```python
import jax
import jax.numpy as jnp
import numpy as np
from jax import lax
from jax.experimental import pallas as pl
from jax.experimental.pallas import tpu as pltpu
from jax.sharding import PartitionSpec as P

norm_epsilon = 1e-06
momentum_decay = 0.9
step_size = 0.01
root_half = 0.7071067811865476
inv_root_tau = 0.3989422804014327

f32 = jnp.float32
bf16 = jnp.bfloat16
any_space = pl.BlockSpec(memory_space=pl.ANY)
light = pl.CostEstimate(flops=1000, bytes_accessed=1000, transcendentals=0)


def params(mib):
    return pltpu.CompilerParams(
        dimension_semantics=("arbitrary",), vmem_limit_bytes=mib * 1024 * 1024
    )


def in_vmem(x):
    return pltpu.with_memory_space_constraint(x, pltpu.VMEM)


def in_hbm(x):
    return pltpu.with_memory_space_constraint(x, pltpu.HBM)


def dot(left, right, over):
    return lax.dot_general(left, right, (over, ((), ())), preferred_element_type=f32)


def tile_of(width):
    return min(512, width)


def forward(per, inputs, w_up, w_down, info, plan, previous, after, places):
    _, _, micro, tokens, model = inputs.shape
    width = w_up.shape[3]
    tile = tile_of(width)
    groups, rows, every = micro // per, per * tokens, micro * tokens

    def body(info_ref, plan_ref, *refs):
        u_refs = refs[:micro]
        p_ref, q_ref = refs[micro : micro + 2]
        outs = refs[len(operands) :]
        us_ref, h_ref, slope_ref, y_ref, r_ref = outs[:5]
        rows_ref, total = outs[-2:]
        j = pl.program_id(0)

        @pl.when(j == 0)
        def _():
            for k in range(micro):
                u = u_refs[k][0, 0, 0]
                rows_ref[k * tokens : (k + 1) * tokens] = u
                us_ref[0, k // per, k % per * tokens : (k % per + 1) * tokens] = u

        for g in range(groups):
            here = slice(g * rows, (g + 1) * rows)
            u = rows_ref[here]
            pre = dot(u, p_ref[0, 0], ((1,), (0,)))
            cdf = 0.5 * (1.0 + lax.erf(pre * root_half))
            hidden = (pre * cdf).astype(bf16)
            slope = cdf + pre * (jnp.exp(-0.5 * pre * pre) * inv_root_tau)
            h_ref[0, g] = hidden
            slope_ref[g] = slope.astype(bf16)
            part = dot(hidden, q_ref[0, 0], ((1,), (0,)))
            base = jnp.where(j == 0, u.astype(f32), total[here])
            total[here] = base + part

        @pl.when(j == pl.num_programs(0) - 1)
        def _():
            for g in range(groups):
                z = total[g * rows : (g + 1) * rows]
                centre = z - jnp.mean(z, axis=-1, keepdims=True)
                r = lax.rsqrt(jnp.mean(centre * centre, axis=-1, keepdims=True) + norm_epsilon)
                y_ref[g] = (centre * r).astype(bf16)
                r_ref[g] = r

    def u_spec(k):
        return pl.BlockSpec(
            (1, 1, 1, tokens, model), lambda j, i, p: (i[0], 0, p[i[2], k], 0, 0)
        )

    in_specs = [u_spec(k) for k in range(micro)] + [
        pl.BlockSpec((1, 1, model, tile), lambda j, i, p: (i[1], 0, 0, j)),
        pl.BlockSpec((1, 1, tile, model), lambda j, i, p: (i[1], 0, j, 0)),
    ]
    operands = [in_hbm(inputs)] * micro + [in_hbm(w_up), in_hbm(w_down)]
    aliases = {}
    if previous is not None:
        aliases = {2 + len(operands) + k: k for k in range(2)}
        in_specs += [any_space] * 2
        operands += [in_hbm(x) for x in previous]
    for x in after:
        in_specs.append(any_space)
        operands.append(in_hbm(x) if x.ndim > 2 else x)
    out_shape = [
        pltpu.HBM((places, groups, rows, model), bf16),
        pltpu.HBM((places, groups, rows, width), bf16),
        pltpu.VMEM((groups, rows, width), bf16),
        pltpu.VMEM((groups, rows, model), bf16),
        pltpu.VMEM((groups, rows, 1), f32),
    ]
    out_specs = [
        pl.BlockSpec((1, groups, rows, model), lambda j, i, p: (i[3], 0, 0, 0)),
        pl.BlockSpec((1, groups, rows, tile), lambda j, i, p: (i[3], 0, 0, j)),
        pl.BlockSpec((groups, rows, tile), lambda j, i, p: (0, 0, j)),
        pl.BlockSpec((groups, rows, model), lambda j, i, p: (0, 0, 0)),
        pl.BlockSpec((groups, rows, 1), lambda j, i, p: (0, 0, 0)),
    ]
    return pl.pallas_call(
        body,
        grid_spec=pltpu.PrefetchScalarGridSpec(
            num_scalar_prefetch=2,
            grid=(width // tile,),
            in_specs=in_specs,
            out_specs=out_specs,
            scratch_shapes=[pltpu.VMEM((every, model), bf16), pltpu.VMEM((every, model), f32)],
        ),
        out_shape=out_shape,
        input_output_aliases=aliases,
        compiler_params=params(30),
        cost_estimate=light,
        name="forward",
    )(info, plan, *operands)


def sum_gradient(e, y, r):
    mean_e = jnp.mean(e, axis=-1, keepdims=True)
    mean_ey = jnp.mean(e * y, axis=-1, keepdims=True)
    return r * (e - mean_e - y * mean_ey)


columns_of_table = 4


def chain_step(call, group, table, recv, top_grad, saved, w_up, w_down, previous, after):
    base = call * columns_of_table
    slopes, ys, rs = saved
    groups, rows, model = ys.shape
    width = w_up.shape[3]
    tile = tile_of(width)
    tokens = top_grad.shape[2]
    per = rows // tokens

    def body(info, e_ref, y_ref, r_ref, slope_ref, p_ref, q_ref, *rest):
        out_ref, pre_ref, sum_ref, whole, low, total = rest[-6:]
        j = pl.program_id(0)
        active = info[base] > 0

        @pl.when(jnp.logical_and(active, j == 0))
        def _():
            e = e_ref[...].reshape(rows, model).astype(f32)
            grad = sum_gradient(e, y_ref[0].astype(f32), r_ref[0])
            whole[...] = grad
            low[...] = grad.T.astype(bf16)
            sum_ref[0] = grad.astype(bf16)

        @pl.when(active)
        def _():
            grad_pre = dot(q_ref[0, 0], low[...], ((1,), (0,))) * slope_ref[0].astype(f32).T
            pre_ref[0] = grad_pre.T.astype(bf16)

            @pl.when(info[base + 3] > 0)
            def _():
                part = dot(p_ref[0, 0], grad_pre.astype(bf16), ((1,), (0,)))

                @pl.when(j == 0)
                def _():
                    total[...] = part

                @pl.when(j > 0)
                def _():
                    total[...] += part

                @pl.when(j == pl.num_programs(0) - 1)
                def _():
                    out_ref[...] = (whole[...] + total[...].T).astype(bf16)

    if recv is None:
        e_spec = pl.BlockSpec((1, per, tokens, model), lambda j, i: (i[base + 1], group, 0, 0))
        operands = [in_hbm(top_grad)]
    else:
        e_spec = pl.BlockSpec((rows, model), lambda j, i: (0, 0))
        operands = [recv]
    in_specs = [
        e_spec,
        pl.BlockSpec((1, rows, model), lambda j, i: (group, 0, 0)),
        pl.BlockSpec((1, rows, 1), lambda j, i: (group, 0, 0)),
        pl.BlockSpec((1, rows, tile), lambda j, i: (group, 0, j * i[base])),
        pl.BlockSpec((1, 1, model, tile), lambda j, i: (i[base + 1], 0, 0, j * i[base + 3])),
        pl.BlockSpec((1, 1, tile, model), lambda j, i: (i[base + 1], 0, j * i[base], 0)),
    ]
    operands += [in_vmem(x) for x in (ys, rs, slopes)] + [in_hbm(w_up), in_hbm(w_down)]
    aliases = {}
    if previous is not None:
        aliases = {1 + len(operands): 1, 2 + len(operands): 2}
        in_specs += [any_space] * 2
        operands += [in_hbm(x) for x in previous]
    for x in after:
        if previous is None or not any(x is y for y in previous):
            in_specs.append(any_space)
            operands.append(in_hbm(x) if x.ndim > 2 else x)
    return pl.pallas_call(
        body,
        grid_spec=pltpu.PrefetchScalarGridSpec(
            num_scalar_prefetch=1,
            grid=(width // tile,),
            in_specs=in_specs,
            out_specs=[
                pl.BlockSpec((rows, model), lambda j, i: (0, 0)),
                pl.BlockSpec((1, rows, tile), lambda j, i: (i[base + 2], 0, j * i[base])),
                pl.BlockSpec((1, rows, model), lambda j, i: (i[base + 2], 0, 0)),
            ],
            scratch_shapes=[
                pltpu.VMEM((rows, model), f32),
                pltpu.VMEM((model, rows), bf16),
                pltpu.VMEM((model, rows), f32),
            ],
        ),
        out_shape=[
            jax.ShapeDtypeStruct((rows, model), bf16),
            pltpu.HBM((groups + 1, rows, width), bf16),
            pltpu.HBM((groups + 1, rows, model), bf16),
        ],
        input_output_aliases=aliases,
        compiler_params=params(20),
        cost_estimate=light,
        name="chain",
    )(table, *operands)


def home_step(info, arrived, top_grad, saved, w_down, after):
    slopes, ys, rs = saved
    groups, rows, model = ys.shape
    micro, tokens = top_grad.shape[1:3]
    width = w_down.shape[2]
    tile = tile_of(width)

    def body(info, *refs):
        e_refs = refs[:groups]
        top_ref, y_ref, r_ref, slope_ref, q_ref = refs[groups : groups + 5]
        pre_ref, sum_ref = refs[-2:]

        @pl.when(pl.program_id(0) == 0)
        def _():
            for g in range(groups):
                top = top_ref[0].reshape(groups, rows, model)[g]
                e = jnp.where(info[0] > 0, top, e_refs[g][...]).astype(f32)
                grad = sum_gradient(e, y_ref[g].astype(f32), r_ref[g])
                sum_ref[g] = grad.astype(bf16)

        low = sum_ref[...].reshape(groups * rows, model)
        slope = slope_ref[...].reshape(groups * rows, tile)
        grad_pre = dot(low, q_ref[0, 0], ((1,), (1,))) * slope.astype(f32)
        pre_ref[...] = grad_pre.astype(bf16).reshape(pre_ref.shape)

    return pl.pallas_call(
        body,
        grid_spec=pltpu.PrefetchScalarGridSpec(
            num_scalar_prefetch=1,
            grid=(width // tile,),
            in_specs=[pl.BlockSpec((rows, model), lambda j, i: (0, 0))] * groups
            + [
                pl.BlockSpec((1, micro, tokens, model), lambda j, i: (1, 0, 0, 0)),
                pl.BlockSpec((groups, rows, model), lambda j, i: (0, 0, 0)),
                pl.BlockSpec((groups, rows, 1), lambda j, i: (0, 0, 0)),
                pl.BlockSpec((groups, rows, tile), lambda j, i: (0, 0, j)),
                pl.BlockSpec((1, 1, tile, model), lambda j, i: (0, 0, j, 0)),
            ]
            + [any_space] * len(after),
            out_specs=[
                pl.BlockSpec((groups, rows, tile), lambda j, i: (0, 0, j)),
                pl.BlockSpec((groups, rows, model), lambda j, i: (0, 0, 0)),
            ],
        ),
        out_shape=[
            pltpu.HBM((groups, rows, width), bf16),
            pltpu.HBM((groups, rows, model), bf16),
        ],
        compiler_params=params(28),
        cost_estimate=light,
        name="home",
    )(
        info,
        *arrived,
        in_hbm(top_grad),
        *[in_vmem(x) for x in (ys, rs, slopes)],
        in_hbm(w_down),
        *[in_hbm(x) if x.ndim > 2 else x for x in after],
    )


def weight_gradient(core, left_a, right_a, left_b, right_b, groups, replicas, split_left, came, after):
    tokens = right_a.shape[-2]
    rows, columns = left_a.shape[-1] // replicas, right_a.shape[-1]
    lines = replicas // 2
    tile = columns if split_left else tile_of(columns)
    steps = lines if split_left else columns // tile
    lefts = 1 if split_left else lines
    pair = rows % 128 != 0
    wide = 2 * rows if pair else rows

    def place(z, i):
        return z if pair else 2 * z + i[0]

    def body(info, *refs):
        def flat(ref):
            return ref[...].reshape(-1, ref.shape[-1])

        def product(left_refs, right_ref):
            left = [flat(ref) for ref in left_refs]
            if pair:
                left = [jnp.where(info[0] == 0, x[:, :rows], x[:, rows:]) for x in left]
            left = left[0] if len(left) == 1 else jnp.concatenate(left, axis=1)
            return dot(left, flat(right_ref), ((0,), (0,)))

        total = product(refs[:lefts], refs[lefts])
        total += product(refs[lefts + 1 : 2 * lefts + 1], refs[2 * lefts + 1])
        total = total.reshape(lefts, rows, tile)
        if came is not None:
            total += refs[2 * lefts + 2][...].astype(f32)
        refs[-1][...] = total.astype(bf16)

    def left_specs(array):
        lead = array.ndim - 3
        block = (1,) * lead + (groups, tokens, wide)
        if split_left:
            return [pl.BlockSpec(block, lambda j, i: (0,) * (lead + 2) + (place(j, i),))]
        return [
            pl.BlockSpec(block, lambda j, i, z=z: (0,) * (lead + 2) + (place(z, i),))
            for z in range(lines)
        ]

    def right_spec(array):
        lead = array.ndim - 3
        block = (1,) * lead + (groups, tokens, tile)
        if split_left:
            return pl.BlockSpec(block, lambda j, i: (0,) * (lead + 3))
        return pl.BlockSpec(block, lambda j, i: (0,) * (lead + 2) + (j,))

    if split_left:
        out_spec = pl.BlockSpec((1, rows, tile), lambda j, i: (j, 0, 0))
    else:
        out_spec = pl.BlockSpec((lines, rows, tile), lambda j, i: (0, 0, j))
    operands = [in_hbm(left_a)] * lefts + [in_hbm(right_a)]
    operands += [in_hbm(left_b)] * lefts + [in_hbm(right_b)]
    in_specs = left_specs(left_a) + [right_spec(right_a)]
    in_specs += left_specs(left_b) + [right_spec(right_b)]
    if came is not None:
        operands.append(came)
        in_specs.append(out_spec)
    in_specs += [any_space] * len(after)
    operands += [in_hbm(x) for x in after]
    return pl.pallas_call(
        body,
        grid_spec=pltpu.PrefetchScalarGridSpec(
            num_scalar_prefetch=1, grid=(steps,), in_specs=in_specs, out_specs=out_spec
        ),
        out_shape=pltpu.HBM((lines, rows, columns), bf16),
        compiler_params=params(28),
        cost_estimate=light,
        name="weights",
    )(core, *operands)


def fold(places, part, came):
    _, rows, columns = part.shape
    tile = min(64, rows)

    def body(info, *refs):
        for k in range(2):
            value = refs[k][0].astype(f32)
            if came:
                value += refs[2 + k][...].astype(f32)
            refs[k - 2][...] = value.astype(bf16)

    plain = pl.BlockSpec((tile, columns), lambda j, i: (j, 0))
    return pl.pallas_call(
        body,
        grid_spec=pltpu.PrefetchScalarGridSpec(
            num_scalar_prefetch=1,
            grid=(rows // tile,),
            in_specs=[
                pl.BlockSpec((1, tile, columns), lambda j, i: (i[0], j, 0)),
                pl.BlockSpec((1, tile, columns), lambda j, i: (i[1], j, 0)),
            ]
            + [plain] * len(came),
            out_specs=[plain] * 2,
        ),
        out_shape=[jax.ShapeDtypeStruct((rows, columns), bf16)] * 2,
        compiler_params=params(16),
        cost_estimate=light,
        name="fold",
    )(places, in_hbm(part), in_hbm(part), *came)


def update(replica, weight, moment, part, came):
    _, rows, columns = moment.shape
    tile = min(64, rows)
    steps = rows // tile

    def body(info, weight_ref, moment_ref, part_ref, right_ref, left_ref, fresh_ref, out_ref):
        total = part_ref[0].astype(f32) + right_ref[...].astype(f32) + left_ref[...].astype(f32)
        fresh_moment = momentum_decay * moment_ref[0] + total
        out_ref[0] = fresh_moment
        fresh_ref[...] = (weight_ref[0, 0].astype(f32) - step_size * fresh_moment).astype(bf16)

    return pl.pallas_call(
        body,
        grid_spec=pltpu.PrefetchScalarGridSpec(
            num_scalar_prefetch=1,
            grid=(steps,),
            in_specs=[
                pl.BlockSpec((1, 1, tile, columns), lambda j, i: (0, 0, i[0] * steps + j, 0)),
                pl.BlockSpec((1, tile, columns), lambda j, i: (0, j, 0)),
                pl.BlockSpec((1, tile, columns), lambda j, i: (i[1], j, 0)),
                pl.BlockSpec((tile, columns), lambda j, i: (j, 0)),
                pl.BlockSpec((tile, columns), lambda j, i: (j, 0)),
            ],
            out_specs=[
                pl.BlockSpec((tile, columns), lambda j, i: (j, 0)),
                pl.BlockSpec((1, tile, columns), lambda j, i: (0, j, 0)),
            ],
        ),
        out_shape=[
            jax.ShapeDtypeStruct((rows, columns), bf16),
            pltpu.HBM((1, rows, columns), f32),
        ],
        compiler_params=params(24),
        cost_estimate=light,
        name="update",
    )(replica, in_hbm(weight), in_hbm(moment), in_hbm(part), *came)


def on_device(section_inputs, top_grad, plan, up_weight, down_weight, up_moment, down_moment):
    sections = lax.axis_size("section")
    position = lax.axis_index("section").astype(jnp.int32)
    micro, tokens, model = top_grad.shape[1:]
    plan = plan.astype(jnp.int32)
    per = 2 if micro % 2 == 0 else 1
    groups, rows = micro // per, per * tokens
    last, half = sections - 1, sections // 2

    def hop(value, pairs):
        return lax.ppermute(value, "section", pairs) if pairs else None

    mirrored = lax.ppermute(
        section_inputs[1, 0], "section", [(i, last - i) for i in range(sections)]
    )[None, None]

    upper = (position >= half).astype(jnp.int32)
    relay = (1 - upper, upper)
    calls = [(stage, group) for stage in range(sections) for group in range(groups)]
    stages = np.array([stage for stage, _ in calls], np.int32)
    own = np.array([group for _, group in calls], np.int32)
    of = jnp.where(stages < half, relay[0], relay[1])
    active = (jnp.where(of == 0, last - position, position) == stages) & ~(
        (of == 1) & (position == last)
    )
    table = jnp.stack(
        [
            active.astype(jnp.int32),
            of,
            jnp.where(active & (of == 0), own, groups),
            (active & (stages < last)).astype(jnp.int32),
        ],
        axis=1,
    ).reshape(-1)
    kinds = [jnp.stack([relay[k]] * 4) for k in range(2)]
    home_kind = jnp.array([0, 0, 1, 0], jnp.int32)

    blocks = None
    saved = [None, None]
    order = []

    def run_forward(kind, after):
        nonlocal blocks, order
        *blocks, slopes, ys, rs = forward(
            per, section_inputs, up_weight, down_weight, kinds[kind], plan, blocks, after, 2
        )
        saved[kind] = (slopes, ys, rs)
        order = [blocks[0]]

    run_forward(0, [])
    received = {}
    arrived = {}
    asked = {(1, 0): [(last - 1, 0)], (half, 0): [(last - 1, g) for g in range(1, groups)]}
    kept = None
    for call, (stage, group) in enumerate(calls):
        if stage == last and group == 0:
            *home_blocks, slopes, ys, rs = forward(
                per, mirrored, up_weight, down_weight, home_kind, plan, None, order, 1
            )
            saved_home = (slopes, ys, rs)
            order = [home_blocks[0]]
        recv = received.pop((stage, group), None)
        out, *kept = chain_step(
            call,
            group,
            table,
            recv,
            top_grad,
            saved[int(stage >= half)],
            up_weight,
            down_weight,
            kept,
            order + [arrived[x] for x in asked.get((stage, group), [])],
        )
        order = [kept[0]]
        pairs = [(last - stage, last - stage - 1)] if stage < last else []
        if stage < last - 1:
            pairs.append((stage, stage + 1))
        got = hop(out, pairs)
        if got is not None:
            received[(stage + 1, group)] = got
        if stage < last:
            to = last - 1 - stage
            arrived[(to, group)] = out if to == stage else hop(out, [(stage, to)])
        if saved[1] is None and group == groups - 1:
            run_forward(1, order + [mirrored[0, 0]])

    side = sorted(arrived)
    *values, kept[1] = lax.optimization_barrier([arrived[x] for x in side] + [kept[1]])
    arrived = dict(zip(side, values))
    came = []
    for group in range(groups):
        value = arrived[(0, group)]
        for k in range(1, last):
            value = jnp.where(position == k, arrived[(k, group)], value)
        came.append(value)
    home_pre, home_sum = home_step(
        (position == last).astype(jnp.int32)[None], came, top_grad, saved_home, down_weight, order
    )

    replicas = lax.axis_size("dp")
    replica = lax.axis_index("dp").astype(jnp.int32)
    lines, place, core = replicas // 2, replica // 2, replica % 2
    swap = [(i, i ^ 1) for i in range(replicas)]
    sources = (
        (blocks[1], kept[1], home_blocks[1], home_sum, groups, replicas, True),
        (blocks[0], kept[0], home_blocks[0], home_pre, groups, replicas, False),
    )
    other = (1 - core)[None]
    sent_down = weight_gradient(other, *sources[0], None, [])
    came_down = lax.ppermute(sent_down, "dp", swap)
    sent_up = weight_gradient(other, *sources[1], None, [sent_down])
    came_up = lax.ppermute(sent_up, "dp", swap)
    parts = [weight_gradient(core[None], *sources[0], came_down, [sent_up])]
    parts.append(weight_gradient(core[None], *sources[1], came_up, [parts[0]]))

    came = [[], []]
    for step in range(1, lines):
        places = jnp.stack(
            [jnp.minimum(place + lines - step, lines - 1), jnp.maximum(place - lines + step, 0)]
        )
        starts = [z for z in range(step) if z + 1 < lines]
        right = [(2 * z + c, 2 * z + 2 + c) for z in starts for c in range(2)]
        left = [(replicas - 1 - i, replicas - 1 - k) for i, k in right]
        for k in range(2):
            to_right, to_left = fold(places, parts[k], came[k])
            came[k] = [lax.ppermute(to_right, "dp", right), lax.ppermute(to_left, "dp", left)]

    where = jnp.stack([replica, place])

    def finish(weight, moment, part, arrivals):
        fresh, fresh_moment = update(where, weight, moment, part, arrivals)
        far = lax.ppermute(fresh, "section", [(i, last - i) for i in range(sections)])
        return jnp.stack([fresh, far])[:, None], fresh_moment

    new_down_weight, new_down_moment = finish(down_weight, down_moment, parts[0], came[0])
    new_up_weight, new_up_moment = finish(up_weight, up_moment, parts[1], came[1])
    return (new_up_weight, new_down_weight, new_up_moment, new_down_moment)


def solution(mesh):
    in_specs = (
        P(None, "section", None, "dp", None),
        P(None, None, "dp", None),
        P(),
        P(None, "section", None, None),
        P(None, "section", None, None),
        P("section", "dp", None),
        P("section", "dp", None),
    )
    out_specs = (
        P(None, "section", "dp", None),
        P(None, "section", "dp", None),
        P("section", "dp", None),
        P("section", "dp", None),
    )
    return jax.shard_map(
        on_device, mesh=mesh, in_specs=in_specs, out_specs=out_specs, check_vma=False
    )
```

```python
import jax
import jax.numpy as jnp
import numpy as np
from jax import lax
from jax.experimental import pallas as pl
from jax.experimental.pallas import tpu as pltpu
from jax.sharding import PartitionSpec as P

norm_epsilon = 1e-06
momentum_decay = 0.9
step_size = 0.01
root_half = 0.7071067811865476
inv_root_tau = 0.3989422804014327

f32 = jnp.float32
bf16 = jnp.bfloat16
any_space = pl.BlockSpec(memory_space=pl.ANY)
light = pl.CostEstimate(flops=1000, bytes_accessed=1000, transcendentals=0)


def params(mib):
    return pltpu.CompilerParams(
        dimension_semantics=("arbitrary",), vmem_limit_bytes=mib * 1024 * 1024
    )


def in_vmem(x):
    return pltpu.with_memory_space_constraint(x, pltpu.VMEM)


def in_hbm(x):
    return pltpu.with_memory_space_constraint(x, pltpu.HBM)


def dot(left, right, over):
    return lax.dot_general(left, right, (over, ((), ())), preferred_element_type=f32)


def tile_of(width):
    return min(512, width)


def forward(per, inputs, w_up, w_down, info, plan, previous, after, places):
    _, _, micro, tokens, model = inputs.shape
    width = w_up.shape[3]
    tile = tile_of(width)
    groups, rows, every = micro // per, per * tokens, micro * tokens

    def body(info_ref, plan_ref, *refs):
        u_refs = refs[:micro]
        p_ref, q_ref = refs[micro : micro + 2]
        outs = refs[len(operands) :]
        us_ref, h_ref, slope_ref, y_ref, r_ref = outs[:5]
        rows_ref, total = outs[-2:]
        j = pl.program_id(0)

        @pl.when(j == 0)
        def _():
            for k in range(micro):
                u = u_refs[k][0, 0, 0]
                rows_ref[k * tokens : (k + 1) * tokens] = u
                us_ref[0, k // per, k % per * tokens : (k % per + 1) * tokens] = u

        for g in range(groups):
            here = slice(g * rows, (g + 1) * rows)
            u = rows_ref[here]
            pre = dot(u, p_ref[0, 0], ((1,), (0,)))
            cdf = 0.5 * (1.0 + lax.erf(pre * root_half))
            hidden = (pre * cdf).astype(bf16)
            slope = cdf + pre * (jnp.exp(-0.5 * pre * pre) * inv_root_tau)
            h_ref[0, g] = hidden
            slope_ref[g] = slope.astype(bf16)
            part = dot(hidden, q_ref[0, 0], ((1,), (0,)))
            base = jnp.where(j == 0, u.astype(f32), total[here])
            total[here] = base + part

        @pl.when(j == pl.num_programs(0) - 1)
        def _():
            for g in range(groups):
                z = total[g * rows : (g + 1) * rows]
                centre = z - jnp.mean(z, axis=-1, keepdims=True)
                r = lax.rsqrt(jnp.mean(centre * centre, axis=-1, keepdims=True) + norm_epsilon)
                y_ref[g] = (centre * r).astype(bf16)
                r_ref[g] = r

    def u_spec(k):
        return pl.BlockSpec(
            (1, 1, 1, tokens, model), lambda j, i, p: (i[0], 0, p[i[2], k], 0, 0)
        )

    in_specs = [u_spec(k) for k in range(micro)] + [
        pl.BlockSpec((1, 1, model, tile), lambda j, i, p: (i[1], 0, 0, j)),
        pl.BlockSpec((1, 1, tile, model), lambda j, i, p: (i[1], 0, j, 0)),
    ]
    operands = [in_hbm(inputs)] * micro + [in_hbm(w_up), in_hbm(w_down)]
    aliases = {}
    if previous is not None:
        aliases = {2 + len(operands) + k: k for k in range(2)}
        in_specs += [any_space] * 2
        operands += [in_hbm(x) for x in previous]
    for x in after:
        in_specs.append(any_space)
        operands.append(in_hbm(x) if x.ndim > 2 else x)
    out_shape = [
        pltpu.HBM((places, groups, rows, model), bf16),
        pltpu.HBM((places, groups, rows, width), bf16),
        pltpu.VMEM((groups, rows, width), bf16),
        pltpu.VMEM((groups, rows, model), bf16),
        pltpu.VMEM((groups, rows, 1), f32),
    ]
    out_specs = [
        pl.BlockSpec((1, groups, rows, model), lambda j, i, p: (i[3], 0, 0, 0)),
        pl.BlockSpec((1, groups, rows, tile), lambda j, i, p: (i[3], 0, 0, j)),
        pl.BlockSpec((groups, rows, tile), lambda j, i, p: (0, 0, j)),
        pl.BlockSpec((groups, rows, model), lambda j, i, p: (0, 0, 0)),
        pl.BlockSpec((groups, rows, 1), lambda j, i, p: (0, 0, 0)),
    ]
    return pl.pallas_call(
        body,
        grid_spec=pltpu.PrefetchScalarGridSpec(
            num_scalar_prefetch=2,
            grid=(width // tile,),
            in_specs=in_specs,
            out_specs=out_specs,
            scratch_shapes=[pltpu.VMEM((every, model), bf16), pltpu.VMEM((every, model), f32)],
        ),
        out_shape=out_shape,
        input_output_aliases=aliases,
        compiler_params=params(30),
        cost_estimate=light,
        name="forward",
    )(info, plan, *operands)


def sum_gradient(e, y, r):
    mean_e = jnp.mean(e, axis=-1, keepdims=True)
    mean_ey = jnp.mean(e * y, axis=-1, keepdims=True)
    return r * (e - mean_e - y * mean_ey)


columns_of_table = 4


def by_halves(left, refs):
    return jnp.concatenate([dot(left, ref[0, 0], ((1,), (1,))) for ref in refs], axis=1)


def chain_step(call, group, table, recv, top_grad, saved, w_up, w_down, previous, after):
    base = call * columns_of_table
    slopes, ys, rs = saved
    groups, rows, model = ys.shape
    width = w_up.shape[3]
    tile = tile_of(width)
    tokens = top_grad.shape[2]
    per = rows // tokens

    def body(info, e_ref, y_ref, r_ref, slope_ref, *rest):
        p_refs, q_refs = rest[:2], rest[2:4]
        out_ref, pre_ref, sum_ref, whole, low, total = rest[-6:]
        j = pl.program_id(0)
        active = info[base] > 0

        @pl.when(jnp.logical_and(active, j == 0))
        def _():
            e = e_ref[...].reshape(rows, model).astype(f32)
            grad = sum_gradient(e, y_ref[0].astype(f32), r_ref[0])
            whole[...] = grad
            low[...] = grad.astype(bf16)
            sum_ref[0] = grad.astype(bf16)

        @pl.when(active)
        def _():
            grad_pre = (
                by_halves(low[...], q_refs) * slope_ref[0].astype(f32)
            ).astype(bf16)
            pre_ref[0] = grad_pre

            @pl.when(info[base + 3] > 0)
            def _():
                part = by_halves(grad_pre, p_refs)

                @pl.when(j == 0)
                def _():
                    total[...] = whole[...] + part

                @pl.when(j > 0)
                def _():
                    total[...] += part

                @pl.when(j == pl.num_programs(0) - 1)
                def _():
                    out_ref[...] = total[...].astype(bf16)

    if recv is None:
        e_spec = pl.BlockSpec((1, per, tokens, model), lambda j, i: (i[base + 1], group, 0, 0))
        operands = [in_hbm(top_grad)]
    else:
        e_spec = pl.BlockSpec((rows, model), lambda j, i: (0, 0))
        operands = [recv]
    in_specs = [
        e_spec,
        pl.BlockSpec((1, rows, model), lambda j, i: (group, 0, 0)),
        pl.BlockSpec((1, rows, 1), lambda j, i: (group, 0, 0)),
        pl.BlockSpec((1, rows, tile), lambda j, i: (group, 0, j * i[base])),
        *[
            pl.BlockSpec(
                (1, 1, model // 2, tile), lambda j, i, k=k: (i[base + 1], 0, k, j * i[base + 3])
            )
            for k in range(2)
        ],
        *[
            pl.BlockSpec(
                (1, 1, tile // 2, model), lambda j, i, k=k: (i[base + 1], 0, 2 * j * i[base] + k, 0)
            )
            for k in range(2)
        ],
    ]
    operands += [in_vmem(x) for x in (ys, rs, slopes)] + [in_hbm(w_up)] * 2 + [in_hbm(w_down)] * 2
    aliases = {}
    if previous is not None:
        aliases = {1 + len(operands): 1, 2 + len(operands): 2}
        in_specs += [any_space] * 2
        operands += [in_hbm(x) for x in previous]
    for x in after:
        if previous is None or not any(x is y for y in previous):
            in_specs.append(any_space)
            operands.append(in_hbm(x) if x.ndim > 2 else x)
    return pl.pallas_call(
        body,
        grid_spec=pltpu.PrefetchScalarGridSpec(
            num_scalar_prefetch=1,
            grid=(width // tile,),
            in_specs=in_specs,
            out_specs=[
                pl.BlockSpec((rows, model), lambda j, i: (0, 0)),
                pl.BlockSpec((1, rows, tile), lambda j, i: (i[base + 2], 0, j * i[base])),
                pl.BlockSpec((1, rows, model), lambda j, i: (i[base + 2], 0, 0)),
            ],
            scratch_shapes=[
                pltpu.VMEM((rows, model), f32),
                pltpu.VMEM((rows, model), bf16),
                pltpu.VMEM((rows, model), f32),
            ],
        ),
        out_shape=[
            jax.ShapeDtypeStruct((rows, model), bf16),
            pltpu.HBM((groups + 1, rows, width), bf16),
            pltpu.HBM((groups + 1, rows, model), bf16),
        ],
        input_output_aliases=aliases,
        compiler_params=params(20),
        cost_estimate=light,
        name="chain",
    )(table, *operands)


def home_step(info, arrived, top_grad, saved, w_down, after):
    slopes, ys, rs = saved
    groups, rows, model = ys.shape
    micro, tokens = top_grad.shape[1:3]
    width = w_down.shape[2]
    tile = tile_of(width)

    def body(info, *refs):
        e_refs = refs[:groups]
        top_ref, y_ref, r_ref, slope_ref, q_ref = refs[groups : groups + 5]
        pre_ref, sum_ref = refs[-2:]

        @pl.when(pl.program_id(0) == 0)
        def _():
            for g in range(groups):
                top = top_ref[0].reshape(groups, rows, model)[g]
                e = jnp.where(info[0] > 0, top, e_refs[g][...]).astype(f32)
                grad = sum_gradient(e, y_ref[g].astype(f32), r_ref[g])
                sum_ref[g] = grad.astype(bf16)

        low = sum_ref[...].reshape(groups * rows, model)
        slope = slope_ref[...].reshape(groups * rows, tile)
        grad_pre = dot(low, q_ref[0, 0], ((1,), (1,))) * slope.astype(f32)
        pre_ref[...] = grad_pre.astype(bf16).reshape(pre_ref.shape)

    return pl.pallas_call(
        body,
        grid_spec=pltpu.PrefetchScalarGridSpec(
            num_scalar_prefetch=1,
            grid=(width // tile,),
            in_specs=[pl.BlockSpec((rows, model), lambda j, i: (0, 0))] * groups
            + [
                pl.BlockSpec((1, micro, tokens, model), lambda j, i: (1, 0, 0, 0)),
                pl.BlockSpec((groups, rows, model), lambda j, i: (0, 0, 0)),
                pl.BlockSpec((groups, rows, 1), lambda j, i: (0, 0, 0)),
                pl.BlockSpec((groups, rows, tile), lambda j, i: (0, 0, j)),
                pl.BlockSpec((1, 1, tile, model), lambda j, i: (0, 0, j, 0)),
            ]
            + [any_space] * len(after),
            out_specs=[
                pl.BlockSpec((groups, rows, tile), lambda j, i: (0, 0, j)),
                pl.BlockSpec((groups, rows, model), lambda j, i: (0, 0, 0)),
            ],
        ),
        out_shape=[
            pltpu.HBM((groups, rows, width), bf16),
            pltpu.HBM((groups, rows, model), bf16),
        ],
        compiler_params=params(28),
        cost_estimate=light,
        name="home",
    )(
        info,
        *arrived,
        in_hbm(top_grad),
        *[in_vmem(x) for x in (ys, rs, slopes)],
        in_hbm(w_down),
        *[in_hbm(x) if x.ndim > 2 else x for x in after],
    )


def weight_gradient(core, left_a, right_a, left_b, right_b, groups, replicas, split_left, came, after):
    tokens = right_a.shape[-2]
    rows, columns = left_a.shape[-1] // replicas, right_a.shape[-1]
    lines = replicas // 2
    tile = columns if split_left else tile_of(columns)
    steps = lines if split_left else columns // tile
    lefts = 1 if split_left else lines
    pair = rows % 128 != 0
    wide = 2 * rows if pair else rows

    def place(z, i):
        return z if pair else 2 * z + i[0]

    def body(info, *refs):
        def flat(ref):
            return ref[...].reshape(-1, ref.shape[-1])

        def product(left_refs, right_ref):
            left = [flat(ref) for ref in left_refs]
            if pair:
                left = [jnp.where(info[0] == 0, x[:, :rows], x[:, rows:]) for x in left]
            left = left[0] if len(left) == 1 else jnp.concatenate(left, axis=1)
            return dot(left, flat(right_ref), ((0,), (0,)))

        total = product(refs[:lefts], refs[lefts])
        total += product(refs[lefts + 1 : 2 * lefts + 1], refs[2 * lefts + 1])
        total = total.reshape(lefts, rows, tile)
        if came is not None:
            total += refs[2 * lefts + 2][...].astype(f32)
        refs[-1][...] = total.astype(bf16)

    def left_specs(array):
        lead = array.ndim - 3
        block = (1,) * lead + (groups, tokens, wide)
        if split_left:
            return [pl.BlockSpec(block, lambda j, i: (0,) * (lead + 2) + (place(j, i),))]
        return [
            pl.BlockSpec(block, lambda j, i, z=z: (0,) * (lead + 2) + (place(z, i),))
            for z in range(lines)
        ]

    def right_spec(array):
        lead = array.ndim - 3
        block = (1,) * lead + (groups, tokens, tile)
        if split_left:
            return pl.BlockSpec(block, lambda j, i: (0,) * (lead + 3))
        return pl.BlockSpec(block, lambda j, i: (0,) * (lead + 2) + (j,))

    if split_left:
        out_spec = pl.BlockSpec((1, rows, tile), lambda j, i: (j, 0, 0))
    else:
        out_spec = pl.BlockSpec((lines, rows, tile), lambda j, i: (0, 0, j))
    operands = [in_hbm(left_a)] * lefts + [in_hbm(right_a)]
    operands += [in_hbm(left_b)] * lefts + [in_hbm(right_b)]
    in_specs = left_specs(left_a) + [right_spec(right_a)]
    in_specs += left_specs(left_b) + [right_spec(right_b)]
    if came is not None:
        operands.append(came)
        in_specs.append(out_spec)
    in_specs += [any_space] * len(after)
    operands += [in_hbm(x) for x in after]
    return pl.pallas_call(
        body,
        grid_spec=pltpu.PrefetchScalarGridSpec(
            num_scalar_prefetch=1, grid=(steps,), in_specs=in_specs, out_specs=out_spec
        ),
        out_shape=pltpu.HBM((lines, rows, columns), bf16),
        compiler_params=params(28),
        cost_estimate=light,
        name="weights",
    )(core, *operands)


def fold(places, part, came):
    _, rows, columns = part.shape
    tile = min(64, rows)

    def body(info, *refs):
        for k in range(2):
            value = refs[k][0].astype(f32)
            if came:
                value += refs[2 + k][...].astype(f32)
            refs[k - 2][...] = value.astype(bf16)

    plain = pl.BlockSpec((tile, columns), lambda j, i: (j, 0))
    return pl.pallas_call(
        body,
        grid_spec=pltpu.PrefetchScalarGridSpec(
            num_scalar_prefetch=1,
            grid=(rows // tile,),
            in_specs=[
                pl.BlockSpec((1, tile, columns), lambda j, i: (i[0], j, 0)),
                pl.BlockSpec((1, tile, columns), lambda j, i: (i[1], j, 0)),
            ]
            + [plain] * len(came),
            out_specs=[plain] * 2,
        ),
        out_shape=[jax.ShapeDtypeStruct((rows, columns), bf16)] * 2,
        compiler_params=params(16),
        cost_estimate=light,
        name="fold",
    )(places, in_hbm(part), in_hbm(part), *came)


def update(replica, weight, moment, part, came):
    _, rows, columns = moment.shape
    tile = min(64, rows)
    steps = rows // tile

    def body(info, weight_ref, moment_ref, part_ref, right_ref, left_ref, fresh_ref, out_ref):
        total = part_ref[0].astype(f32) + right_ref[...].astype(f32) + left_ref[...].astype(f32)
        fresh_moment = momentum_decay * moment_ref[0] + total
        out_ref[0] = fresh_moment
        fresh_ref[...] = (weight_ref[0, 0].astype(f32) - step_size * fresh_moment).astype(bf16)

    return pl.pallas_call(
        body,
        grid_spec=pltpu.PrefetchScalarGridSpec(
            num_scalar_prefetch=1,
            grid=(steps,),
            in_specs=[
                pl.BlockSpec((1, 1, tile, columns), lambda j, i: (0, 0, i[0] * steps + j, 0)),
                pl.BlockSpec((1, tile, columns), lambda j, i: (0, j, 0)),
                pl.BlockSpec((1, tile, columns), lambda j, i: (i[1], j, 0)),
                pl.BlockSpec((tile, columns), lambda j, i: (j, 0)),
                pl.BlockSpec((tile, columns), lambda j, i: (j, 0)),
            ],
            out_specs=[
                pl.BlockSpec((tile, columns), lambda j, i: (j, 0)),
                pl.BlockSpec((1, tile, columns), lambda j, i: (0, j, 0)),
            ],
        ),
        out_shape=[
            jax.ShapeDtypeStruct((rows, columns), bf16),
            pltpu.HBM((1, rows, columns), f32),
        ],
        compiler_params=params(24),
        cost_estimate=light,
        name="update",
    )(replica, in_hbm(weight), in_hbm(moment), in_hbm(part), *came)


def on_device(section_inputs, top_grad, plan, up_weight, down_weight, up_moment, down_moment):
    sections = lax.axis_size("section")
    position = lax.axis_index("section").astype(jnp.int32)
    micro, tokens, model = top_grad.shape[1:]
    plan = plan.astype(jnp.int32)
    per = 2 if micro % 2 == 0 else 1
    groups, rows = micro // per, per * tokens
    last, half = sections - 1, sections // 2

    def hop(value, pairs):
        return lax.ppermute(value, "section", pairs) if pairs else None

    mirrored = lax.ppermute(
        section_inputs[1, 0], "section", [(i, last - i) for i in range(sections)]
    )[None, None]

    upper = (position >= half).astype(jnp.int32)
    relay = (1 - upper, upper)
    calls = [(stage, group) for stage in range(sections) for group in range(groups)]
    stages = np.array([stage for stage, _ in calls], np.int32)
    own = np.array([group for _, group in calls], np.int32)
    of = jnp.where(stages < half, relay[0], relay[1])
    active = (jnp.where(of == 0, last - position, position) == stages) & ~(
        (of == 1) & (position == last)
    )
    table = jnp.stack(
        [
            active.astype(jnp.int32),
            of,
            jnp.where(active & (of == 0), own, groups),
            (active & (stages < last)).astype(jnp.int32),
        ],
        axis=1,
    ).reshape(-1)
    kinds = [jnp.stack([relay[k]] * 4) for k in range(2)]
    home_kind = jnp.array([0, 0, 1, 0], jnp.int32)

    blocks = None
    saved = [None, None]
    order = []

    def run_forward(kind, after):
        nonlocal blocks, order
        *blocks, slopes, ys, rs = forward(
            per, section_inputs, up_weight, down_weight, kinds[kind], plan, blocks, after, 2
        )
        saved[kind] = (slopes, ys, rs)
        order = [blocks[0]]

    run_forward(0, [])
    received = {}
    arrived = {}
    asked = {(1, 0): [(last - 1, 0)], (half, 0): [(last - 1, g) for g in range(1, groups)]}
    kept = None
    for call, (stage, group) in enumerate(calls):
        if stage == last and group == 0:
            *home_blocks, slopes, ys, rs = forward(
                per, mirrored, up_weight, down_weight, home_kind, plan, None, order, 1
            )
            saved_home = (slopes, ys, rs)
            order = [home_blocks[0]]
        recv = received.pop((stage, group), None)
        out, *kept = chain_step(
            call,
            group,
            table,
            recv,
            top_grad,
            saved[int(stage >= half)],
            up_weight,
            down_weight,
            kept,
            order + [arrived[x] for x in asked.get((stage, group), [])],
        )
        order = [kept[0]]
        pairs = [(last - stage, last - stage - 1)] if stage < last else []
        if stage < last - 1:
            pairs.append((stage, stage + 1))
        got = hop(out, pairs)
        if got is not None:
            received[(stage + 1, group)] = got
        if stage < last:
            to = last - 1 - stage
            arrived[(to, group)] = out if to == stage else hop(out, [(stage, to)])
        if saved[1] is None and group == groups - 1:
            run_forward(1, order + [mirrored[0, 0]])

    side = sorted(arrived)
    *values, kept[1] = lax.optimization_barrier([arrived[x] for x in side] + [kept[1]])
    arrived = dict(zip(side, values))
    came = []
    for group in range(groups):
        value = arrived[(0, group)]
        for k in range(1, last):
            value = jnp.where(position == k, arrived[(k, group)], value)
        came.append(value)
    home_pre, home_sum = home_step(
        (position == last).astype(jnp.int32)[None], came, top_grad, saved_home, down_weight, order
    )

    replicas = lax.axis_size("dp")
    replica = lax.axis_index("dp").astype(jnp.int32)
    lines, place, core = replicas // 2, replica // 2, replica % 2
    swap = [(i, i ^ 1) for i in range(replicas)]
    sources = (
        (blocks[1], kept[1], home_blocks[1], home_sum, groups, replicas, True),
        (blocks[0], kept[0], home_blocks[0], home_pre, groups, replicas, False),
    )
    other = (1 - core)[None]
    sent_down = weight_gradient(other, *sources[0], None, [])
    came_down = lax.ppermute(sent_down, "dp", swap)
    sent_up = weight_gradient(other, *sources[1], None, [sent_down])
    came_up = lax.ppermute(sent_up, "dp", swap)
    parts = [weight_gradient(core[None], *sources[0], came_down, [sent_up])]
    parts.append(weight_gradient(core[None], *sources[1], came_up, [parts[0]]))

    came = [[], []]
    for step in range(1, lines):
        places = jnp.stack(
            [jnp.minimum(place + lines - step, lines - 1), jnp.maximum(place - lines + step, 0)]
        )
        starts = [z for z in range(step) if z + 1 < lines]
        right = [(2 * z + c, 2 * z + 2 + c) for z in starts for c in range(2)]
        left = [(replicas - 1 - i, replicas - 1 - k) for i, k in right]
        for k in range(2):
            to_right, to_left = fold(places, parts[k], came[k])
            came[k] = [lax.ppermute(to_right, "dp", right), lax.ppermute(to_left, "dp", left)]

    where = jnp.stack([replica, place])

    def finish(weight, moment, part, arrivals):
        fresh, fresh_moment = update(where, weight, moment, part, arrivals)
        far = lax.ppermute(fresh, "section", [(i, last - i) for i in range(sections)])
        return jnp.stack([fresh, far])[:, None], fresh_moment

    new_down_weight, new_down_moment = finish(down_weight, down_moment, parts[0], came[0])
    new_up_weight, new_up_moment = finish(up_weight, up_moment, parts[1], came[1])
    return (new_up_weight, new_down_weight, new_up_moment, new_down_moment)


def solution(mesh):
    in_specs = (
        P(None, "section", None, "dp", None),
        P(None, None, "dp", None),
        P(),
        P(None, "section", None, None),
        P(None, "section", None, None),
        P("section", "dp", None),
        P("section", "dp", None),
    )
    out_specs = (
        P(None, "section", "dp", None),
        P(None, "section", "dp", None),
        P("section", "dp", None),
        P("section", "dp", None),
    )
    return jax.shard_map(
        on_device, mesh=mesh, in_specs=in_specs, out_specs=out_specs, check_vma=False
    )
```

```python
import jax
import jax.numpy as jnp
import numpy as np
from jax import lax
from jax.experimental import pallas as pl
from jax.experimental.pallas import tpu as pltpu
from jax.sharding import PartitionSpec as P

norm_epsilon = 1e-06
momentum_decay = 0.9
step_size = 0.01
root_half = 0.7071067811865476
inv_root_tau = 0.3989422804014327

f32 = jnp.float32
bf16 = jnp.bfloat16
any_space = pl.BlockSpec(memory_space=pl.ANY)
light = pl.CostEstimate(flops=1000, bytes_accessed=1000, transcendentals=0)


def params(mib):
    return pltpu.CompilerParams(
        dimension_semantics=("arbitrary",), vmem_limit_bytes=mib * 1024 * 1024
    )


def in_vmem(x):
    return pltpu.with_memory_space_constraint(x, pltpu.VMEM)


def in_hbm(x):
    return pltpu.with_memory_space_constraint(x, pltpu.HBM)


def dot(left, right, over):
    return lax.dot_general(left, right, (over, ((), ())), preferred_element_type=f32)


def tile_of(width):
    return min(512, width)


def forward(per, inputs, w_up, w_down, info, plan, previous, after, places):
    _, _, micro, tokens, model = inputs.shape
    width = w_up.shape[3]
    tile = tile_of(width)
    groups, rows, every = micro // per, per * tokens, micro * tokens

    def body(info_ref, plan_ref, *refs):
        u_refs = refs[:micro]
        p_ref, q_ref = refs[micro : micro + 2]
        outs = refs[len(operands) :]
        us_ref, h_ref, slope_ref, y_ref, r_ref = outs[:5]
        rows_ref, total = outs[-2:]
        j = pl.program_id(0)

        @pl.when(j == 0)
        def _():
            for k in range(micro):
                u = u_refs[k][0, 0, 0]
                rows_ref[k * tokens : (k + 1) * tokens] = u
                us_ref[0, k // per, k % per * tokens : (k % per + 1) * tokens] = u

        for g in range(groups):
            here = slice(g * rows, (g + 1) * rows)
            u = rows_ref[here]
            pre = dot(u, p_ref[0, 0], ((1,), (0,)))
            cdf = 0.5 * (1.0 + lax.erf(pre * root_half))
            hidden = (pre * cdf).astype(bf16)
            slope = cdf + pre * (jnp.exp(-0.5 * pre * pre) * inv_root_tau)
            h_ref[0, g] = hidden
            slope_ref[g] = slope.astype(bf16)
            part = dot(hidden, q_ref[0, 0], ((1,), (0,)))
            base = jnp.where(j == 0, u.astype(f32), total[here])
            total[here] = base + part

        @pl.when(j == pl.num_programs(0) - 1)
        def _():
            for g in range(groups):
                z = total[g * rows : (g + 1) * rows]
                centre = z - jnp.mean(z, axis=-1, keepdims=True)
                r = lax.rsqrt(jnp.mean(centre * centre, axis=-1, keepdims=True) + norm_epsilon)
                y_ref[g] = (centre * r).astype(bf16)
                r_ref[g] = r

    def u_spec(k):
        return pl.BlockSpec(
            (1, 1, 1, tokens, model), lambda j, i, p: (i[0], 0, p[i[2], k], 0, 0)
        )

    in_specs = [u_spec(k) for k in range(micro)] + [
        pl.BlockSpec((1, 1, model, tile), lambda j, i, p: (i[1], 0, 0, j)),
        pl.BlockSpec((1, 1, tile, model), lambda j, i, p: (i[1], 0, j, 0)),
    ]
    operands = [in_hbm(inputs)] * micro + [in_hbm(w_up), in_hbm(w_down)]
    aliases = {}
    if previous is not None:
        aliases = {2 + len(operands) + k: k for k in range(2)}
        in_specs += [any_space] * 2
        operands += [in_hbm(x) for x in previous]
    for x in after:
        in_specs.append(any_space)
        operands.append(in_hbm(x) if x.ndim > 2 else x)
    out_shape = [
        pltpu.HBM((places, groups, rows, model), bf16),
        pltpu.HBM((places, groups, rows, width), bf16),
        pltpu.VMEM((groups, rows, width), bf16),
        pltpu.VMEM((groups, rows, model), bf16),
        pltpu.VMEM((groups, rows, 1), f32),
    ]
    out_specs = [
        pl.BlockSpec((1, groups, rows, model), lambda j, i, p: (i[3], 0, 0, 0)),
        pl.BlockSpec((1, groups, rows, tile), lambda j, i, p: (i[3], 0, 0, j)),
        pl.BlockSpec((groups, rows, tile), lambda j, i, p: (0, 0, j)),
        pl.BlockSpec((groups, rows, model), lambda j, i, p: (0, 0, 0)),
        pl.BlockSpec((groups, rows, 1), lambda j, i, p: (0, 0, 0)),
    ]
    return pl.pallas_call(
        body,
        grid_spec=pltpu.PrefetchScalarGridSpec(
            num_scalar_prefetch=2,
            grid=(width // tile,),
            in_specs=in_specs,
            out_specs=out_specs,
            scratch_shapes=[pltpu.VMEM((every, model), bf16), pltpu.VMEM((every, model), f32)],
        ),
        out_shape=out_shape,
        input_output_aliases=aliases,
        compiler_params=params(30),
        cost_estimate=light,
        name="forward",
    )(info, plan, *operands)


def sum_gradient(e, y, r):
    mean_e = jnp.mean(e, axis=-1, keepdims=True)
    mean_ey = jnp.mean(e * y, axis=-1, keepdims=True)
    return r * (e - mean_e - y * mean_ey)


columns_of_table = 4


def chain_step(call, group, table, recv, top_grad, saved, w_up, w_down, previous, after):
    base = call * columns_of_table
    slopes, ys, rs = saved
    groups, rows, model = ys.shape
    width = w_up.shape[3]
    tile = tile_of(width)
    tokens = top_grad.shape[2]
    per = rows // tokens

    def body(info, e_ref, y_ref, r_ref, slope_ref, p_ref, q_ref, *rest):
        out_ref, pre_ref, sum_ref, whole, low, total = rest[-6:]
        j = pl.program_id(0)
        active = info[base] > 0

        @pl.when(jnp.logical_and(active, j == 0))
        def _():
            e = e_ref[...].reshape(rows, model).astype(f32)
            grad = sum_gradient(e, y_ref[0].astype(f32), r_ref[0])
            whole[...] = grad
            low[...] = grad.astype(bf16)
            sum_ref[0] = grad.astype(bf16)

        @pl.when(active)
        def _():
            grad_pre = (
                dot(low[...], q_ref[0, 0], ((1,), (1,))) * slope_ref[0].astype(f32)
            ).astype(bf16)
            pre_ref[0] = grad_pre

            @pl.when(info[base + 3] > 0)
            def _():
                part = dot(grad_pre, p_ref[0, 0], ((1,), (1,)))

                @pl.when(j == 0)
                def _():
                    total[...] = whole[...] + part

                @pl.when(j > 0)
                def _():
                    total[...] += part

                @pl.when(j == pl.num_programs(0) - 1)
                def _():
                    out_ref[...] = total[...].astype(bf16)

    if recv is None:
        e_spec = pl.BlockSpec((1, per, tokens, model), lambda j, i: (i[base + 1], group, 0, 0))
        operands = [in_hbm(top_grad)]
    else:
        e_spec = pl.BlockSpec((rows, model), lambda j, i: (0, 0))
        operands = [recv]
    in_specs = [
        e_spec,
        pl.BlockSpec((1, rows, model), lambda j, i: (group, 0, 0)),
        pl.BlockSpec((1, rows, 1), lambda j, i: (group, 0, 0)),
        pl.BlockSpec((1, rows, tile), lambda j, i: (group, 0, j * i[base])),
        pl.BlockSpec((1, 1, model, tile), lambda j, i: (i[base + 1], 0, 0, j * i[base + 3])),
        pl.BlockSpec((1, 1, tile, model), lambda j, i: (i[base + 1], 0, j * i[base], 0)),
    ]
    operands += [in_vmem(x) for x in (ys, rs, slopes)] + [in_hbm(w_up), in_hbm(w_down)]
    aliases = {}
    if previous is not None:
        aliases = {1 + len(operands): 1, 2 + len(operands): 2}
        in_specs += [any_space] * 2
        operands += [in_hbm(x) for x in previous]
    for x in after:
        if previous is None or not any(x is y for y in previous):
            in_specs.append(any_space)
            operands.append(in_hbm(x) if x.ndim > 2 else x)
    return pl.pallas_call(
        body,
        grid_spec=pltpu.PrefetchScalarGridSpec(
            num_scalar_prefetch=1,
            grid=(width // tile,),
            in_specs=in_specs,
            out_specs=[
                pl.BlockSpec((rows, model), lambda j, i: (0, 0)),
                pl.BlockSpec((1, rows, tile), lambda j, i: (i[base + 2], 0, j * i[base])),
                pl.BlockSpec((1, rows, model), lambda j, i: (i[base + 2], 0, 0)),
            ],
            scratch_shapes=[
                pltpu.VMEM((rows, model), f32),
                pltpu.VMEM((rows, model), bf16),
                pltpu.VMEM((rows, model), f32),
            ],
        ),
        out_shape=[
            jax.ShapeDtypeStruct((rows, model), bf16),
            pltpu.HBM((groups + 1, rows, width), bf16),
            pltpu.HBM((groups + 1, rows, model), bf16),
        ],
        input_output_aliases=aliases,
        compiler_params=params(20),
        cost_estimate=light,
        name="chain",
    )(table, *operands)


def home_step(info, arrived, top_grad, saved, w_down, after):
    slopes, ys, rs = saved
    groups, rows, model = ys.shape
    micro, tokens = top_grad.shape[1:3]
    width = w_down.shape[2]
    tile = tile_of(width)

    def body(info, *refs):
        e_refs = refs[:groups]
        top_ref, y_ref, r_ref, slope_ref, q_ref = refs[groups : groups + 5]
        pre_ref, sum_ref = refs[-2:]

        @pl.when(pl.program_id(0) == 0)
        def _():
            for g in range(groups):
                top = top_ref[0].reshape(groups, rows, model)[g]
                e = jnp.where(info[0] > 0, top, e_refs[g][...]).astype(f32)
                grad = sum_gradient(e, y_ref[g].astype(f32), r_ref[g])
                sum_ref[g] = grad.astype(bf16)

        low = sum_ref[...].reshape(groups * rows, model)
        slope = slope_ref[...].reshape(groups * rows, tile)
        grad_pre = dot(low, q_ref[0, 0], ((1,), (1,))) * slope.astype(f32)
        pre_ref[...] = grad_pre.astype(bf16).reshape(pre_ref.shape)

    return pl.pallas_call(
        body,
        grid_spec=pltpu.PrefetchScalarGridSpec(
            num_scalar_prefetch=1,
            grid=(width // tile,),
            in_specs=[pl.BlockSpec((rows, model), lambda j, i: (0, 0))] * groups
            + [
                pl.BlockSpec((1, micro, tokens, model), lambda j, i: (1, 0, 0, 0)),
                pl.BlockSpec((groups, rows, model), lambda j, i: (0, 0, 0)),
                pl.BlockSpec((groups, rows, 1), lambda j, i: (0, 0, 0)),
                pl.BlockSpec((groups, rows, tile), lambda j, i: (0, 0, j)),
                pl.BlockSpec((1, 1, tile, model), lambda j, i: (0, 0, j, 0)),
            ]
            + [any_space] * len(after),
            out_specs=[
                pl.BlockSpec((groups, rows, tile), lambda j, i: (0, 0, j)),
                pl.BlockSpec((groups, rows, model), lambda j, i: (0, 0, 0)),
            ],
        ),
        out_shape=[
            pltpu.HBM((groups, rows, width), bf16),
            pltpu.HBM((groups, rows, model), bf16),
        ],
        compiler_params=params(28),
        cost_estimate=light,
        name="home",
    )(
        info,
        *arrived,
        in_hbm(top_grad),
        *[in_vmem(x) for x in (ys, rs, slopes)],
        in_hbm(w_down),
        *[in_hbm(x) if x.ndim > 2 else x for x in after],
    )


def weight_gradient(core, left_a, right_a, left_b, right_b, groups, replicas, split_left, came, after):
    tokens = right_a.shape[-2]
    rows, columns = left_a.shape[-1] // replicas, right_a.shape[-1]
    lines = replicas // 2
    tile = columns if split_left else tile_of(columns)
    steps = lines if split_left else columns // tile
    lefts = 1 if split_left else lines
    pair = rows % 128 != 0
    wide = 2 * rows if pair else rows

    def place(z, i):
        return z if pair else 2 * z + i[0]

    def body(info, *refs):
        def flat(ref):
            return ref[...].reshape(-1, ref.shape[-1])

        def product(left_refs, right_ref):
            left = [flat(ref) for ref in left_refs]
            if pair:
                left = [jnp.where(info[0] == 0, x[:, :rows], x[:, rows:]) for x in left]
            left = left[0] if len(left) == 1 else jnp.concatenate(left, axis=1)
            return dot(left, flat(right_ref), ((0,), (0,)))

        total = product(refs[:lefts], refs[lefts])
        total += product(refs[lefts + 1 : 2 * lefts + 1], refs[2 * lefts + 1])
        total = total.reshape(lefts, rows, tile)
        if came is not None:
            total += refs[2 * lefts + 2][...].astype(f32)
        refs[-1][...] = total.astype(bf16)

    def left_specs(array):
        lead = array.ndim - 3
        block = (1,) * lead + (groups, tokens, wide)
        if split_left:
            return [pl.BlockSpec(block, lambda j, i: (0,) * (lead + 2) + (place(j, i),))]
        return [
            pl.BlockSpec(block, lambda j, i, z=z: (0,) * (lead + 2) + (place(z, i),))
            for z in range(lines)
        ]

    def right_spec(array):
        lead = array.ndim - 3
        block = (1,) * lead + (groups, tokens, tile)
        if split_left:
            return pl.BlockSpec(block, lambda j, i: (0,) * (lead + 3))
        return pl.BlockSpec(block, lambda j, i: (0,) * (lead + 2) + (j,))

    if split_left:
        out_spec = pl.BlockSpec((1, rows, tile), lambda j, i: (j, 0, 0))
    else:
        out_spec = pl.BlockSpec((lines, rows, tile), lambda j, i: (0, 0, j))
    operands = [in_hbm(left_a)] * lefts + [in_hbm(right_a)]
    operands += [in_hbm(left_b)] * lefts + [in_hbm(right_b)]
    in_specs = left_specs(left_a) + [right_spec(right_a)]
    in_specs += left_specs(left_b) + [right_spec(right_b)]
    if came is not None:
        operands.append(came)
        in_specs.append(out_spec)
    in_specs += [any_space] * len(after)
    operands += [in_hbm(x) for x in after]
    return pl.pallas_call(
        body,
        grid_spec=pltpu.PrefetchScalarGridSpec(
            num_scalar_prefetch=1, grid=(steps,), in_specs=in_specs, out_specs=out_spec
        ),
        out_shape=pltpu.HBM((lines, rows, columns), bf16),
        compiler_params=params(28),
        cost_estimate=light,
        name="weights",
    )(core, *operands)


def fold(places, part, came):
    _, rows, columns = part.shape
    tile = min(rows, max(8, 131072 // columns))

    def body(info, *refs):
        for k in range(2):
            value = refs[k][0].astype(f32)
            if came:
                value += refs[2 + k][...].astype(f32)
            refs[k - 2][...] = value.astype(bf16)

    plain = pl.BlockSpec((tile, columns), lambda j, i: (j, 0))
    return pl.pallas_call(
        body,
        grid_spec=pltpu.PrefetchScalarGridSpec(
            num_scalar_prefetch=1,
            grid=(rows // tile,),
            in_specs=[
                pl.BlockSpec((1, tile, columns), lambda j, i: (i[0], j, 0)),
                pl.BlockSpec((1, tile, columns), lambda j, i: (i[1], j, 0)),
            ]
            + [plain] * len(came),
            out_specs=[plain] * 2,
        ),
        out_shape=[jax.ShapeDtypeStruct((rows, columns), bf16)] * 2,
        compiler_params=params(16),
        cost_estimate=light,
        name="fold",
    )(places, in_hbm(part), in_hbm(part), *came)


def update(replica, weight, moment, part, came):
    _, rows, columns = moment.shape
    tile = min(rows, max(8, 131072 // columns))
    steps = rows // tile

    def body(info, weight_ref, moment_ref, part_ref, right_ref, left_ref, fresh_ref, out_ref):
        total = part_ref[0].astype(f32) + right_ref[...].astype(f32) + left_ref[...].astype(f32)
        fresh_moment = momentum_decay * moment_ref[0] + total
        out_ref[0] = fresh_moment
        fresh_ref[...] = (weight_ref[0, 0].astype(f32) - step_size * fresh_moment).astype(bf16)

    return pl.pallas_call(
        body,
        grid_spec=pltpu.PrefetchScalarGridSpec(
            num_scalar_prefetch=1,
            grid=(steps,),
            in_specs=[
                pl.BlockSpec((1, 1, tile, columns), lambda j, i: (0, 0, i[0] * steps + j, 0)),
                pl.BlockSpec((1, tile, columns), lambda j, i: (0, j, 0)),
                pl.BlockSpec((1, tile, columns), lambda j, i: (i[1], j, 0)),
                pl.BlockSpec((tile, columns), lambda j, i: (j, 0)),
                pl.BlockSpec((tile, columns), lambda j, i: (j, 0)),
            ],
            out_specs=[
                pl.BlockSpec((tile, columns), lambda j, i: (j, 0)),
                pl.BlockSpec((1, tile, columns), lambda j, i: (0, j, 0)),
            ],
        ),
        out_shape=[
            jax.ShapeDtypeStruct((rows, columns), bf16),
            pltpu.HBM((1, rows, columns), f32),
        ],
        compiler_params=params(24),
        cost_estimate=light,
        name="update",
    )(replica, in_hbm(weight), in_hbm(moment), in_hbm(part), *came)


def on_device(section_inputs, top_grad, plan, up_weight, down_weight, up_moment, down_moment):
    sections = lax.axis_size("section")
    position = lax.axis_index("section").astype(jnp.int32)
    micro, tokens, model = top_grad.shape[1:]
    plan = plan.astype(jnp.int32)
    per = 2 if micro % 2 == 0 else 1
    groups, rows = micro // per, per * tokens
    last, half = sections - 1, sections // 2

    def hop(value, pairs):
        return lax.ppermute(value, "section", pairs) if pairs else None

    mirrored = lax.ppermute(
        section_inputs[1, 0], "section", [(i, last - i) for i in range(sections)]
    )[None, None]

    upper = (position >= half).astype(jnp.int32)
    relay = (1 - upper, upper)
    calls = [(stage, group) for stage in range(sections) for group in range(groups)]
    stages = np.array([stage for stage, _ in calls], np.int32)
    own = np.array([group for _, group in calls], np.int32)
    of = jnp.where(stages < half, relay[0], relay[1])
    active = (jnp.where(of == 0, last - position, position) == stages) & ~(
        (of == 1) & (position == last)
    )
    table = jnp.stack(
        [
            active.astype(jnp.int32),
            of,
            jnp.where(active & (of == 0), own, groups),
            (active & (stages < last)).astype(jnp.int32),
        ],
        axis=1,
    ).reshape(-1)
    kinds = [jnp.stack([relay[k]] * 4) for k in range(2)]
    home_kind = jnp.array([0, 0, 1, 0], jnp.int32)

    blocks = None
    saved = [None, None]
    order = []

    def run_forward(kind, after):
        nonlocal blocks, order
        *blocks, slopes, ys, rs = forward(
            per, section_inputs, up_weight, down_weight, kinds[kind], plan, blocks, after, 2
        )
        saved[kind] = (slopes, ys, rs)
        order = [blocks[0]]

    run_forward(0, [])
    received = {}
    arrived = {}
    asked = {(1, 0): [(last - 1, 0)], (half, 0): [(last - 1, g) for g in range(1, groups)]}
    kept = None
    for call, (stage, group) in enumerate(calls):
        if stage == last and group == 0:
            *home_blocks, slopes, ys, rs = forward(
                per, mirrored, up_weight, down_weight, home_kind, plan, None, order, 1
            )
            saved_home = (slopes, ys, rs)
            order = [home_blocks[0]]
        recv = received.pop((stage, group), None)
        out, *kept = chain_step(
            call,
            group,
            table,
            recv,
            top_grad,
            saved[int(stage >= half)],
            up_weight,
            down_weight,
            kept,
            order + [arrived[x] for x in asked.get((stage, group), [])],
        )
        order = [kept[0]]
        pairs = [(last - stage, last - stage - 1)] if stage < last else []
        if stage < last - 1:
            pairs.append((stage, stage + 1))
        got = hop(out, pairs)
        if got is not None:
            received[(stage + 1, group)] = got
        if stage < last:
            to = last - 1 - stage
            arrived[(to, group)] = out if to == stage else hop(out, [(stage, to)])
        if saved[1] is None and group == groups - 1:
            run_forward(1, order + [mirrored[0, 0]])

    side = sorted(arrived)
    *values, kept[1] = lax.optimization_barrier([arrived[x] for x in side] + [kept[1]])
    arrived = dict(zip(side, values))
    came = []
    for group in range(groups):
        value = arrived[(0, group)]
        for k in range(1, last):
            value = jnp.where(position == k, arrived[(k, group)], value)
        came.append(value)
    home_pre, home_sum = home_step(
        (position == last).astype(jnp.int32)[None], came, top_grad, saved_home, down_weight, order
    )

    replicas = lax.axis_size("dp")
    replica = lax.axis_index("dp").astype(jnp.int32)
    lines, place, core = replicas // 2, replica // 2, replica % 2
    swap = [(i, i ^ 1) for i in range(replicas)]
    sources = (
        (blocks[1], kept[1], home_blocks[1], home_sum, groups, replicas, True),
        (blocks[0], kept[0], home_blocks[0], home_pre, groups, replicas, False),
    )
    other = (1 - core)[None]
    sent_down = weight_gradient(other, *sources[0], None, [])
    came_down = lax.ppermute(sent_down, "dp", swap)
    sent_up = weight_gradient(other, *sources[1], None, [sent_down])
    came_up = lax.ppermute(sent_up, "dp", swap)
    parts = [weight_gradient(core[None], *sources[0], came_down, [sent_up])]
    parts.append(weight_gradient(core[None], *sources[1], came_up, [parts[0]]))

    came = [[], []]
    for step in range(1, lines):
        places = jnp.stack(
            [jnp.minimum(place + lines - step, lines - 1), jnp.maximum(place - lines + step, 0)]
        )
        starts = [z for z in range(step) if z + 1 < lines]
        right = [(2 * z + c, 2 * z + 2 + c) for z in starts for c in range(2)]
        left = [(replicas - 1 - i, replicas - 1 - k) for i, k in right]
        for k in range(2):
            to_right, to_left = fold(places, parts[k], came[k])
            came[k] = [lax.ppermute(to_right, "dp", right), lax.ppermute(to_left, "dp", left)]

    where = jnp.stack([replica, place])

    def finish(weight, moment, part, arrivals):
        fresh, fresh_moment = update(where, weight, moment, part, arrivals)
        far = lax.ppermute(fresh, "section", [(i, last - i) for i in range(sections)])
        return jnp.stack([fresh, far])[:, None], fresh_moment

    new_down_weight, new_down_moment = finish(down_weight, down_moment, parts[0], came[0])
    new_up_weight, new_up_moment = finish(up_weight, up_moment, parts[1], came[1])
    return (new_up_weight, new_down_weight, new_up_moment, new_down_moment)


def solution(mesh):
    in_specs = (
        P(None, "section", None, "dp", None),
        P(None, None, "dp", None),
        P(),
        P(None, "section", None, None),
        P(None, "section", None, None),
        P("section", "dp", None),
        P("section", "dp", None),
    )
    out_specs = (
        P(None, "section", "dp", None),
        P(None, "section", "dp", None),
        P("section", "dp", None),
        P("section", "dp", None),
    )
    return jax.shard_map(
        on_device, mesh=mesh, in_specs=in_specs, out_specs=out_specs, check_vma=False
    )
```
